32 devices in a mesh: dp: 16 (over z, y, x), tp: 2 (over core).
Axes of the slice: x: 2, y: 2, z: 4, core: 2. Of those that a mesh axis runs over, the one named last changes fastest.
Arguments:
- tokens: bfloat16 [16384, 768], P('dp'), may hold values from -6 to 6
- seq_lengths: int32 [32], P('dp'), may hold values from 1 to 512, as said below
- out_grad: bfloat16 [16384, 768], P('dp'), may hold values from -6 to 6
- w_query: bfloat16 [768, 768], P(None, 'tp'), may hold values from -0.21875 to 0.21875
- bias_query: bfloat16 [768], P('tp'), may hold values from -1.75 to 1.75
- w_key: bfloat16 [768, 768], P(None, 'tp'), may hold values from -0.21875 to 0.21875
- w_value: bfloat16 [768, 768], P(None, 'tp'), may hold values from -0.21875 to 0.21875
- bias_value: bfloat16 [768], P('tp'), may hold values from -1.75 to 1.75
- w_out: bfloat16 [768, 768], P('tp'), may hold values from -1.75 to 1.75
- bias_out: bfloat16 [768], replicated, may hold values from -1.75 to 1.75
- gain_one: bfloat16 [768], replicated, may hold values from 0.25 to 1.75
- shift_one: bfloat16 [768], replicated, may hold values from -1.75 to 1.75
- w_up: bfloat16 [768, 3072], P(None, 'tp'), may hold values from -0.21875 to 0.21875
- bias_up: bfloat16 [3072], P('tp'), may hold values from -1.75 to 1.75
- w_down: bfloat16 [3072, 768], P('tp'), may hold values from -0.109375 to 0.109375
- bias_down: bfloat16 [768], replicated, may hold values from -1.75 to 1.75
- gain_two: bfloat16 [768], replicated, may hold values from 0.25 to 1.75
- shift_two: bfloat16 [768], replicated, may hold values from -1.75 to 1.75
Outputs:
- layer_output: bfloat16 [16384, 768], P('dp')
- input_grad: bfloat16 [16384, 768], P('dp')
- grad_w_query: float32 [768, 768], P('dp', 'tp')
- grad_w_key: float32 [768, 768], P('dp', 'tp')
- grad_w_value: float32 [768, 768], P('dp', 'tp')
- grad_bias_query: float32 [768], P('tp')
- grad_bias_value: float32 [768], P('tp')
- grad_w_out: float32 [768, 768], P('tp', 'dp')
- grad_bias_out: float32 [768], replicated
- grad_gain_one: float32 [768], replicated
- grad_shift_one: float32 [768], replicated
- grad_w_up: float32 [768, 3072], P('dp', 'tp')
- grad_bias_up: float32 [3072], P('tp')
- grad_w_down: float32 [3072, 768], P('tp', 'dp')
- grad_bias_down: float32 [768], replicated
- grad_gain_two: float32 [768], replicated
- grad_shift_two: float32 [768], replicated
The draws below stay inside these ranges and needn't reach their ends.
Inputs may be any that keep to these rules, and one draw needn't show every extreme that they name: `seq_lengths`: tokens at or beyond a sequence's length are padding: their keys are masked and their output rows are zero. Some sequence has 512 tokens in every draw.
All inputs are finite; a program needn't handle non-finite values.
Results may differ from the reference program's by a relative error of at most 0.018.
Values may be sent and summed in bfloat16 or wider, within the bound.
No kernel may reach another device: no remote copies, remote signals or barrier semaphores. Data moves between devices by JAX's collectives and lax.ppermute only.
A program may use at most 128 MiB of HBM per device.

```python
import math
import jax
import jax.numpy as jnp
from jax import lax

D = 768
HEADS = 12
HEAD = 64
FF = 3072
LENGTH = 512
SEQS = 32
TOKENS = 16384


def draw_seq_lengths(key, part):
    key = jax.random.fold_in(key, 11)
    first, second, third = jax.random.split(key, 3)
    draws = jax.random.randint(first, (4, SEQS), 1, LENGTH + 1)
    shortest = jnp.min(draws, axis=0)
    chosen = jax.random.randint(third, (), 0, SEQS)
    whole = (jax.random.randint(second, (SEQS,), 0, 16) == 0) | (jnp.arange(SEQS) == chosen)
    return jnp.where(whole, LENGTH, shortest).astype(jnp.int32)


def strengthened(result, own_key, source, target, parts, factor):
    owner, partner = [(jnp.arange(result.shape[axis_at]) // (result.shape[axis_at] // parts)).reshape([-1 if axis == axis_at else 1 for axis in range(result.ndim)]) for axis_at in (source, target)]
    chosen = jax.random.permutation(own_key, parts)[partner]
    strong = (owner == chosen) | (owner == (partner + parts // 2) % parts)
    return jnp.where(strong, factor * result, result)


def levels(key, shape, cuts, low, top_value):
    level = 1.0
    for position, blocks in cuts:
        steps = jax.random.uniform(jax.random.fold_in(jax.random.fold_in(key, 6), position), (blocks,), jnp.float32, low / len(cuts), top_value / len(cuts))
        level = level * jnp.repeat(jnp.exp(steps), shape[position] // blocks).reshape((-1,) + (1,) * (len(shape) - 1 - position))
    return level


def gaussian(stream_key, shape, width, bound, pieces=(), held_as=jnp.bfloat16):
    factor_of = levels(stream_key, shape, pieces, -0.22, 0.18) if pieces else 1.0
    array = jax.random.normal(stream_key, shape, jnp.float32) * width * factor_of
    return jnp.minimum(jnp.maximum(array, -bound), bound).astype(held_as)


def heavy_noise(rng, extent, deviation, bound, cuts, heavy, kind=jnp.bfloat16):
    drawn = deviation * jax.random.normal(rng, extent, jnp.float32)
    if cuts:
        drawn = drawn * levels(rng, extent, cuts, -0.22, 0.18)
    return jnp.clip(strengthened(drawn, jax.random.fold_in(rng, 3), *heavy), -bound, bound).astype(kind)


def setup_inputs(seed: int = 0) -> dict:
    keys = jax.random.split(jax.random.key(seed), 19)
    tokens = heavy_noise(keys[0], (TOKENS, D), 1.0, 6.0, ((0, 16),), (0, 1, 16, 2.0))
    seq_lengths = draw_seq_lengths(jax.random.fold_in(keys[18], 71), 0)
    out_grad = heavy_noise(keys[2], (TOKENS, D), 1.0, 6.0, ((0, 16),), (0, 1, 16, 2.0))
    w_query = gaussian(keys[3], (D, D), D ** -0.5, 0.21875, ((1, 2),))
    bias_query = gaussian(keys[4], (D,), 0.3, 1.75, ((0, 2),))
    w_key = gaussian(keys[5], (D, D), D ** -0.5, 0.21875, ((1, 2),))
    w_value = gaussian(keys[6], (D, D), D ** -0.5, 0.21875, ((1, 2),))
    bias_value = gaussian(keys[7], (D,), 0.3, 1.75, ((0, 2),))
    w_out = gaussian(keys[8], (D, D), (max(D // 64, 8)) ** -0.5, 1.75, ((0, 2),))
    bias_out = gaussian(keys[9], (D,), 0.3, 1.75)
    gain_one = jnp.clip(1.0 + 0.15 * jax.random.normal(keys[10], (D,), jnp.float32), 0.25, 1.75).astype(jnp.bfloat16)
    shift_one = gaussian(keys[11], (D,), 0.3, 1.75)
    w_up = gaussian(keys[12], (D, FF), D ** -0.5, 0.21875, ((1, 2),))
    bias_up = gaussian(keys[13], (FF,), 0.3, 1.75, ((0, 2),))
    w_down = gaussian(keys[14], (FF, D), FF ** -0.5, 0.109375, ((0, 2),))
    bias_down = gaussian(keys[15], (D,), 0.3, 1.75)
    gain_two = jnp.clip(1.0 + 0.15 * jax.random.normal(keys[16], (D,), jnp.float32), 0.25, 1.75).astype(jnp.bfloat16)
    shift_two = gaussian(keys[17], (D,), 0.3, 1.75)
    return {"tokens": tokens, "seq_lengths": seq_lengths, "out_grad": out_grad, "w_query": w_query, "bias_query": bias_query, "w_key": w_key, "w_value": w_value, "bias_value": bias_value, "w_out": w_out, "bias_out": bias_out, "gain_one": gain_one, "shift_one": shift_one, "w_up": w_up, "bias_up": bias_up, "w_down": w_down, "bias_down": bias_down, "gain_two": gain_two, "shift_two": shift_two}


EPS = 1e-05

@jax.custom_vjp
def low(v):
    return lax.optimization_barrier(v.astype(jnp.bfloat16)).astype(jnp.float32)

@jax.custom_vjp
def low_back(v):
    return v

def low_keep(v):
    return (low(v), None)

def low_pass(kept, grad):
    return (grad,)

def back_keep(v):
    return (v, None)

def back_low(kept, grad):
    return (low(grad),)
low.defvjp(low_keep, low_pass)
low_back.defvjp(back_keep, back_low)

def product(left, right):
    return jnp.dot(left, right, precision=lax.Precision.HIGHEST, preferred_element_type=jnp.float32)

def layer_norm(values, gain, shift):
    average = lax.optimization_barrier(jnp.mean(values, axis=-1, keepdims=True))
    centred = values - average
    spread = lax.rsqrt(lax.optimization_barrier(jnp.mean(centred * centred, axis=-1, keepdims=True)) + EPS)
    return centred * spread * gain + shift

def forward(inputs, lengths, params):
    w_query, bias_query, w_key, w_value, bias_value, w_out, bias_out, gain_one, shift_one, w_up, bias_up, w_down, bias_down, gain_two, shift_two = params
    groups = inputs.shape[0]
    flat = inputs.reshape(groups * LENGTH, D)
    key_mask = jnp.arange(LENGTH)[None, :] < lengths[:, None]
    row_mask = key_mask.reshape(groups * LENGTH, 1).astype(jnp.float32)
    query = low(low_back(product(flat, w_query) + bias_query))
    keyed = low(low_back(product(flat, w_key)))
    valued = low(low_back(product(flat, w_value) + bias_value))

    def split_heads(values):
        return values.reshape(groups, LENGTH, HEADS, HEAD)
    raw = jnp.einsum('bqhd,bkhd->bhqk', split_heads(query), split_heads(keyed), precision=lax.Precision.HIGHEST) * HEAD ** (-0.5)
    masked = jnp.where(key_mask[:, None, None, :], low_back(raw), -1e+30)
    top = lax.optimization_barrier(jnp.max(masked, axis=-1, keepdims=True))
    expo = jnp.exp(masked - top)
    probs = low(expo / lax.optimization_barrier(jnp.sum(expo, axis=-1, keepdims=True)))
    mixed = jnp.einsum('bhqk,bkhd->bqhd', probs, split_heads(valued), precision=lax.Precision.HIGHEST)
    attended = low(low_back(mixed.reshape(groups * LENGTH, D)))
    attn_sum = low_back(product(attended, w_out))
    hidden = layer_norm(flat + (attn_sum + bias_out), gain_one, shift_one)
    up = low_back(product(low(hidden), w_up) + bias_up)
    act = low(jax.nn.gelu(up, approximate=False))
    ffn_sum = low_back(product(act, w_down))
    return layer_norm(hidden + ffn_sum + bias_down, gain_two, shift_two) * row_mask

def reference(tokens, seq_lengths, out_grad, w_query, bias_query, w_key, w_value, bias_value, w_out, bias_out, gain_one, shift_one, w_up, bias_up, w_down, bias_down, gain_two, shift_two):
    params = tuple((item.astype(jnp.float32) for item in (w_query, bias_query, w_key, w_value, bias_value, w_out, bias_out, gain_one, shift_one, w_up, bias_up, w_down, bias_down, gain_two, shift_two)))
    groups = math.gcd(SEQS, max(1, 4096 // LENGTH))
    count = SEQS // groups
    inputs = tokens.astype(jnp.float32).reshape(count, groups, LENGTH, D)
    cotangent = out_grad.astype(jnp.float32).reshape(count, groups, LENGTH * D)
    lengths = seq_lengths.reshape(count, groups)

    def step(totals, item):
        group_inputs, group_cot, group_lengths = item
        output, pull = jax.vjp(lambda first, second: forward(first, group_lengths, second), group_inputs, params)
        grad_inputs, grad_params = pull(group_cot.reshape(groups * LENGTH, D))
        totals = jax.tree.map(jnp.add, totals, grad_params)
        return (totals, (output.astype(jnp.bfloat16), grad_inputs.reshape(groups * LENGTH, D).astype(jnp.bfloat16)))
    zeros = jax.tree.map(jnp.zeros_like, params)
    totals, (outputs, grad_rows) = lax.scan(step, zeros, (inputs, cotangent, lengths))
    grad_wq, grad_bq, grad_wk, grad_wv, grad_bv, grad_wo, grad_bo, grad_g1, grad_s1, grad_wu, grad_bu, grad_wd, grad_bd, grad_g2, grad_s2 = totals
    return (outputs.reshape(TOKENS, D), grad_rows.reshape(TOKENS, D), grad_wq, grad_wk, grad_wv, grad_bq, grad_bv, grad_wo, grad_bo, grad_g1, grad_s1, grad_wu, grad_bu, grad_wd, grad_bd, grad_g2, grad_s2)
```

```python
import jax
import jax.numpy as jnp
from jax import lax
from jax.experimental import pallas as pl
from jax.experimental.pallas import tpu as pltpu
from jax.sharding import PartitionSpec as P

HEAD = 64
PAIR = 128
EPS = 1e-05
GROUPS = 16
BF16 = jnp.bfloat16
F32 = jnp.float32
ROWS = 128
HIDDEN = 512


def nn(left, right):
    return lax.dot_general(left, right, (((1,), (0,)), ((), ())), preferred_element_type=F32)


def nt(left, right):
    return lax.dot_general(left, right, (((1,), (1,)), ((), ())), preferred_element_type=F32)


def mean(values):
    return jnp.mean(values, axis=-1, keepdims=True)


def column_sum(values):
    return jnp.sum(values, axis=0, keepdims=True)


class Load:
    def __init__(self, source, target, sem):
        self.target = target
        self.copy = pltpu.make_async_copy(source, target, sem)
        self.copy.start()
        self.waited = False

    def ref(self):
        if not self.waited:
            self.copy.wait()
            self.waited = True
        return self.target


class Store:
    def __init__(self, target, buffer, sems, first):
        self.target, self.ref, self.sems, self.next = target, buffer, sems, first
        self.copies = []

    def send(self, *index):
        source = self.ref.at[index] if index else self.ref
        target = self.target.at[index] if index else self.target
        copy = pltpu.make_async_copy(source, target, self.sems.at[self.next])
        copy.start()
        self.next += 1
        self.copies.append(copy)

    def finish(self):
        if not self.copies:
            self.send()
        for copy in self.copies:
            copy.wait()


PARTS = 8


def call(body, name, info, ins, outs, scratch=(), vmem=40, flops=0, own_rows=()):
    n_in, n_out = len(ins), len(outs)

    def shape_of(at):
        array = ins[at]
        if at in own_rows:
            return (own_rows[at],) + array.shape[1:]
        return array.shape

    def kernel(info_ref, *refs):
        in_refs, refs = refs[:n_in], refs[n_in:]
        out_refs, refs = refs[:n_out], refs[n_out:]
        in_bufs, refs = refs[:n_in], refs[n_in:]
        out_bufs, refs = refs[:n_out], refs[n_out:]
        in_sems, out_sems, refs = refs[0], refs[1], refs[2:]
        loads = []
        for at in range(n_in):
            source = in_refs[at]
            if at in own_rows:
                rows = own_rows[at]
                source = source.at[pl.ds(pl.multiple_of(info_ref[0] * rows, rows), rows)]
            loads.append(Load(source, in_bufs[at], in_sems.at[at]))
        stores = [
            Store(out_refs[at], out_bufs[at], out_sems, at * PARTS) for at in range(n_out)
        ]
        body(info_ref, loads, stores, refs)
        for load in loads:
            load.ref()
        for store in stores:
            store.finish()

    moved = sum(a.size * a.dtype.itemsize for a in (*ins, *outs))
    return pl.pallas_call(
        kernel,
        name=name,
        out_shape=outs,
        in_specs=[pl.BlockSpec(memory_space=pltpu.SMEM)]
        + [pl.BlockSpec(memory_space=pl.ANY)] * n_in,
        out_specs=[pl.BlockSpec(memory_space=pl.ANY)] * n_out,
        scratch_shapes=[pltpu.VMEM(shape_of(at), ins[at].dtype) for at in range(n_in)]
        + [pltpu.VMEM(out.shape, out.dtype) for out in outs]
        + [pltpu.SemaphoreType.DMA((n_in,)), pltpu.SemaphoreType.DMA((n_out * PARTS,))]
        + list(scratch),
        compiler_params=pltpu.CompilerParams(vmem_limit_bytes=vmem * 2**20),
        cost_estimate=pl.CostEstimate(flops=flops, bytes_accessed=moved, transcendentals=0),
    )(info, *ins)


def shape(dims, dtype=BF16):
    return jax.ShapeDtypeStruct(dims, dtype)


def put_turned(info, target, values, at):
    turned = values.T
    size = turned.shape[0] // GROUPS
    for group in range(GROUPS):
        target[info[2 + group], :, at : at + values.shape[0]] = turned[
            group * size : (group + 1) * size
        ].astype(BF16)


def attend(info, tokens, w_query, w_key, w_value, bias, length, turn):
    width = w_query.shape[1]
    model = tokens.shape[1]
    heads = width // HEAD
    pairs = width // PAIR

    def body(info, loads, stores, scratch):
        rows, wq, wk, wv, vec = loads
        q_out, k_out, v_out, e_out, att_out, inv_out = stores[:6]
        (v_turned,) = scratch
        x = rows.ref()
        vec = vec.ref()
        q_out.ref[...] = (
            (nn(x[...], wq.ref()[...]) + vec[0:1]).astype(BF16).astype(F32) * HEAD**-0.5
        ).astype(BF16)
        k_out.ref[...] = nn(x[...], wk.ref()[...]).astype(BF16)
        value = (nn(x[...], wv.ref()[...]) + vec[1:2]).astype(BF16)
        v_out.ref[...] = value
        v_turned[...] = value.astype(F32).T.astype(BF16)
        for out in (q_out, k_out, v_out):
            out.send()
        lane = lax.broadcasted_iota(jnp.int32, (length, PAIR), 1)
        row = lax.broadcasted_iota(jnp.int32, (length, PAIR), 0)
        masked = jnp.where((lane == 0) & (row >= info[1]), -1e30, 0.0).astype(BF16)
        marker = jnp.where(lane == 0, 1.0, 0.0).astype(BF16)
        ones = jnp.ones((16, length), BF16)
        for pair in range(pairs):
            cut = slice(pair * PAIR, (pair + 1) * PAIR)
            queries = q_out.ref[:, cut]
            keys = jnp.concatenate([k_out.ref[:, cut], masked], axis=1)
            mixed, inverse = [], []
            for half in range(2):
                head = pair * 2 + half
                own = jnp.where(lane // HEAD == half, queries, jnp.zeros_like(queries))
                scores = nt(keys, jnp.concatenate([own, marker], axis=1))
                top = jnp.max(scores, axis=0, keepdims=True)
                e_out.ref[head] = jnp.exp(scores - top).astype(BF16)
                e_out.send(head)
                left = jnp.concatenate([v_turned[head * HEAD : (head + 1) * HEAD], ones], axis=0)
                sums = nn(left, e_out.ref[head])
                inv = 1.0 / sums[HEAD : HEAD + 1]
                mixed.append(sums[:HEAD] * inv)
                inverse.append(jnp.broadcast_to(inv, (HEAD, length)))
            att_out.ref[:, cut] = jnp.concatenate(mixed, axis=0).T.astype(BF16)
            inv_out.ref[:, cut] = jnp.concatenate(inverse, axis=0).T
        if turn:
            for start in range(0, length, ROWS):
                put_turned(
                    info, stores[6].ref, x[start : start + ROWS, :].astype(F32), start
                )

    outs = [
        shape((length, width)),
        shape((length, width)),
        shape((length, width)),
        shape((heads, length, length)),
        shape((length, width)),
        shape((length, width), F32),
    ]
    if turn:
        outs.append(shape((GROUPS, model // GROUPS, length)))
    return call(
        body,
        "attend",
        info,
        [tokens, w_query, w_key, w_value, bias],
        outs,
        scratch=[pltpu.VMEM((width, length), BF16)],
        vmem=32,
        flops=2 * length * (3 * model * width + 4 * length * width),
        own_rows={0: length},
    )


def forward(info, tokens, out_grad, vectors, att, w_out, bias_up, w_up, w_down, length):
    model = tokens.shape[1]
    inner = w_up[0].shape[1]
    size = model // GROUPS

    def body(info, loads, stores, scratch):
        rows, cot, vec = loads[:3]
        att_a, att_b, wo_a, wo_b = loads[3:7]
        bu_a, bu_b, wu_a, wu_b, wd_a, wd_b = loads[7:13]
        (layer_out, normed_out, spread_out, turned_out, grad_turned, grad_out, grad_low) = stores[:7]
        act_a, act_b, slope_a, slope_b, small_out, down_out = stores[7:]
        total, hidden, low = scratch
        total[...] = nn(att_a.ref()[...], wo_a.ref()[...]) + nn(att_b.ref()[...], wo_b.ref()[...])
        vec = vec.ref()
        x = rows.ref()
        bo, g1, s1, bd, g2, s2 = (vec[i : i + 1] for i in range(6))
        for start in range(0, length, ROWS):
            cut = slice(start, start + ROWS)
            value = x[cut].astype(F32) + (total[cut] + bo)
            centred = value - mean(value)
            spread = lax.rsqrt(mean(centred * centred) + EPS)
            normed = centred * spread
            normed_out.ref[cut] = normed
            spread_out.ref[cut] = jnp.broadcast_to(spread, (ROWS, 128))
            full = normed * g1 + s1
            hidden[cut] = full
            low[cut] = full.astype(BF16)
            put_turned(info, turned_out.ref, full, start)
        for out in (normed_out, spread_out, turned_out):
            out.send()
        first = True
        for wu, bu, wd, act_out, slope_out in (
            (wu_a, bu_a, wd_a, act_a, slope_a),
            (wu_b, bu_b, wd_b, act_b, slope_b),
        ):
            for start in range(0, inner, HIDDEN):
                cut = slice(start, start + HIDDEN)
                up = nn(low[...], wu.ref()[:, cut]) + bu.ref()[0:1, cut]
                phi = 0.5 * (1.0 + lax.erf(up * (0.5**0.5)))
                act_out.ref[:, cut] = (up * phi).astype(BF16)
                slope_out.ref[:, cut] = (
                    phi + up * (jnp.exp(-0.5 * up * up) * 0.3989422804014327)
                ).astype(BF16)
                part = nn(act_out.ref[:, cut], wd.ref()[cut, :])
                if first:
                    total[...] = part
                    first = False
                else:
                    total[...] += part
            act_out.send()
            slope_out.send()
        cot = cot.ref()
        sums = [jnp.zeros((1, model), F32)] * 3
        for start in range(0, length, ROWS):
            cut = slice(start, start + ROWS)
            place = lax.broadcasted_iota(jnp.int32, (ROWS, model), 0) + start
            valid = jnp.where(place < info[1], 1.0, 0.0)
            value = hidden[cut] + total[cut] + bd
            centred = value - mean(value)
            spread = lax.rsqrt(mean(centred * centred) + EPS)
            normed = centred * spread
            layer_out.ref[cut] = ((normed * g2 + s2) * valid).astype(BF16)
            grad = cot[cut].astype(F32) * valid
            scaled = grad * g2
            resid = spread * (scaled - mean(scaled) - normed * mean(scaled * normed))
            sums = [
                sums[0] + column_sum(grad * normed),
                sums[1] + column_sum(grad),
                sums[2] + column_sum(resid),
            ]
            grad_out.ref[cut] = resid
            grad_low.ref[cut] = resid.astype(BF16)
            put_turned(info, grad_turned.ref, resid, start)
        for at in range(3):
            small_out.ref[at : at + 1] = sums[at]
        small_out.ref[3:8] = jnp.zeros((5, model), F32)
        for out in (layer_out, grad_turned, grad_out, grad_low, small_out):
            out.send()
        weight_part(down_out, grad_turned.ref, act_b.ref, inner, size, True)

    outs = [
        shape((length, model)),
        shape((length, model), F32),
        shape((length, 128), F32),
        shape((GROUPS, size, length)),
        shape((GROUPS, size, length)),
        shape((length, model), F32),
        shape((length, model)),
        shape((length, inner)),
        shape((length, inner)),
        shape((length, inner)),
        shape((length, inner)),
        shape((8, model), F32),
        shape((model, inner)),
    ]
    return call(
        body,
        "forward",
        info,
        [tokens, out_grad, vectors, *att, *w_out, *bias_up, *w_up, *w_down],
        outs,
        scratch=[
            pltpu.VMEM((length, model), F32),
            pltpu.VMEM((length, model), F32),
            pltpu.VMEM((length, model), BF16),
        ],
        vmem=56,
        flops=2 * length * (model * model + 5 * model * inner),
        own_rows={0: length, 1: length},
    )


SWAP = [True]


def left_rows(turned, quarter):
    part = turned[quarter * 4 : (quarter + 1) * 4]
    return part.reshape(part.shape[0] * part.shape[1], part.shape[2])


def weight_part(out, turned, right, inner, size, partner):
    rows = size * 4
    order = (0, 2, 1, 3) if partner and SWAP[0] else (0, 1, 2, 3)
    for quarter in range(4):
        left = left_rows(turned, quarter)
        to = order[quarter]
        for start in range(0, inner, HIDDEN):
            cut = slice(start, min(start + HIDDEN, inner))
            out.ref[to * rows : (to + 1) * rows, cut] = nn(left, right[:, cut]).astype(BF16)
        out.send(pl.ds(to * rows, rows))


def weight_own(keep, send, turned, right, came, inner, size):
    rows = size * 4
    for quarter in (2, 3, 0, 1):
        out = send if quarter >= 2 else keep
        to = quarter % 2
        left = left_rows(turned, quarter)
        for start in range(0, inner, HIDDEN):
            cut = slice(start, min(start + HIDDEN, inner))
            other = came[quarter * rows : (quarter + 1) * rows, cut].astype(F32)
            out.ref[to * rows : (to + 1) * rows, cut] = (nn(left, right[:, cut]) + other).astype(BF16)
        out.send(pl.ds(to * rows, rows))


def up_back(info, grad_low, w_down, slope, turned, w_up, length):
    model, inner = w_up.shape
    size = model // GROUPS

    def body(info, loads, stores, scratch):
        grad, wd, slopes, left, wu = loads
        out, back, bias = stores
        (ups,) = scratch
        grad = grad.ref()
        for start in range(0, inner, HIDDEN):
            cut = slice(start, start + HIDDEN)
            value = nt(grad[...], wd.ref()[cut, :]) * slopes.ref()[:, cut].astype(F32)
            value = value.astype(BF16)
            ups[:, cut] = value
            bias.ref[:, cut] = jnp.broadcast_to(column_sum(value.astype(F32)), (8, HIDDEN))
        weight_part(out, left.ref(), ups, inner, size, True)
        back.ref[...] = nt(ups[...], wu.ref()[...])

    return call(
        body,
        "up_back",
        info,
        [grad_low, w_down, slope, turned, w_up],
        [shape((model, inner)), shape((length, model), F32), shape((8, inner), F32)],
        scratch=[pltpu.VMEM((length, inner), BF16)],
        vmem=32,
        flops=6 * length * model * inner,
    )


def down_own(info, turned, act, came, length):
    model = came.shape[0]
    inner = came.shape[1]
    size = model // GROUPS

    def body(info, loads, stores, scratch):
        left, right, other = loads
        keep, send = stores
        weight_own(keep, send, left.ref(), right.ref(), other.ref(), inner, size)

    half = shape((model // 2, inner))
    return call(
        body,
        "down_own",
        info,
        [turned, act, came],
        [half, half],
        vmem=24,
        flops=2 * length * model * inner,
    )


def up_own(info, grad_low, w_down, slope, w_up, resid, back, normed, spread, vectors, length):
    model, inner = w_up.shape
    size = model // GROUPS

    def body(info, loads, stores, scratch):
        grad, wd, slopes, wu, grad_resid, share, norm, spr, vec = loads
        ups, first_out, low_out, turned_out, small_out, bias = stores
        (total,) = scratch
        grad = grad.ref()
        for start in range(0, inner, HIDDEN):
            cut = slice(start, start + HIDDEN)
            value = nt(grad[...], wd.ref()[cut, :]) * slopes.ref()[:, cut].astype(F32)
            value = value.astype(BF16)
            ups.ref[:, cut] = value
            bias.ref[:, cut] = jnp.broadcast_to(column_sum(value.astype(F32)), (8, HIDDEN))
        ups.send()
        total[...] = nt(ups.ref[...], wu.ref()[...])
        gain = vec.ref()[1:2]
        sums = [jnp.zeros((1, model), F32)] * 3
        grad_resid, share, norm, spr = (item.ref() for item in (grad_resid, share, norm, spr))
        for start in range(0, length, ROWS):
            cut = slice(start, start + ROWS)
            value = grad_resid[cut] + (total[cut] + share[cut])
            normed = norm[cut]
            scaled = value * gain
            first = spr[cut, 0:1] * (scaled - mean(scaled) - normed * mean(scaled * normed))
            sums = [
                sums[0] + column_sum(value * normed),
                sums[1] + column_sum(value),
                sums[2] + column_sum(first),
            ]
            first_out.ref[cut] = first
            low_out.ref[cut] = first.astype(BF16)
            put_turned(info, turned_out.ref, first, start)
        for at in range(3):
            small_out.ref[at : at + 1] = sums[at]
        small_out.ref[3:8] = jnp.zeros((5, model), F32)

    return call(
        body,
        "up_own",
        info,
        [grad_low, w_down, slope, w_up, resid, back, normed, spread, vectors],
        [
            shape((length, inner)),
            shape((length, model), F32),
            shape((length, model)),
            shape((GROUPS, size, length)),
            shape((8, model), F32),
            shape((8, inner), F32),
        ],
        scratch=[pltpu.VMEM((length, model), F32)],
        vmem=32,
        flops=4 * length * model * inner,
    )


def attend_back(info, low, first_turned, token_turned, w_out, saved, came, length):
    query, keyed, valued, expo, att, inv = saved
    width, model = w_out.shape
    size = model // GROUPS
    pairs = width // PAIR

    def body(info, loads, stores, scratch):
        grad, first_t, token_t, wo, q, k, v, e, attended, inverse = loads[:10]
        dq, dk, dv, bias = stores[:4]
        grads_out = stores[4:]
        mixed, k_turned = scratch
        mixed[...] = nt(grad.ref()[...], wo.ref()[...]).astype(BF16)
        q, k, v = q.ref(), k.ref(), v.ref()
        k_turned[...] = k[...].astype(F32).T.astype(BF16)
        e, attended, inverse = e.ref(), attended.ref(), inverse.ref()
        lane = lax.broadcasted_iota(jnp.int32, (length, PAIR), 1)
        marker = jnp.where(lane < 2, 1.0, 0.0).astype(BF16)
        for pair in range(pairs):
            cut = slice(pair * PAIR, (pair + 1) * PAIR)
            scaled = mixed[:, cut].astype(F32) * inverse[:, cut]
            product = scaled * attended[:, cut].astype(F32)
            scaled = scaled.astype(BF16)
            values = jnp.concatenate([v[:, cut], marker], axis=1)
            queries = q[:, cut]
            dvs, dks, dqs = [], [], []
            for half in range(2):
                head = pair * 2 + half
                mine = lane // HEAD == half
                inner = -jnp.sum(jnp.where(mine, product, 0.0), axis=1, keepdims=True)
                high = inner.astype(BF16).astype(F32)
                extra = jnp.where(lane == 0, high, jnp.where(lane == 1, inner - high, 0.0))
                right = jnp.concatenate(
                    [jnp.where(mine, scaled, jnp.zeros_like(scaled)), extra.astype(BF16)], axis=1
                )
                scores = (e[head].astype(F32) * nt(values, right)).astype(BF16)
                dvs.append(nn(e[head], scaled))
                dks.append(nn(scores, queries))
                dqs.append(nn(k_turned[head * HEAD : (head + 1) * HEAD], scores))
            dv.ref[:, cut] = jnp.where(lane < HEAD, dvs[0], dvs[1]).astype(BF16)
            dk.ref[:, cut] = jnp.where(lane < HEAD, dks[0], dks[1]).astype(BF16)
            dq.ref[:, cut] = (jnp.concatenate(dqs, axis=0).T * HEAD**-0.5).astype(BF16)
        bias.ref[...] = jnp.zeros_like(bias.ref)
        bias.ref[0:1] = column_sum(dq.ref[...].astype(F32))
        bias.ref[1:2] = column_sum(dv.ref[...].astype(F32))
        for out in (dq, dk, dv, bias):
            out.send()
        jobs = (
            (token_t.ref(), dq.ref),
            (token_t.ref(), dk.ref),
            (token_t.ref(), dv.ref),
            (first_t.ref(), attended),
        )
        rows = size * 4
        if came is None:
            order = (0, 2, 1, 3) if SWAP[0] else (0, 1, 2, 3)
            for quarter in range(4):
                to = order[quarter]
                for at, (left, right) in enumerate(jobs):
                    grads_out[0].ref[to * rows : (to + 1) * rows, at * width : (at + 1) * width] = nn(
                        left_rows(left, quarter), right[...]
                    ).astype(BF16)
                grads_out[0].send(pl.ds(to * rows, rows))
        else:
            other = loads[10].ref()
            keep, send = grads_out
            for quarter in (2, 3, 0, 1):
                out = send if quarter >= 2 else keep
                to = quarter % 2
                for at, (left, right) in enumerate(jobs):
                    add = other[quarter * rows : (quarter + 1) * rows, at * width : (at + 1) * width]
                    out.ref[to * rows : (to + 1) * rows, at * width : (at + 1) * width] = (
                        nn(left_rows(left, quarter), right[...]) + add.astype(F32)
                    ).astype(BF16)
                out.send(pl.ds(to * rows, rows))

    some = shape((length, width))
    outs = [some, some, some, shape((8, width), F32)]
    if came is None:
        outs.append(shape((model, 4 * width)))
    else:
        outs += [shape((model // 2, 4 * width))] * 2
    ins = [low, first_turned, token_turned, w_out, query, keyed, valued, expo, att, inv]
    if came is not None:
        ins.append(came)
    return call(
        body,
        "attend_back",
        info,
        ins,
        outs,
        scratch=[pltpu.VMEM((length, width), BF16), pltpu.VMEM((width, length), BF16)],
        vmem=40,
        flops=2 * length * width * (5 * model + 8 * length),
    )


def input_part(info, first, parts, weights, length):
    model = first.shape[1]

    def body(info, loads, stores, scratch):
        total = loads[0].ref()[...]
        for at in range(6):
            total += nt(loads[1 + at].ref()[...], loads[7 + at].ref()[...])
        stores[0].ref[...] = total.astype(BF16)

    return call(
        body,
        "input_part",
        info,
        [first, *parts, *weights],
        [shape((length, model))],
        vmem=24,
        flops=6 * length * model * model,
    )


def both(values, tp):
    other = swap(values)
    first = tp == 0
    return jnp.concatenate([jnp.where(first, values, other), jnp.where(first, other, values)], axis=0)


def swap(values):
    return lax.ppermute(values, "tp", [(0, 1), (1, 0)])


def flips(size, bits):
    return [(2 * d + c, 2 * (d ^ bits[c]) + c) for d in range(size) for c in range(2)]


def flip(values, size, *bits):
    bits = bits if len(bits) == 2 else bits * 2
    return lax.ppermute(values, ("dp", "tp"), flips(size, bits))


def add(left, right):
    return left.astype(F32) + right.astype(F32)


def scatter(keep, send, dp):
    rows, columns = keep.shape
    if dp != GROUPS:
        whole = jnp.concatenate([keep, send], axis=0).astype(F32)
        return lax.psum_scatter(whole, "dp", scatter_dimension=0, tiled=True)
    came = flip(send, dp, 1, 2)
    half = rows // 2
    onward = add(keep[half:], came[half:]).astype(BF16)
    came_next = flip(onward, dp, 2, 1)
    mine = (add(keep[:half], came[:half]) + came_next.astype(F32)).astype(BF16)
    share = half // 4
    parts = [mine[at * share : (at + 1) * share] for at in range(4)]
    others = [flip(parts[at], dp, 4 * at) for at in (1, 2, 3)]
    return add(parts[0], others[0]) + add(others[1], others[2])


def gather_sum(values, dp):
    if dp != GROUPS:
        return lax.psum(values, "dp")
    values = values + flip(values, dp, 1)
    values = values + flip(values, dp, 2)
    others = [flip(values, dp, 4 * at) for at in (1, 2, 3)]
    return (values + others[0]) + (others[1] + others[2])


def local(
    tokens,
    seq_lengths,
    out_grad,
    w_query,
    bias_query,
    w_key,
    w_value,
    bias_value,
    w_out,
    bias_out,
    gain_one,
    shift_one,
    w_up,
    bias_up,
    w_down,
    bias_down,
    gain_two,
    shift_two,
):
    dp = lax.axis_size("dp")
    tp = lax.axis_index("tp")
    place = lax.axis_index("dp")
    SWAP[0] = dp == GROUPS
    model = tokens.shape[1]
    length = tokens.shape[0] // seq_lengths.shape[0]
    width = w_query.shape[1]
    inner = w_up.shape[1]

    group = jnp.arange(GROUPS, dtype=jnp.int32)
    if dp == GROUPS:
        rel = group ^ place
        x_bit, y_bit, z_bits = rel & 1, (rel >> 1) & 1, rel >> 2
        near, far = jnp.where(tp == 0, x_bit, y_bit), jnp.where(tp == 0, y_bit, x_bit)
        group = (near * 2 + far) * 4 + z_bits
    own_length = lax.dynamic_index_in_dim(seq_lengths, tp, keepdims=True)
    info = jnp.concatenate([tp.reshape(1).astype(jnp.int32), own_length, group])

    wq_b, wk_b, wv_b = swap(w_query), swap(w_key), swap(w_value)
    biases = jnp.concatenate([bias_query, bias_value, bias_up])
    biases_b = swap(biases)
    wo_b, wu_b, wd_b = swap(w_out), swap(w_up), swap(w_down)

    def bias_rows(flat):
        flat = flat.astype(F32)
        return flat[: 2 * width].reshape(2, width), flat[2 * width :].reshape(1, inner)

    vectors = jnp.stack(
        [bias_out, gain_one, shift_one, bias_down, gain_two, shift_two] + [bias_out] * 2
    ).astype(F32)
    qv_a, bu_a = bias_rows(biases)
    qv_b, bu_b = bias_rows(biases_b)

    *saved_a, token_turned = attend(info, tokens, w_query, w_key, w_value, qv_a, length, True)
    saved_b = attend(info, tokens, wq_b, wk_b, wv_b, qv_b, length, False)
    (
        layer_own,
        normed,
        spread,
        hidden_turned,
        grad_turned,
        resid,
        grad_low,
        act_a,
        act_b,
        slope_a,
        slope_b,
        small_two,
        down_b,
    ) = forward(
        info,
        tokens,
        out_grad,
        vectors,
        (saved_a[4], saved_b[4]),
        (w_out, wo_b),
        (bu_a, bu_b),
        (w_up, wu_b),
        (w_down, wd_b),
        length,
    )
    down_came = swap(down_b)
    up_b, back_b, bias_up_b = up_back(info, grad_low, wd_b, slope_b, hidden_turned, wu_b, length)
    up_came = swap(up_b)
    down_keep, down_send = down_own(info, grad_turned, act_a, down_came, length)
    grad_down = scatter(down_keep, down_send, dp).T
    ups, first, first_low, first_turned, small_one, bias_up_a = up_own(
        info, grad_low, w_down, slope_a, w_up, resid, back_b, normed, spread, vectors, length
    )
    up_keep, up_send = down_own(info, hidden_turned, ups, up_came, length)
    grad_up = scatter(up_keep, up_send, dp)
    layer_output = both(layer_own, tp)
    dq_b, dk_b, dv_b, bias_b, heads_b = attend_back(
        info, first_low, first_turned, token_turned, wo_b, saved_b, None, length
    )
    heads_came = swap(heads_b)
    common = jnp.concatenate([small_two[:3], small_one[:3]], axis=0).reshape(-1)
    small_send = jnp.concatenate([common, bias_up_b[0], bias_b[0], bias_b[1]]).reshape(-1, 128)
    small_came = swap(small_send)
    dq_a, dk_a, dv_a, bias_a, heads_keep, heads_send = attend_back(
        info, first_low, first_turned, token_turned, w_out, saved_a, heads_came, length
    )
    grad_heads = scatter(heads_keep, heads_send, dp)
    small = jnp.concatenate([common, bias_up_a[0], bias_a[0], bias_a[1]]).reshape(-1, 128)
    small = gather_sum(small + small_came, dp).reshape(-1)
    (input_own,) = input_part(
        info,
        first,
        (dq_a, dk_a, dv_a, dq_b, dk_b, dv_b),
        (w_query, w_key, w_value, wq_b, wk_b, wv_b),
        length,
    )
    input_grad = both(input_own, tp)

    def cut(start, size):
        return small[start : start + size]

    return (
        layer_output,
        input_grad,
        grad_heads[:, :width],
        grad_heads[:, width : 2 * width],
        grad_heads[:, 2 * width : 3 * width],
        cut(6 * model + inner, width),
        cut(6 * model + inner + width, width),
        grad_heads[:, 3 * width :].T,
        cut(5 * model, model),
        cut(3 * model, model),
        cut(4 * model, model),
        grad_up,
        cut(6 * model, inner),
        grad_down,
        cut(2 * model, model),
        cut(0, model),
        cut(model, model),
    )


def solution(mesh):
    return jax.shard_map(
        local,
        mesh=mesh,
        in_specs=(
            P("dp", None),
            P("dp"),
            P("dp", None),
            P(None, "tp"),
            P("tp"),
            P(None, "tp"),
            P(None, "tp"),
            P("tp"),
            P("tp", None),
            P(),
            P(),
            P(),
            P(None, "tp"),
            P("tp"),
            P("tp", None),
            P(),
            P(),
            P(),
        ),
        out_specs=(
            P("dp", None),
            P("dp", None),
            P("dp", "tp"),
            P("dp", "tp"),
            P("dp", "tp"),
            P("tp"),
            P("tp"),
            P("tp", "dp"),
            P(),
            P(),
            P(),
            P("dp", "tp"),
            P("tp"),
            P("tp", "dp"),
            P(),
            P(),
            P(),
        ),
        check_vma=False,
    )
```

```python
import jax
import jax.numpy as jnp
from jax import lax
from jax.experimental import pallas as pl
from jax.experimental.pallas import tpu as pltpu
from jax.sharding import PartitionSpec as P

HEAD = 64
PAIR = 128
EPS = 1e-05
GROUPS = 16
BF16 = jnp.bfloat16
F32 = jnp.float32
ROWS = 128
HIDDEN = 512


def nn(left, right):
    return lax.dot_general(left, right, (((1,), (0,)), ((), ())), preferred_element_type=F32)


def nt(left, right):
    return lax.dot_general(left, right, (((1,), (1,)), ((), ())), preferred_element_type=F32)


def mean(values):
    return jnp.mean(values, axis=-1, keepdims=True)


def column_sum(values):
    return jnp.sum(values, axis=0, keepdims=True)


class Load:
    def __init__(self, source, target, sems, first, item):
        self.target, self.item = target, item
        self.copies = [
            pltpu.make_async_copy(*item.ends(source, target, at), sems.at[first + at])
            for at in range(item.parts)
        ]
        self.waited = set()

    def part(self, at):
        if at not in self.waited:
            self.copies[at].wait()
            self.waited.add(at)
        return self.target

    def columns(self, start, stop):
        if self.item.parts > 1:
            size = self.item.dims[self.item.axis] // self.item.parts
            for at in range(start // size, -(-stop // size)):
                self.part(at)
            return self.target
        return self.ref()

    def ref(self):
        for at in range(len(self.copies)):
            self.part(at)
        return self.target


class Store:
    def __init__(self, target, buffer, sems, first):
        self.target, self.ref, self.sems, self.next = target, buffer, sems, first
        self.copies = []

    def send(self, *index):
        source = self.ref.at[index] if index else self.ref
        target = self.target.at[index] if index else self.target
        copy = pltpu.make_async_copy(source, target, self.sems.at[self.next])
        copy.start()
        self.next += 1
        self.copies.append(copy)

    def finish(self):
        for copy in self.copies:
            copy.wait()


PARTS = 8


class Whole:
    def __init__(self, array, parts=1, axis=-1, late=False):
        self.array, self.dims = array, array.shape
        self.parts, self.axis, self.late = parts, axis % array.ndim, late

    def ends(self, source, target, at):
        if self.parts == 1:
            return source, target
        size = self.dims[self.axis] // self.parts
        cut = tuple(
            pl.ds(at * size, size) if axis == self.axis else pl.ds(0, dim)
            for axis, dim in enumerate(self.dims)
        )
        return source.at[cut], target.at[cut]


class OwnRows(Whole):
    def __init__(self, array, rows, late=False):
        super().__init__(array, late=late)
        self.dims = (rows,) + array.shape[1:]

    def ends(self, source, target, at):
        rows = self.dims[0]
        start = pl.multiple_of(lax.axis_index("tp") * rows, rows)
        return source.at[pl.ds(start, rows)], target


class BothRows(Whole):
    def __init__(self, array, rows):
        super().__init__(array, 2, 0)
        self.rows = rows

    def ends(self, source, target, at):
        core = lax.axis_index("tp")
        start = pl.multiple_of((core if at == 0 else 1 - core) * self.rows, self.rows)
        return source.at[pl.ds(start, self.rows)], target.at[pl.ds(at * self.rows, self.rows)]


def call(body, name, lengths, ins, outs, scratch=(), vmem=64, after=(), joins=()):
    ins = [item if isinstance(item, Whole) else Whole(item) for item in ins]
    n_in, n_out, n_after, n_join = len(ins), len(outs), len(after), len(joins)
    joined = [shape((2 * own.shape[0],) + own.shape[1:], own.dtype) for own, _ in joins]

    def kernel(lengths_ref, *refs):
        in_refs, refs = refs[:n_in], refs[n_in + n_after :]
        pair_refs, refs = refs[: 2 * n_join], refs[2 * n_join :]
        out_refs, refs = refs[:n_out], refs[n_out:]
        join_refs, refs = refs[:n_join], refs[n_join:]
        in_bufs, refs = refs[:n_in], refs[n_in:]
        out_bufs, refs = refs[:n_out], refs[n_out:]
        join_bufs, refs = refs[:n_join], refs[n_join:]
        in_sems, out_sems, join_sems, refs = refs[0], refs[1], refs[2], refs[3:]
        core = lax.axis_index("tp")
        copies = []
        for at in range(n_join):
            for side in range(2):
                source = pair_refs[2 * at + side]
                rows = source.shape[0]
                start = pl.multiple_of((core if side == 0 else 1 - core) * rows, rows)
                copies.append(
                    pltpu.make_async_copy(
                        source, join_bufs[at].at[pl.ds(start, rows)], join_sems.at[2 * at + side]
                    )
                )
        loads, first = [], 0
        for item, source, buffer in zip(ins, in_refs, in_bufs):
            loads.append(Load(source, buffer, in_sems, first, item))
            first += item.parts
        for late in (False, True):
            for at in range(max(item.parts for item in ins) if ins else 0):
                for load in loads:
                    if load.item.late == late and at < load.item.parts:
                        load.copies[at].start()
        stores = [
            Store(out_refs[at], out_bufs[at], out_sems, at * PARTS) for at in range(n_out)
        ]
        for copy in copies:
            copy.start()
        started = []

        def join():
            for copy in copies:
                copy.wait()
            for at in range(n_join):
                started.append(
                    pltpu.make_async_copy(join_bufs[at], join_refs[at], join_sems.at[2 * at])
                )
                started[-1].start()
            copies.clear()

        body(lengths_ref, loads, stores, (*refs, join))
        if copies:
            join()
        for store in stores:
            if not store.copies:
                store.send()
        for load in loads:
            load.ref()
        for store in stores:
            store.finish()
        for copy in started:
            copy.wait()

    return pl.pallas_call(
        kernel,
        name=name,
        out_shape=[*outs, *joined],
        in_specs=[pl.BlockSpec(memory_space=pltpu.SMEM)]
        + [pl.BlockSpec(memory_space=pl.ANY)] * (n_in + n_after + 2 * n_join),
        out_specs=[pl.BlockSpec(memory_space=pl.ANY)] * (n_out + n_join),
        scratch_shapes=[pltpu.VMEM(item.dims, item.array.dtype) for item in ins]
        + [pltpu.VMEM(out.shape, out.dtype) for out in [*outs, *joined]]
        + [
            pltpu.SemaphoreType.DMA((sum(item.parts for item in ins) + 1,)),
            pltpu.SemaphoreType.DMA((max(n_out, 1) * PARTS,)),
            pltpu.SemaphoreType.DMA((max(2 * n_join, 1),)),
        ]
        + list(scratch),
        compiler_params=pltpu.CompilerParams(vmem_limit_bytes=vmem * 2**20),
        cost_estimate=pl.CostEstimate(flops=1, bytes_accessed=1, transcendentals=0),
    )(lengths, *(item.array for item in ins), *after, *(item for pair in joins for item in pair))


def line(load):
    ref = load.ref()
    return ref[...].astype(F32).reshape(1, ref.shape[0])


def length_of(lengths, at):
    core = lax.axis_index("tp")
    return lengths[core if at == 0 else 1 - core]


def places(order):
    if not SWAP[0]:
        return list(range(GROUPS))
    place, core = lax.axis_index("dp"), lax.axis_index("tp")
    found = []
    for group in range(GROUPS):
        rel = jnp.bitwise_xor(place, group)
        bits = [rel % 2, (rel // 2) % 2, (rel // 4) % 2, rel // 8]
        near = jnp.where(core == 0, bits[0], bits[1])
        bits[:2] = near, bits[0] + bits[1] - near
        found.append(sum(bit * (8 // 2**step) for bit, step in zip(bits, order)))
    return found


PLANE_FIRST = (0, 1, 2, 3)
Z_BETWEEN = (0, 2, 1, 3)


Z_FIRST = (1, 2, 0, 3)


def reordered(at, order, other):
    if not SWAP[0]:
        return at
    return sum((at >> (3 - step) & 1) << (3 - to) for step, to in zip(order, other))


def partner_place(at, order):
    if not SWAP[0]:
        return at
    near, far = 8 // 2 ** order[0], 8 // 2 ** order[1]
    left, right = bool(at & near), bool(at & far)
    return at if left == right else at ^ near ^ far


def by_length(lengths, at, length, run):
    count = length_of(lengths, at)
    sizes = [size for size in (128, 256) if size < length] + [length]
    below = None
    for size in sizes:
        fits = count <= size
        if below is not None:
            fits = fits & (count > below)

        @pl.when(fits)
        def _(size=size):
            run(size)

        below = size


def shape(dims, dtype=BF16):
    return jax.ShapeDtypeStruct(dims, dtype)


def put_turned(place, target, values, at):
    turned = values.T
    size = turned.shape[0] // GROUPS
    for group in range(GROUPS):
        target[place[group], :, at : at + values.shape[0]] = turned[
            group * size : (group + 1) * size
        ].astype(BF16)


def attend(lengths, tokens, w_query, w_key, w_value, bias_query, bias_value, length):
    width = w_query.shape[1]
    model = tokens.shape[1]
    heads = width // HEAD

    def body(lengths, loads, stores, scratch):
        rows, wk, wq, wv, bq, bv = loads
        q_out, k_out, v_out, e_out, own_out, other_out, inv_out, turned_out = stores
        (v_turned,) = scratch[:1]
        bq, bv = line(bq), line(bv)

        def lanes(head):
            return slice(head // 2 * PAIR, (head // 2 + 1) * PAIR)

        def sequence(at, size):
            near = slice(at * length, at * length + size)
            lane = lax.broadcasted_iota(jnp.int32, (size, PAIR), 1)
            row = lax.broadcasted_iota(jnp.int32, (size, PAIR), 0)
            count = length_of(lengths, at)
            masked = jnp.where((lane == 0) & (row >= count), -1e30, 0.0).astype(BF16)
            marker = jnp.where(lane == 0, 1.0, 0.0).astype(BF16)
            ones = jnp.ones((16, size), BF16)
            att_out = (own_out, other_out)[at]

            def scores(head):
                queries = q_out.ref[near, lanes(head)]
                own = jnp.where(lane // HEAD == head % 2, queries, jnp.zeros_like(queries))
                keys = jnp.concatenate([k_out.ref[near, lanes(head)], masked], axis=1)
                return nt(keys, jnp.concatenate([own, marker], axis=1))

            mixed, inverse = [], []

            def mix(head):
                values = v_turned[at, head * HEAD : (head + 1) * HEAD, :size]
                left = jnp.concatenate([values, ones], axis=0)
                sums = nn(left, e_out.ref[at * heads + head, :size, :size])
                inv = 1.0 / sums[HEAD : HEAD + 1]
                mixed.append(sums[:HEAD] * inv)
                inverse.append(jnp.broadcast_to(inv, (HEAD, size)))
                if head % 2:
                    att_out.ref[:size, lanes(head)] = (
                        jnp.concatenate(mixed, axis=0).astype(BF16).T
                    )
                    inv_out.ref[near, lanes(head)] = jnp.concatenate(inverse, axis=0).T
                    mixed.clear()
                    inverse.clear()

            now = scores(0)
            for head in range(heads):
                later = scores(head + 1) if head + 1 < heads else None
                top = jnp.max(now, axis=0, keepdims=True)
                e_out.ref[at * heads + head, :size, :size] = jnp.exp(now - top).astype(BF16)
                if head:
                    mix(head - 1)
                now = later
            mix(heads - 1)
            if size < length:
                att_out.ref[size:] = jnp.zeros((length - size, width), BF16)

        place = places(Z_BETWEEN)
        for at in range(2):
            x = rows.part(at)
            near = slice(at * length, (at + 1) * length)
            k_out.ref[near] = nn(x[near], wk.ref()[...]).astype(BF16)
            q_out.ref[near] = (
                (nn(x[near], wq.ref()[...]) + bq).astype(BF16).astype(F32) * HEAD**-0.5
            ).astype(BF16)
            value = (nn(x[near], wv.ref()[...]) + bv).astype(BF16)
            v_out.ref[near] = value
            v_turned[at] = value.T
            for start in range(at * length, (at + 1) * length, ROWS):
                put_turned(place, turned_out.ref, x[start : start + ROWS, :], start)
            by_length(lengths, at, length, lambda size: sequence(at, size))
            e_out.send(pl.ds(at * heads, heads))
            for out in (q_out, k_out, v_out, inv_out):
                out.send(pl.ds(at * length, length))
            (own_out, other_out)[at].send()

    both = 2 * length
    return call(
        body,
        "attend",
        lengths,
        [BothRows(tokens, length), w_key, w_query, w_value, bias_query, bias_value],
        [
            shape((both, width)),
            shape((both, width)),
            shape((both, width)),
            shape((2 * heads, length, length)),
            shape((length, width)),
            shape((length, width)),
            shape((both, width), F32),
            shape((GROUPS, model // GROUPS, both)),
        ],
        scratch=[pltpu.VMEM((2, width, length), BF16)],
    )


def up_half(low, wu, bu, wd, act, slope_out, total, fresh):
    inner = slope_out.ref.shape[1]

    def project(start):
        weights = wu.columns(start, start + HIDDEN)
        return nn(low[...], weights[:, start : start + HIDDEN]) + bu[:, start : start + HIDDEN]

    now = project(0)
    for start in range(0, inner, HIDDEN):
        cut = slice(start, start + HIDDEN)
        later = project(start + HIDDEN) if start + HIDDEN < inner else None
        phi = 0.5 * (1.0 + lax.erf(now * (0.5**0.5)))
        act[:, cut] = (now * phi).astype(BF16)
        slope_out.ref[:, cut] = (
            phi + now * (jnp.exp(-0.5 * now * now) * 0.3989422804014327)
        ).astype(BF16)
        slope_out.send(slice(None), pl.ds(start, HIDDEN))
        part = nn(act[:, cut], wd.columns(start, start + HIDDEN)[cut, :])
        if fresh and start == 0:
            total[...] = part
        else:
            total[...] += part
        now = later


def middle(lengths, tokens, out_grad, att, w_out, vectors, bias_up, w_up, w_down, length):
    model = tokens.shape[1]
    inner = w_up[0].shape[1]
    size = model // GROUPS

    def body(lengths, loads, stores, scratch):
        att_a, wo_a, att_b, wo_b, rows, bo, g1, s1 = loads[:8]
        wu_a, bu_a, wd_a, wu_b, bu_b, wd_b, cot, bd, g2, s2 = loads[8:]
        normed_out, spread_out, turned_out, layer_out, grad_low = stores[:5]
        slope_a, slope_b, small_out, down_out, own_out = stores[5:]
        total, hidden, low, act_a, act_b, grad_turned = scratch[:6]
        total[...] = nn(att_a.ref()[...], wo_a.ref()[...]) + nn(att_b.ref()[...], wo_b.ref()[...])
        x = rows.ref()
        bo, g1, s1 = line(bo), line(g1), line(s1)
        place = places(PLANE_FIRST)
        for start in range(0, length, ROWS):
            cut = slice(start, start + ROWS)
            value = x[cut].astype(F32) + (total[cut] + bo)
            centred = value - mean(value)
            spread = lax.rsqrt(mean(centred * centred) + EPS)
            normed = centred * spread
            normed_out.ref[cut] = normed.astype(BF16)
            spread_out.ref[cut] = jnp.broadcast_to(spread, (ROWS, 128))
            full = normed * g1 + s1
            hidden[cut] = full
            full = full.astype(BF16)
            low[cut] = full
            put_turned(place, turned_out.ref, full, start)
        for out in (normed_out, spread_out, turned_out):
            out.send()
        up_half(low, wu_a, line(bu_a), wd_a, act_a, slope_a, total, True)
        up_half(low, wu_b, line(bu_b), wd_b, act_b, slope_b, total, False)
        cot = cot.ref()
        bd, g2, s2 = line(bd), line(g2), line(s2)
        place = places(Z_BETWEEN)
        sums = [jnp.zeros((1, model), F32)] * 3
        for start in range(0, length, ROWS):
            cut = slice(start, start + ROWS)
            row = lax.broadcasted_iota(jnp.int32, (ROWS, model), 0) + start
            valid = jnp.where(row < length_of(lengths, 0), 1.0, 0.0)
            value = hidden[cut] + total[cut] + bd
            centred = value - mean(value)
            spread = lax.rsqrt(mean(centred * centred) + EPS)
            normed = centred * spread
            layer_out.ref[cut] = ((normed * g2 + s2) * valid).astype(BF16)
            grad = cot[cut].astype(F32) * valid
            scaled = grad * g2
            resid = spread * (scaled - mean(scaled) - normed * mean(scaled * normed))
            sums = [
                sums[0] + column_sum(grad * normed),
                sums[1] + column_sum(grad),
                sums[2] + column_sum(resid),
            ]
            resid = resid.astype(BF16)
            grad_low.ref[cut] = resid
            put_turned(place, grad_turned, resid, start)
        for at in range(3):
            small_out.ref[at : at + 1] = sums[at]
        small_out.ref[3:8] = jnp.zeros((5, model), F32)
        for out in (grad_low, layer_out, small_out):
            out.send()
        weight(down_out, grad_turned, act_b, Z_BETWEEN)
        weight(own_out, grad_turned, act_a, None)

    return call(
        body,
        "middle",
        lengths,
        [att[0], w_out[0], att[1], w_out[1], OwnRows(tokens, length), *vectors[:3]]
        + [Whole(w_up[0], 3, 1), bias_up[0], Whole(w_down[0], 3, 0)]
        + [Whole(w_up[1], late=True), Whole(bias_up[1], late=True), Whole(w_down[1], late=True)]
        + [OwnRows(out_grad, length, late=True)]
        + [Whole(item, late=True) for item in vectors[3:]],
        [
            shape((length, model)),
            shape((length, 128), F32),
            shape((GROUPS, size, length)),
            shape((length, model)),
            shape((length, model)),
            shape((length, inner)),
            shape((length, inner)),
            shape((8, model), F32),
            shape((model, inner)),
            shape((model, inner)),
        ],
        scratch=[
            pltpu.VMEM((length, model), F32),
            pltpu.VMEM((length, model), F32),
            pltpu.VMEM((length, model), BF16),
            pltpu.VMEM((length, inner), BF16),
            pltpu.VMEM((length, inner), BF16),
            pltpu.VMEM((GROUPS, size, length), BF16),
        ],
    )


SWAP = [True]


def matrix(turned):
    groups, size, length = turned.shape
    return turned.reshape(groups * size, length)


def weight(out, turned, right, order):
    left = matrix(turned[...])
    size = left.shape[0] // GROUPS
    columns = right.shape[1]
    for start in range(0, columns, HIDDEN):
        cut = slice(start, start + HIDDEN)
        product = nn(left, right[:, cut]).astype(BF16)
        if order is None:
            out.ref[:, cut] = product
        else:
            for group in range(GROUPS):
                to = partner_place(group, order) * size
                out.ref[to : to + size, cut] = product[group * size : (group + 1) * size]
        out.send(slice(None), pl.ds(start, HIDDEN))


def slope_back(grad, wd, slopes, ups, bias):
    inner = ups.shape[1]

    def project(start):
        return nt(grad[...], wd.columns(start, start + HIDDEN)[start : start + HIDDEN, :])

    now = project(0)
    for start in range(0, inner, HIDDEN):
        cut = slice(start, start + HIDDEN)
        later = project(start + HIDDEN) if start + HIDDEN < inner else None
        value = (now * slopes.columns(start, start + HIDDEN)[:, cut].astype(F32)).astype(BF16)
        ups[:, cut] = value
        bias[:, cut] = jnp.broadcast_to(column_sum(value.astype(F32)), (8, HIDDEN))
        now = later


def up_back(lengths, grad_low, w_down, slope, turned, w_up, length):
    model, inner = w_up.shape
    size = model // GROUPS

    def body(lengths, loads, stores, scratch):
        grad, wd, slopes, left, wu = loads
        out, back, bias = stores
        ups = scratch[0]
        slope_back(grad.ref(), wd, slopes, ups, bias.ref)
        weight(out, left.ref(), ups, PLANE_FIRST)
        back.ref[...] = nt(ups[...], wu.ref()[...]).astype(BF16)

    return call(
        body,
        "up_back",
        lengths,
        [grad_low, Whole(w_down, 3, 0), Whole(slope, 3, 1), turned, Whole(w_up, late=True)],
        [shape((model, inner)), shape((length, model)), shape((8, inner), F32)],
        scratch=[pltpu.VMEM((length, inner), BF16)],
    )


def up_own(
    lengths, grad_low, w_down, slope, w_up, back, normed, spread, gain, turned, smalls, length, after
):
    model, inner = w_up.shape
    size = model // GROUPS

    def body(lengths, loads, stores, scratch):
        grad, wd, slopes, left, wu, share, norm, spr, vec = loads[:9]
        grad_resid = grad
        small_two, bias_b = loads[9:]
        low_out, first_out, turned_out, packed, out = stores
        total, ups, bias = scratch[:3]
        slope_back(grad.ref(), wd, slopes, ups, bias)
        weight(out, left.ref(), ups, None)
        total[...] = nt(ups[...], wu.ref()[...])
        gain = line(vec)
        place = places(Z_BETWEEN)
        sums = [jnp.zeros((1, model), F32)] * 3
        grad_resid, share, norm, spr = (item.ref() for item in (grad_resid, share, norm, spr))
        for start in range(0, length, ROWS):
            cut = slice(start, start + ROWS)
            value = grad_resid[cut].astype(F32) + (total[cut] + share[cut].astype(F32))
            normed = norm[cut].astype(F32)
            scaled = value * gain
            first = spr[cut, 0:1] * (scaled - mean(scaled) - normed * mean(scaled * normed))
            sums = [
                sums[0] + column_sum(value * normed),
                sums[1] + column_sum(value),
                sums[2] + column_sum(first),
            ]
            first_out.ref[cut] = first
            first = first.astype(BF16)
            low_out.ref[cut] = first
            put_turned(place, turned_out.ref, first, start)
        lines = [small_two.ref()[at : at + 1] for at in range(3)] + sums
        pack(packed.ref, [*lines, bias_b.ref()[0:1], bias[0:1]])

    return call(
        body,
        "up_own",
        lengths,
        [grad_low, Whole(w_down, 3, 0), Whole(slope, 3, 1), turned]
        + [Whole(item, late=True) for item in (w_up, back, normed, spread, gain, *smalls)],
        [
            shape((length, model)),
            shape((length, model), F32),
            shape((GROUPS, size, length)),
            shape(((6 * model + 2 * inner) // 128, 128), F32),
            shape((model, inner)),
        ],
        scratch=[
            pltpu.VMEM((length, model), F32),
            pltpu.VMEM((length, inner), BF16),
            pltpu.VMEM((8, inner), F32),
        ],
        after=after,
    )


def pack(target, lines):
    at = 0
    for values in lines:
        for start in range(0, values.shape[1], 128):
            target[at : at + 1] = values[:, start : start + 128]
            at += 1


def attend_back(
    lengths, low, first_turned, token_turned, w_out, saved, smalls, joins, length, after=()
):
    query, keyed, valued, expo, att_own, att_other, inv = saved
    width, model = w_out.shape
    heads = width // HEAD
    both = 2 * length

    def body(lengths, loads, stores, scratch):
        grad_a, wo, k, v, inverse, att_a, e, q, grad_b, att_b = loads[:10]
        token_t, first_t, small, small_came = loads[10:]
        dq, dk, dv, packed, *halves = stores
        mixed, k_turned, kept, turned, attended = scratch[:5]
        wo = wo.ref()
        atts = (att_a, att_b)

        def lanes(head):
            return slice(head // 2 * PAIR, (head // 2 + 1) * PAIR)

        def sequence(at, size):
            near = slice(at * length, at * length + size)
            lane = lax.broadcasted_iota(jnp.int32, (size, PAIR), 1)
            marker = jnp.where(lane < 2, 1.0, 0.0).astype(BF16)
            scaled_of, product_of = {}, {}

            def scores(head):
                cut, mine = lanes(head), lane // HEAD == head % 2
                if head % 2 == 0:
                    scaled = mixed[:size, cut].astype(F32) * inverse.target[near, cut]
                    product_of[head // 2] = scaled * atts[at].target[:size, cut].astype(F32)
                    scaled_of[head // 2] = scaled.astype(BF16)
                scaled, product = scaled_of[head // 2], product_of[head // 2]
                inner = -jnp.sum(jnp.where(mine, product, 0.0), axis=1, keepdims=True)
                high = inner.astype(BF16).astype(F32)
                extra = jnp.where(lane == 0, high, jnp.where(lane == 1, inner - high, 0.0))
                right = jnp.concatenate(
                    [jnp.where(mine, scaled, jnp.zeros_like(scaled)), extra.astype(BF16)], axis=1
                )
                return nt(jnp.concatenate([v.target[near, cut], marker], axis=1), right)

            dvs, dks, dqs = [], [], []

            def products(head):
                cut = lanes(head)
                grads = kept[head % 2, :size, :size]
                dks.append(nn(grads, q.target[near, cut]))
                dqs.append(nn(k_turned[head * HEAD : (head + 1) * HEAD, :size], grads))
                if head % 2:
                    dk.ref[near, cut] = jnp.where(lane < HEAD, dks[0], dks[1]).astype(BF16)
                    dq.ref[near, cut] = (jnp.concatenate(dqs, axis=0) * HEAD**-0.5).astype(BF16).T
                    dks.clear()
                    dqs.clear()

            now = scores(0)
            for head in range(heads):
                later = scores(head + 1) if head + 1 < heads else None
                expo = e.target[at * heads + head, :size, :size]
                kept[head % 2, :size, :size] = (expo.astype(F32) * now).astype(BF16)
                dvs.append(nn(expo, scaled_of[head // 2]))
                if head % 2:
                    dv.ref[near, lanes(head)] = jnp.where(lane < HEAD, dvs[0], dvs[1]).astype(BF16)
                    dvs.clear()
                if head:
                    products(head - 1)
                now = later
            products(heads - 1)
            if size < length:
                rest = slice(at * length + size, (at + 1) * length)
                for out in (dq, dk, dv):
                    out.ref[rest] = jnp.zeros((length - size, width), BF16)

        place = places(Z_BETWEEN)
        for at, grad in enumerate((grad_a, grad_b)):
            near = slice(at * length, (at + 1) * length)
            rows = grad.ref()
            mixed[...] = nt(rows[...], wo[...]).astype(BF16)
            if at:
                for start in range(0, length, ROWS):
                    put_turned(place, turned, rows[start : start + ROWS, :], start)
            k_turned[...] = k.part(at)[near].T
            for load in (inverse, v, q, e):
                load.part(at)
            attended[near] = atts[at].ref()[...]
            by_length(lengths, at, length, lambda size: sequence(at, size))
            for out in (dq, dk, dv):
                out.send(pl.ds(at * length, length))
        wide = (6 * model) // 128
        high = wide + (small.target.shape[0] - wide) // 2
        packed.ref[:wide] = small.ref()[:wide] + small_came.ref()[:wide]
        packed.ref[wide:high] = small.ref()[high:] + small_came.ref()[wide:high]
        lines = [column_sum(out.ref[...].astype(F32)) for out in (dq, dv)]
        pack(packed.ref.at[pl.ds(high, 2 * width // 128)], lines)
        packed.send()
        if joins:
            scratch[-1]()
        def put(product, at, column, order):
            cut = slice(column, column + width)
            size = model // GROUPS
            for group in range(GROUPS):
                half, to = divmod(reordered(group, Z_BETWEEN, order), GROUPS // 2)
                halves[at + half].ref[to * size : (to + 1) * size, cut] = product[
                    group * size : (group + 1) * size
                ]
            for out in halves[at : at + 2]:
                out.send(slice(None), pl.ds(column, width))

        left = matrix(token_t.ref()[...])
        put(nn(left, dq.ref[...]).astype(BF16), 0, 0, Z_BETWEEN)
        put(nn(left, dk.ref[...]).astype(BF16), 0, width, Z_BETWEEN)
        put(nn(left, dv.ref[...]).astype(BF16), 2, 0, Z_FIRST)
        product = nn(matrix(first_t.ref()[...]), attended[:length])
        product = (product + nn(matrix(turned[...]), attended[length:])).astype(BF16)
        put(product, 2, width, Z_FIRST)

    some = shape((both, width))
    small_rows = smalls[0].shape[0] - (smalls[0].shape[0] - 6 * model // 128) // 2 + 2 * width // 128
    return call(
        body,
        "attend_back",
        lengths,
        [low[0], w_out, *(Whole(item, 2, 0) for item in (keyed, valued, inv)), att_own]
        + [Whole(expo, 2, 0), Whole(query, 2, 0)]
        + [Whole(item, late=True) for item in (low[1], att_other, token_turned, first_turned)]
        + [Whole(item, late=True) for item in smalls],
        [some, some, some, shape((small_rows, 128), F32)] + [shape((model // 2, 2 * width))] * 4,
        scratch=[
            pltpu.VMEM((length, width), BF16),
            pltpu.VMEM((width, length), BF16),
            pltpu.VMEM((2, length, length), BF16),
            pltpu.VMEM((GROUPS, model // GROUPS, length), BF16),
            pltpu.VMEM((both, width), BF16),
        ],
        after=after,
        joins=joins,
    )


def input_part(lengths, first, parts, weights, length, after=()):
    model = first.shape[1]

    def body(lengths, loads, stores, scratch):
        for at in (1, 0):
            near = slice(at * length, (at + 1) * length)
            total = nt(loads[1].ref()[near], loads[4].ref()[...])
            total += nt(loads[2].ref()[near], loads[5].ref()[...])
            total += nt(loads[3].ref()[near], loads[6].ref()[...])
            if at:
                stores[1].ref[...] = total.astype(BF16)
                stores[1].send()
            else:
                stores[0].ref[...] = loads[0].ref()[...] + total

    return call(
        body,
        "input_part",
        lengths,
        [first, *parts, *weights],
        [shape((length, model), F32), shape((length, model))],
        after=after,
    )


def swap(values):
    return lax.ppermute(values, "tp", [(0, 1), (1, 0)])


def together(*values):
    return lax.optimization_barrier(values)


def flip(values, bits):
    size = lax.axis_size("dp")
    perm = [(2 * d + c, 2 * (d ^ bits[c]) + c) for d in range(size) for c in range(2)]
    return lax.ppermute(values, ("dp", "tp"), perm)


NEAR, FAR, LOW, HIGH = (1, 2), (2, 1), (4, 4), (8, 8)


def total(parts):
    parts = [part.astype(F32) for part in parts]
    while len(parts) > 1:
        parts = [sum(parts[at : at + 2]) for at in range(0, len(parts), 2)]
    return parts[0]


def second_half(parts):
    rows = parts[0].shape[0] // 2
    return total([part[rows:] for part in parts]).astype(BF16)


def halve(parts, came):
    rows = parts[0].shape[0] // 2
    return [part[:rows] for part in parts] + [came]


def step(parts, bits):
    sent = second_half(parts)
    return halve(parts, flip(sent, bits)), sent


def small_step(values, came, mark, bits):
    values = values + together(came, mark)[0]
    return (values, flip(values, bits)), values


def scatter(whole):
    return lax.psum_scatter(whole, "dp", scatter_dimension=0, tiled=True)


def local(
    tokens,
    seq_lengths,
    out_grad,
    w_query,
    bias_query,
    w_key,
    w_value,
    bias_value,
    w_out,
    bias_out,
    gain_one,
    shift_one,
    w_up,
    bias_up,
    w_down,
    bias_down,
    gain_two,
    shift_two,
):
    near = lax.axis_size("dp") == GROUPS
    SWAP[0] = near
    lengths = seq_lengths
    model = tokens.shape[1]
    length = tokens.shape[0] // seq_lengths.shape[0]
    width = w_query.shape[1]
    inner = w_up.shape[1]

    wo_b, wu_b, wd_b, bu_b = swap(w_out), swap(w_up), swap(w_down), swap(bias_up)
    query, keyed, valued, expo, att_own, att_other, inv, token_turned = attend(
        lengths, tokens, w_query, w_key, w_value, bias_query, bias_value, length
    )
    (
        normed,
        spread,
        hidden_turned,
        layer_own,
        grad_low,
        slope,
        slope_b,
        small_two,
        down_b,
        down_a,
    ) = middle(
        lengths,
        tokens,
        out_grad,
        (att_own, swap(att_other)),
        (w_out, wo_b),
        (bias_out, gain_one, shift_one, bias_down, gain_two, shift_two),
        (bias_up, bu_b),
        (w_up, wu_b),
        (w_down, wd_b),
        length,
    )
    down_came = swap(down_b)
    layer_other = swap(layer_own)
    up_b, back_b, bias_up_b = up_back(lengths, grad_low, wd_b, slope_b, hidden_turned, wu_b, length)
    up_came = swap(up_b)
    down = [down_a, down_came]
    after = [back_b]
    if near:
        down_send = second_half(down)
        down = halve(down, flip(down_send, NEAR))
        after = [down_send]
    first_low, first, first_turned, small, up_a = up_own(
        lengths,
        grad_low,
        w_down,
        slope,
        w_up,
        back_b,
        normed,
        spread,
        gain_one,
        hidden_turned,
        (small_two, bias_up_b),
        length,
        after,
    )
    first_came = swap(first_low)
    small_came = swap(small)
    up = [up_a, up_came]
    after = []
    if near:
        up_send = second_half(up)
        up = halve(up, flip(up_send, NEAR))
        down_send = second_half(down)
        down = halve(down, flip(down_send, LOW))
        after = [up_send, down_send]
    dq, dk, dv, small, keep_p, send_p, keep_q, send_q, layer_output = attend_back(
        lengths,
        (first_low, first_came),
        first_turned,
        token_turned,
        w_out,
        (query, keyed, valued, expo, att_own, att_other, inv),
        (small, small_came),
        [(layer_own, layer_other)],
        length,
        after,
    )
    sizes = [model] * 6 + [inner, width, width]
    after = []
    if near:
        up[-1], down[-1], _ = together(up[-1], down[-1], keep_p)
        came_p, came_q = flip(send_p, NEAR), flip(send_q, LOW)
        up, up_send = step(up, FAR)
        down, down_send = step(down, FAR)
        small_came = flip(small, (1, 1))
        after = [up_send, down_send]
    input_sum, input_other = input_part(
        lengths, first, (dq, dk, dv), (w_query, w_key, w_value), length, after
    )
    input_other = swap(input_other)
    if near:
        down[-1] = together(down[-1], input_sum)[0]
        down, mark = step(down, HIGH)
        up[-1], came_p = together(up[-1], came_p, mark)[:2]
        heads_p, mark = step([keep_p, came_p], LOW)
        came_q = together(came_q, mark)[0]
        heads_q, mark = step([keep_q, came_q], NEAR)
        up, mark = step(up, LOW)
        small, mark = small_step(small, small_came, mark, (2, 2))
        heads_p[-1], heads_q[-1], up[-1], down[-1] = together(
            heads_p[-1], heads_q[-1], up[-1], down[-1], mark
        )[:4]
        heads_p, mark = step(heads_p, FAR)
        heads_q[-1] = together(heads_q[-1], mark)[0]
        heads_q, mark = step(heads_q, FAR)
        up, mark = step(up, HIGH)
        grad_down = total(down).T
        small, mark = small_step(*small, mark, LOW)
        input_other = together(input_other, mark)[0]
        heads_p[-1], heads_q[-1], up[-1] = together(heads_p[-1], heads_q[-1], up[-1], mark)[:3]
        heads_p, mark = step(heads_p, HIGH)
        heads_q[-1] = together(heads_q[-1], mark)[0]
        heads_q, mark = step(heads_q, HIGH)
        small, mark = small_step(*small, mark, HIGH)
        grad_up = total(up)
        small = small[0] + small[1]
        heads_p, heads_q = total(heads_p), total(heads_q)
    else:
        grad_down = scatter(total(down)).T
        grad_up = scatter(total(up))
        heads_p = scatter(jnp.concatenate([keep_p, send_p], axis=0).astype(F32))
        heads_q = scatter(jnp.concatenate([keep_q, send_q], axis=0).astype(F32))
        small = lax.psum(small, "dp")
    input_own = (input_sum + input_other.astype(F32)).astype(BF16)
    (input_grad,) = call(
        lambda *_: None, "join", lengths, [], [], joins=[(input_own, swap(input_own))]
    )
    grad_query, grad_key = heads_p[:, :width], heads_p[:, width:]
    grad_value, grad_out = heads_q[:, :width], heads_q[:, width:].T
    small = small.reshape(-1)
    smalls, at = [], 0
    for size in sizes:
        smalls.append(small[at : at + size])
        at += size
    gain_two_grad, shift_two_grad, bias_down_grad = smalls[:3]
    gain_one_grad, shift_one_grad, bias_out_grad = smalls[3:6]
    bias_up_grad, bias_query_grad, bias_value_grad = smalls[6:]
    return (
        layer_output,
        input_grad,
        grad_query,
        grad_key,
        grad_value,
        bias_query_grad,
        bias_value_grad,
        grad_out,
        bias_out_grad,
        gain_one_grad,
        shift_one_grad,
        grad_up,
        bias_up_grad,
        grad_down,
        bias_down_grad,
        gain_two_grad,
        shift_two_grad,
    )


def solution(mesh):
    return jax.shard_map(
        local,
        mesh=mesh,
        in_specs=(
            P("dp", None),
            P("dp"),
            P("dp", None),
            P(None, "tp"),
            P("tp"),
            P(None, "tp"),
            P(None, "tp"),
            P("tp"),
            P("tp", None),
            P(),
            P(),
            P(),
            P(None, "tp"),
            P("tp"),
            P("tp", None),
            P(),
            P(),
            P(),
        ),
        out_specs=(
            P("dp", None),
            P("dp", None),
            P("dp", "tp"),
            P("dp", "tp"),
            P("dp", "tp"),
            P("tp"),
            P("tp"),
            P("tp", "dp"),
            P(),
            P(),
            P(),
            P("dp", "tp"),
            P("tp"),
            P("tp", "dp"),
            P(),
            P(),
            P(),
        ),
        check_vma=False,
    )
```

```python
import jax
import jax.numpy as jnp
from jax import lax
from jax.experimental import pallas as pl
from jax.experimental.pallas import tpu as pltpu
from jax.sharding import PartitionSpec as P

HEAD = 64
PAIR = 128
EPS = 1e-05
GROUPS = 16
BF16 = jnp.bfloat16
F32 = jnp.float32
ROWS = 128
HIDDEN = 512


def nn(left, right):
    return lax.dot_general(left, right, (((1,), (0,)), ((), ())), preferred_element_type=F32)


def nt(left, right):
    return lax.dot_general(left, right, (((1,), (1,)), ((), ())), preferred_element_type=F32)


def mean(values):
    return jnp.mean(values, axis=-1, keepdims=True)


def column_sum(values):
    return jnp.sum(values, axis=0, keepdims=True)


class Load:
    def __init__(self, source, target, sems, first, item):
        self.target, self.item = target, item
        self.source, self.sems, self.first = source, sems, first
        self.copies = []
        self.waited = set()
        if isinstance(item, Manual):
            return
        self.copies = [
            pltpu.make_async_copy(*item.ends(source, target, at), sems.at[first + at])
            for at in range(item.parts)
        ]

    def part(self, at):
        if at not in self.waited:
            self.copies[at].wait()
            self.waited.add(at)
        return self.target

    def columns(self, start, stop):
        if self.item.parts > 1:
            size = self.item.dims[self.item.axis] // self.item.parts
            for at in range(start // size, -(-stop // size)):
                self.part(at)
            return self.target
        return self.ref()

    def ref(self):
        for at in range(len(self.copies)):
            self.part(at)
        return self.target


class Store:
    def __init__(self, target, buffer, sems, first):
        self.target, self.ref, self.sems, self.next = target, buffer, sems, first
        self.copies = []
        self.manual = False

    def send(self, *index):
        source = self.ref.at[index] if index else self.ref
        target = self.target.at[index] if index else self.target
        copy = pltpu.make_async_copy(source, target, self.sems.at[self.next])
        copy.start()
        self.next += 1
        self.copies.append(copy)

    def finish(self):
        for copy in self.copies:
            copy.wait()


PARTS = 8


class Whole:
    def __init__(self, array, parts=1, axis=-1, late=False):
        self.array, self.dims = array, array.shape
        self.parts, self.axis, self.late = parts, axis % array.ndim, late

    def ends(self, source, target, at):
        if self.parts == 1:
            return source, target
        size = self.dims[self.axis] // self.parts
        cut = tuple(
            pl.ds(at * size, size) if axis == self.axis else pl.ds(0, dim)
            for axis, dim in enumerate(self.dims)
        )
        return source.at[cut], target.at[cut]


class Manual(Whole):
    pass


class OwnRows(Whole):
    def __init__(self, array, rows, late=False):
        super().__init__(array, late=late)
        self.dims = (rows,) + array.shape[1:]

    def ends(self, source, target, at):
        rows = self.dims[0]
        start = pl.multiple_of(lax.axis_index("tp") * rows, rows)
        return source.at[pl.ds(start, rows)], target


class Rows(Whole):
    def __init__(self, array, start, rows, parts=1, last=False):
        super().__init__(array, parts, 0)
        self.dims, self.start, self.last = (rows,) + array.shape[1:], start, last

    def ends(self, source, target, at):
        size = self.dims[0] // self.parts
        at = (self.parts - 1 - at if self.last else at) * size
        return source.at[pl.ds(self.start + at, size)], target.at[pl.ds(at, size)]


class BothRows(Whole):
    def __init__(self, array, rows):
        super().__init__(array, 2, 0)
        self.rows = rows

    def ends(self, source, target, at):
        core = lax.axis_index("tp")
        start = pl.multiple_of((core if at == 0 else 1 - core) * self.rows, self.rows)
        return source.at[pl.ds(start, self.rows)], target.at[pl.ds(at * self.rows, self.rows)]


def call(body, name, lengths, ins, outs, scratch=(), vmem=64, after=(), joins=(), early=None, cost=1):
    ins = [item if isinstance(item, Whole) else Whole(item) for item in ins]
    n_in, n_out, n_after, n_join = len(ins), len(outs), len(after), len(joins)
    joined = [shape((2 * own.shape[0],) + own.shape[1:], own.dtype) for own, _ in joins]

    def kernel(lengths_ref, *refs):
        in_refs, refs = refs[:n_in], refs[n_in + n_after :]
        pair_refs, refs = refs[: 2 * n_join], refs[2 * n_join :]
        out_refs, refs = refs[:n_out], refs[n_out:]
        join_refs, refs = refs[:n_join], refs[n_join:]
        in_bufs, refs = refs[:n_in], refs[n_in:]
        out_bufs, refs = refs[:n_out], refs[n_out:]
        join_bufs, refs = refs[:n_join], refs[n_join:]
        in_sems, out_sems, join_sems, refs = refs[0], refs[1], refs[2], refs[3:]
        core = lax.axis_index("tp")
        copies = []
        for at in range(n_join):
            for side in range(2):
                source = pair_refs[2 * at + side]
                rows = source.shape[0]
                start = pl.multiple_of((core if side == 0 else 1 - core) * rows, rows)
                copies.append(
                    pltpu.make_async_copy(
                        source, join_bufs[at].at[pl.ds(start, rows)], join_sems.at[2 * at + side]
                    )
                )
        loads, first = [], 0
        for item, source, buffer in zip(ins, in_refs, in_bufs):
            loads.append(Load(source, buffer, in_sems, first, item))
            first += item.parts
        for late in (False, True):
            if late and early is not None:
                early(lengths_ref, loads)
            for at in range(max(item.parts for item in ins) if ins else 0):
                for load in loads:
                    if load.item.late == late and at < len(load.copies):
                        load.copies[at].start()
        stores = [
            Store(out_refs[at], out_bufs[at], out_sems, at * PARTS) for at in range(n_out)
        ]
        for copy in copies:
            copy.start()
        started = []

        def join():
            for copy in copies:
                copy.wait()
            for at in range(n_join):
                started.append(
                    pltpu.make_async_copy(join_bufs[at], join_refs[at], join_sems.at[2 * at])
                )
                started[-1].start()
            copies.clear()

        body(lengths_ref, loads, stores, (*refs, join))
        if copies:
            join()
        for store in stores:
            if not store.copies and not store.manual:
                store.send()
        for load in loads:
            load.ref()
        for store in stores:
            store.finish()
        for copy in started:
            copy.wait()

    return pl.pallas_call(
        kernel,
        name=name,
        out_shape=[*outs, *joined],
        in_specs=[pl.BlockSpec(memory_space=pltpu.SMEM)]
        + [pl.BlockSpec(memory_space=pl.ANY)] * (n_in + n_after + 2 * n_join),
        out_specs=[pl.BlockSpec(memory_space=pl.ANY)] * (n_out + n_join),
        scratch_shapes=[pltpu.VMEM(item.dims, item.array.dtype) for item in ins]
        + [pltpu.VMEM(out.shape, out.dtype) for out in [*outs, *joined]]
        + [
            pltpu.SemaphoreType.DMA((sum(item.parts for item in ins) + 1,)),
            pltpu.SemaphoreType.DMA((max(n_out, 1) * PARTS,)),
            pltpu.SemaphoreType.DMA((max(2 * n_join, 1),)),
        ]
        + list(scratch),
        compiler_params=pltpu.CompilerParams(vmem_limit_bytes=vmem * 2**20),
        cost_estimate=pl.CostEstimate(flops=cost, bytes_accessed=1, transcendentals=0),
    )(lengths, *(item.array for item in ins), *after, *(item for pair in joins for item in pair))


def line(load):
    ref = load.ref()
    return ref[...].astype(F32).reshape(1, ref.shape[0])


def length_of(lengths, at):
    core = lax.axis_index("tp")
    return lengths[core if at == 0 else 1 - core]


def places(order):
    if not SWAP[0]:
        return list(range(GROUPS))
    place, core = lax.axis_index("dp"), lax.axis_index("tp")
    found = []
    for group in range(GROUPS):
        rel = jnp.bitwise_xor(place, group)
        bits = [rel % 2, (rel // 2) % 2, (rel // 4) % 2, rel // 8]
        near = jnp.where(core == 0, bits[0], bits[1])
        bits[:2] = near, bits[0] + bits[1] - near
        found.append(sum(bit * (8 // 2**step) for bit, step in zip(bits, order)))
    return found


PLANE_FIRST = (0, 1, 3, 2)
FAR_LAST = (0, 3, 1, 2)
Z_BETWEEN = (0, 2, 1, 3)


Z_FIRST = (1, 2, 0, 3)


def reordered(at, order, other):
    if not SWAP[0]:
        return at
    return sum((at >> (3 - step) & 1) << (3 - to) for step, to in zip(order, other))


def partner_place(at, order):
    if not SWAP[0]:
        return at
    near, far = 8 // 2 ** order[0], 8 // 2 ** order[1]
    left, right = bool(at & near), bool(at & far)
    return at if left == right else at ^ near ^ far


def by_length(lengths, at, length, run):
    count = length_of(lengths, at)
    sizes = [size for size in (128, 256) if size < length] + [length]
    below = None
    for size in sizes:
        fits = count <= size
        if below is not None:
            fits = fits & (count > below)

        @pl.when(fits)
        def _(size=size):
            run(size)

        below = size


def shape(dims, dtype=BF16):
    return jax.ShapeDtypeStruct(dims, dtype)


def put_turned(place, target, values, at):
    turned = values.T
    size = turned.shape[0] // GROUPS
    for group in range(GROUPS):
        target[place[group], :, at : at + values.shape[0]] = turned[
            group * size : (group + 1) * size
        ].astype(BF16)


def attend(lengths, tokens, w_query, w_key, w_value, bias_query, bias_value, length):
    width = w_query.shape[1]
    model = tokens.shape[1]
    heads = width // HEAD

    def body(lengths, loads, stores, scratch):
        rows, wk, wq, wv, bq, bv = loads
        q_out, k_out, v_out, e_out, own_out, other_out, inv_out, turned_out = stores
        (v_turned,) = scratch[:1]
        e_out.manual = True
        bq, bv = line(bq), line(bv)

        def lanes(head):
            return slice(head // 2 * PAIR, (head // 2 + 1) * PAIR)

        def sequence(at, size):
            near = slice(at * length, at * length + size)
            lane = lax.broadcasted_iota(jnp.int32, (size, PAIR), 1)
            row = lax.broadcasted_iota(jnp.int32, (size, PAIR), 0)
            count = length_of(lengths, at)
            masked = jnp.where((lane == 0) & (row >= count), -1e30, 0.0).astype(BF16)
            marker = jnp.where(lane == 0, 1.0, 0.0).astype(BF16)
            ones = jnp.ones((16, size), BF16)
            att_out = (own_out, other_out)[at]

            def scores(head):
                queries = q_out.ref[near, lanes(head)]
                own = jnp.where(lane // HEAD == head % 2, queries, jnp.zeros_like(queries))
                keys = jnp.concatenate([k_out.ref[near, lanes(head)], masked], axis=1)
                return nt(keys, jnp.concatenate([own, marker], axis=1))

            mixed, inverse = [], []

            def mix(head):
                values = v_turned[at, head * HEAD : (head + 1) * HEAD, :size]
                left = jnp.concatenate([values, ones], axis=0)
                sums = nn(left, e_out.ref[at * heads + head, :size, :size])
                inv = 1.0 / sums[HEAD : HEAD + 1]
                mixed.append(sums[:HEAD] * inv)
                inverse.append(jnp.broadcast_to(inv, (HEAD, size)))
                if head % 2:
                    att_out.ref[:size, lanes(head)] = (
                        jnp.concatenate(mixed, axis=0).astype(BF16).T
                    )
                    inv_out.ref[near, lanes(head)] = jnp.concatenate(inverse, axis=0).T
                    mixed.clear()
                    inverse.clear()

            now = scores(0)
            for head in range(heads):
                later = scores(head + 1) if head + 1 < heads else None
                top = jnp.max(now, axis=0, keepdims=True)
                e_out.ref[at * heads + head, :size, :size] = jnp.exp(now - top).astype(BF16)
                if head:
                    mix(head - 1)
                now = later
            mix(heads - 1)
            if size < length:
                att_out.ref[size:] = jnp.zeros((length - size, width), BF16)
            square(at, size).start()

        def square(at, size):
            cut = (pl.ds(at * heads, heads), pl.ds(0, size), pl.ds(0, size))
            return pltpu.make_async_copy(
                e_out.ref.at[cut], e_out.target.at[cut], e_out.sems.at[e_out.next + at]
            )

        place = places(Z_BETWEEN)
        for at in range(2):
            x = rows.part(at)
            near = slice(at * length, (at + 1) * length)
            k_out.ref[near] = nn(x[near], wk.ref()[...]).astype(BF16)
            q_out.ref[near] = (
                (nn(x[near], wq.ref()[...]) + bq).astype(BF16).astype(F32) * HEAD**-0.5
            ).astype(BF16)
            value = (nn(x[near], wv.ref()[...]) + bv).astype(BF16)
            v_out.ref[near] = value
            v_turned[at] = value.T
            for start in range(at * length, (at + 1) * length, ROWS):
                put_turned(place, turned_out.ref, x[start : start + ROWS, :], start)
            by_length(lengths, at, length, lambda size: sequence(at, size))
            for out in (q_out, k_out, v_out, inv_out):
                out.send(pl.ds(at * length, length))
            (own_out, other_out)[at].send()
        for at in range(2):
            by_length(lengths, at, length, lambda size: square(at, size).wait())

    both = 2 * length
    return call(
        body,
        "attend",
        lengths,
        [BothRows(tokens, length), w_key, w_query, w_value, bias_query, bias_value],
        [
            shape((both, width)),
            shape((both, width)),
            shape((both, width)),
            shape((2 * heads, length, length)),
            shape((length, width)),
            shape((length, width)),
            shape((both, width), F32),
            shape((GROUPS, model // GROUPS, both)),
        ],
        scratch=[pltpu.VMEM((2, width, length), BF16)],
    )


def up_half(low, wu, bu, wd, act, slope_out, total, fresh):
    inner = slope_out.ref.shape[1]

    def project(start):
        weights = wu.columns(start, start + HIDDEN)
        return nn(low[...], weights[:, start : start + HIDDEN]) + bu[:, start : start + HIDDEN]

    now = project(0)
    for start in range(0, inner, HIDDEN):
        cut = slice(start, start + HIDDEN)
        later = project(start + HIDDEN) if start + HIDDEN < inner else None
        phi = 0.5 * (1.0 + lax.erf(now * (0.5**0.5)))
        act[:, cut] = (now * phi).astype(BF16)
        slope_out.ref[:, cut] = (
            phi + now * (jnp.exp(-0.5 * now * now) * 0.3989422804014327)
        ).astype(BF16)
        slope_out.send(slice(None), pl.ds(start, HIDDEN))
        part = nn(act[:, cut], wd.columns(start, start + HIDDEN)[cut, :])
        if fresh and start == 0:
            total[...] = part
        else:
            total[...] += part
        now = later


def middle(lengths, tokens, out_grad, att, w_out, vectors, bias_up, w_up, w_down, length):
    model = tokens.shape[1]
    inner = w_up[0].shape[1]
    size = model // GROUPS

    def body(lengths, loads, stores, scratch):
        att_a, wo_a, att_b, wo_b, rows, bo, g1, s1 = loads[:8]
        wu_a, bu_a, wd_a, wu_b, bu_b, wd_b, cot, bd, g2, s2 = loads[8:]
        normed_out, spread_out, turned_out, layer_out, grad_low = stores[:5]
        slope_a, slope_b, small_out, down_out, own_out = stores[5:]
        total, hidden, low, act_a, act_b, grad_turned = scratch[:6]
        total[...] = nn(att_a.ref()[...], wo_a.ref()[...]) + nn(att_b.ref()[...], wo_b.ref()[...])
        x = rows.ref()
        bo, g1, s1 = line(bo), line(g1), line(s1)
        place = places(PLANE_FIRST)
        for start in range(0, length, ROWS):
            cut = slice(start, start + ROWS)
            value = x[cut].astype(F32) + (total[cut] + bo)
            centred = value - mean(value)
            spread = lax.rsqrt(mean(centred * centred) + EPS)
            normed = centred * spread
            normed_out.ref[cut] = normed.astype(BF16)
            spread_out.ref[cut] = jnp.broadcast_to(spread, (ROWS, 128))
            full = normed * g1 + s1
            hidden[cut] = full
            full = full.astype(BF16)
            low[cut] = full
            put_turned(place, turned_out.ref, full, start)
        for out in (normed_out, spread_out, turned_out):
            out.send()
        up_half(low, wu_a, line(bu_a), wd_a, act_a, slope_a, total, True)
        up_half(low, wu_b, line(bu_b), wd_b, act_b, slope_b, total, False)
        cot = cot.ref()
        bd, g2, s2 = line(bd), line(g2), line(s2)
        place = places(FAR_LAST)
        sums = [jnp.zeros((1, model), F32)] * 3
        for start in range(0, length, ROWS):
            cut = slice(start, start + ROWS)
            row = lax.broadcasted_iota(jnp.int32, (ROWS, model), 0) + start
            valid = jnp.where(row < length_of(lengths, 0), 1.0, 0.0)
            value = hidden[cut] + total[cut] + bd
            centred = value - mean(value)
            spread = lax.rsqrt(mean(centred * centred) + EPS)
            normed = centred * spread
            layer_out.ref[cut] = ((normed * g2 + s2) * valid).astype(BF16)
            grad = cot[cut].astype(F32) * valid
            scaled = grad * g2
            resid = spread * (scaled - mean(scaled) - normed * mean(scaled * normed))
            sums = [
                sums[0] + column_sum(grad * normed),
                sums[1] + column_sum(grad),
                sums[2] + column_sum(resid),
            ]
            resid = resid.astype(BF16)
            grad_low.ref[cut] = resid
            put_turned(place, grad_turned, resid, start)
        for at in range(3):
            small_out.ref[at : at + 1] = sums[at]
        small_out.ref[3:8] = jnp.zeros((5, model), F32)
        for out in (grad_low, layer_out, small_out):
            out.send()
        weight(down_out, grad_turned, act_b, FAR_LAST)
        weight(own_out, grad_turned, act_a, None)

    return call(
        body,
        "middle",
        lengths,
        [att[0], w_out[0], att[1], w_out[1], OwnRows(tokens, length), *vectors[:3]]
        + [Whole(w_up[0], 3, 1), bias_up[0], Whole(w_down[0], 3, 0)]
        + [Whole(w_up[1], late=True), Whole(bias_up[1], late=True), Whole(w_down[1], late=True)]
        + [OwnRows(out_grad, length, late=True)]
        + [Whole(item, late=True) for item in vectors[3:]],
        [
            shape((length, model)),
            shape((length, 128), F32),
            shape((GROUPS, size, length)),
            shape((length, model)),
            shape((length, model)),
            shape((length, inner)),
            shape((length, inner)),
            shape((8, model), F32),
            shape((model, inner)),
            shape((model, inner)),
        ],
        scratch=[
            pltpu.VMEM((length, model), F32),
            pltpu.VMEM((length, model), F32),
            pltpu.VMEM((length, model), BF16),
            pltpu.VMEM((length, inner), BF16),
            pltpu.VMEM((length, inner), BF16),
            pltpu.VMEM((GROUPS, size, length), BF16),
        ],
    )


SWAP = [True]


def matrix(turned):
    groups, size, length = turned.shape
    return turned.reshape(groups * size, length)


def weight(out, turned, right, order):
    left = matrix(turned[...])
    size = left.shape[0] // GROUPS
    columns = right.shape[1]
    for start in range(0, columns, HIDDEN):
        cut = slice(start, start + HIDDEN)
        product = nn(left, right[:, cut]).astype(BF16)
        if order is None:
            out.ref[:, cut] = product
        else:
            for group in range(GROUPS):
                to = partner_place(group, order) * size
                out.ref[to : to + size, cut] = product[group * size : (group + 1) * size]
        out.send(slice(None), pl.ds(start, HIDDEN))


def slope_back(grad, wd, slopes, ups, bias):
    inner = ups.shape[1]

    def project(start):
        return nt(grad[...], wd.columns(start, start + HIDDEN)[start : start + HIDDEN, :])

    now = project(0)
    for start in range(0, inner, HIDDEN):
        cut = slice(start, start + HIDDEN)
        later = project(start + HIDDEN) if start + HIDDEN < inner else None
        value = (now * slopes.columns(start, start + HIDDEN)[:, cut].astype(F32)).astype(BF16)
        ups[:, cut] = value
        bias[:, cut] = jnp.broadcast_to(column_sum(value.astype(F32)), (8, HIDDEN))
        now = later


def up_back(lengths, grad_low, w_down, slope, turned, w_up, length):
    model, inner = w_up.shape
    size = model // GROUPS

    def body(lengths, loads, stores, scratch):
        grad, wd, slopes, left, wu = loads
        out, back, bias = stores
        ups = scratch[0]
        slope_back(grad.ref(), wd, slopes, ups, bias.ref)
        weight(out, left.ref(), ups, PLANE_FIRST)
        back.ref[...] = nt(ups[...], wu.ref()[...]).astype(BF16)

    return call(
        body,
        "up_back",
        lengths,
        [grad_low, Whole(w_down, 3, 0), Whole(slope, 3, 1), turned, Whole(w_up, late=True)],
        [shape((model, inner)), shape((length, model)), shape((8, inner), F32)],
        scratch=[pltpu.VMEM((length, inner), BF16)],
    )


def up_own(
    lengths, grad_low, w_down, slope, w_up, back, normed, spread, gain, turned, smalls, length, after
):
    model, inner = w_up.shape
    size = model // GROUPS

    def body(lengths, loads, stores, scratch):
        grad, wd, slopes, left, wu, share, norm, spr, vec = loads[:9]
        grad_resid = grad
        small_two, bias_b = loads[9:]
        low_out, turned_out, packed, out = stores
        total, ups, bias = scratch[:3]
        slope_back(grad.ref(), wd, slopes, ups, bias)
        weight(out, left.ref(), ups, None)
        total[...] = nt(ups[...], wu.ref()[...])
        gain = line(vec)
        place = places(Z_BETWEEN)
        sums = [jnp.zeros((1, model), F32)] * 3
        grad_resid, share, norm, spr = (item.ref() for item in (grad_resid, share, norm, spr))
        for start in range(0, length, ROWS):
            cut = slice(start, start + ROWS)
            value = grad_resid[cut].astype(F32) + (total[cut] + share[cut].astype(F32))
            normed = norm[cut].astype(F32)
            scaled = value * gain
            first = spr[cut, 0:1] * (scaled - mean(scaled) - normed * mean(scaled * normed))
            sums = [
                sums[0] + column_sum(value * normed),
                sums[1] + column_sum(value),
                sums[2] + column_sum(first),
            ]
            first = first.astype(BF16)
            low_out.ref[cut] = first
            put_turned(place, turned_out.ref, first, start)
        lines = [small_two.ref()[at : at + 1] for at in range(3)] + sums
        for at in range(3):
            packed.ref[at : at + 1, :model] = lines[2 * at]
            packed.ref[at : at + 1, model:] = lines[2 * at + 1]
        packed.ref[3:4] = bias[0:1]
        packed.ref[4:5] = bias_b.ref()[0:1]
        packed.ref[5:8] = jnp.zeros((3, inner), F32)

    return call(
        body,
        "up_own",
        lengths,
        [grad_low, Whole(w_down, 3, 0), Whole(slope, 3, 1), turned]
        + [Whole(item, late=True) for item in (w_up, back, normed, spread, gain, *smalls)],
        [
            shape((length, model)),
            shape((GROUPS, size, length)),
            shape((8, inner), F32),
            shape((model, inner)),
        ],
        scratch=[
            pltpu.VMEM((length, model), F32),
            pltpu.VMEM((length, inner), BF16),
            pltpu.VMEM((8, inner), F32),
        ],
        after=after,
    )


def attend_back(
    lengths, low, first_turned, token_turned, w_out, saved, joins, length, after=()
):
    query, keyed, valued, expo, att_own, att_other, inv = saved
    width, model = w_out.shape
    heads = width // HEAD
    both = 2 * length

    def square(e, at, size):
        cut = (pl.ds(at * heads, heads), pl.ds(0, size), pl.ds(0, size))
        return pltpu.make_async_copy(e.source.at[cut], e.target.at[cut], e.sems.at[e.first + at])

    def early(lengths, loads):
        for at in range(2):
            by_length(lengths, at, length, lambda size: square(loads[6], at, size).start())

    def body(lengths, loads, stores, scratch):
        grad_a, wo, k, v, inverse, att_a, e, q, grad_b, att_b = loads[:10]
        token_t, first_t = loads[10:]
        grads, small, *halves = stores
        dq, dk, dv = (grads.ref.at[:, pl.ds(at * width, width)] for at in range(3))
        mixed, k_turned, kept, turned, attended = scratch[:5]
        wo = wo.ref()
        atts = (att_a, att_b)

        def lanes(head):
            return slice(head // 2 * PAIR, (head // 2 + 1) * PAIR)

        def sequence(at, size):
            near = slice(at * length, at * length + size)
            lane = lax.broadcasted_iota(jnp.int32, (size, PAIR), 1)
            marker = jnp.where(lane < 2, 1.0, 0.0).astype(BF16)
            scaled_of, product_of = {}, {}

            def scores(head):
                cut, mine = lanes(head), lane // HEAD == head % 2
                if head % 2 == 0:
                    scaled = mixed[:size, cut].astype(F32) * inverse.target[near, cut]
                    product_of[head // 2] = scaled * atts[at].target[:size, cut].astype(F32)
                    scaled_of[head // 2] = scaled.astype(BF16)
                scaled, product = scaled_of[head // 2], product_of[head // 2]
                inner = -jnp.sum(jnp.where(mine, product, 0.0), axis=1, keepdims=True)
                high = inner.astype(BF16).astype(F32)
                extra = jnp.where(lane == 0, high, jnp.where(lane == 1, inner - high, 0.0))
                right = jnp.concatenate(
                    [jnp.where(mine, scaled, jnp.zeros_like(scaled)), extra.astype(BF16)], axis=1
                )
                return nt(jnp.concatenate([v.target[near, cut], marker], axis=1), right)

            dvs, dks, dqs = [], [], []

            def products(head):
                cut = lanes(head)
                grads = kept[head % 2, :size, :size]
                dks.append(nn(grads, q.target[near, cut]))
                dqs.append(nn(k_turned[head * HEAD : (head + 1) * HEAD, :size], grads))
                if head % 2:
                    dk[near, cut] = jnp.where(lane < HEAD, dks[0], dks[1]).astype(BF16)
                    dq[near, cut] = (jnp.concatenate(dqs, axis=0) * HEAD**-0.5).astype(BF16).T
                    dks.clear()
                    dqs.clear()

            square(e, at, size).wait()
            now = scores(0)
            for head in range(heads):
                later = scores(head + 1) if head + 1 < heads else None
                expo = e.target[at * heads + head, :size, :size]
                kept[head % 2, :size, :size] = (expo.astype(F32) * now).astype(BF16)
                dvs.append(nn(expo, scaled_of[head // 2]))
                if head % 2:
                    dv[near, lanes(head)] = jnp.where(lane < HEAD, dvs[0], dvs[1]).astype(BF16)
                    dvs.clear()
                if head:
                    products(head - 1)
                now = later
            products(heads - 1)
            if size < length:
                rest = slice(at * length + size, (at + 1) * length)
                grads.ref[rest] = jnp.zeros((length - size, 3 * width), BF16)

        place = places(Z_BETWEEN)
        for at, grad in enumerate((grad_a, grad_b)):
            near = slice(at * length, (at + 1) * length)
            rows = grad.ref()
            mixed[...] = nt(rows[...], wo[...]).astype(BF16)
            if at:
                for start in range(0, length, ROWS):
                    put_turned(place, turned, rows[start : start + ROWS, :], start)
            k_turned[...] = k.part(at)[near].T
            for load in (inverse, v, q):
                load.part(at)
            attended[near] = atts[at].ref()[...]
            by_length(lengths, at, length, lambda size: sequence(at, size))
            grads.send(pl.ds(at * length, length))
        sums = [column_sum(out[...].astype(F32)) for out in (dq, dv)]
        sums = jnp.concatenate(sums, axis=1)
        high = sums.astype(BF16).astype(F32)
        low = (sums - high).astype(BF16).astype(F32)
        first = lax.broadcasted_iota(jnp.int32, (8, 2 * width), 0) == 0
        small.ref[...] = jnp.where(first, high + low, 0.0)
        small.send()
        rest = halves[1].ref.at[pl.ds(model // 2, 16)]
        rest[...] = jnp.concatenate(
            [jnp.where(first, high, 0.0), jnp.where(first, low, 0.0)], axis=0
        ).astype(BF16)
        if joins:
            scratch[-1]()
        def put(product, at, column, order):
            cut = slice(column, column + width)
            size = model // GROUPS
            for group in range(GROUPS):
                half, to = divmod(reordered(group, Z_BETWEEN, order), GROUPS // 2)
                halves[at + half].ref[to * size : (to + 1) * size, cut] = product[
                    group * size : (group + 1) * size
                ]
            for out in halves[at : at + 2]:
                out.send(slice(None), pl.ds(column, width))

        left = matrix(token_t.ref()[...])
        put(nn(left, dq[...]).astype(BF16), 0, 0, Z_BETWEEN)
        put(nn(left, dk[...]).astype(BF16), 0, width, Z_BETWEEN)
        put(nn(left, dv[...]).astype(BF16), 2, 0, Z_FIRST)
        product = nn(matrix(first_t.ref()[...]), attended[:length])
        product = (product + nn(matrix(turned[...]), attended[length:])).astype(BF16)
        put(product, 2, width, Z_FIRST)

    half = shape((model // 2, 2 * width))
    return call(
        body,
        "attend_back",
        lengths,
        [low[0], w_out, *(Whole(item, 2, 0) for item in (keyed, valued, inv)), att_own]
        + [Manual(expo, 2, 0), Whole(query, 2, 0)]
        + [Whole(item, late=True) for item in (low[1], att_other, token_turned, first_turned)],
        [shape((both, 3 * width)), shape((8, 2 * width), F32), half, shape((model // 2 + 16, 2 * width))]
        + [half, half],
        scratch=[
            pltpu.VMEM((length, width), BF16),
            pltpu.VMEM((width, length), BF16),
            pltpu.VMEM((2, length, length), BF16),
            pltpu.VMEM((GROUPS, model // GROUPS, length), BF16),
            pltpu.VMEM((both, width), BF16),
        ],
        after=after,
        joins=joins,
        early=early,
    )


def input_part(lengths, first, grads, weights, length, after=()):
    model, width = weights[0].shape

    def body(lengths, loads, stores, scratch):
        side = scratch[0]
        copies = [
            pltpu.make_async_copy(
                load.source, side.at[:, pl.ds(at * width, width)], load.sems.at[load.first]
            )
            for at, load in enumerate(loads[1:4])
        ]
        for copy in copies:
            copy.start()
        for copy in copies:
            copy.wait()
        for at in (1, 0):
            near = slice(at * length, (at + 1) * length)
            total = nt(loads[0].part(at)[near], side[...])
            if not at:
                total += loads[4].ref()[...].astype(F32)
            stores[at].ref[...] = total.astype(BF16)
            stores[at].send()

    return call(
        body,
        "input_part",
        lengths,
        [Whole(grads, 2, 0), *(Manual(item) for item in weights), Whole(first, late=True)],
        [shape((length, model))] * 2,
        scratch=[pltpu.VMEM((model, 3 * width), BF16)],
        after=after,
    )


def swap(values):
    return lax.ppermute(values, "tp", [(0, 1), (1, 0)])


def together(*values):
    return lax.optimization_barrier(values)


def flip(values, bits):
    size = lax.axis_size("dp")
    perm = [(2 * d + c, 2 * (d ^ bits[c]) + c) for d in range(size) for c in range(2)]
    return lax.ppermute(values, ("dp", "tp"), perm)


NEAR, FAR, LOW, HIGH = (1, 2), (2, 1), (4, 4), (8, 8)


def add(left, right):
    return left.astype(F32) + right.astype(F32)


def total(parts):
    parts = [part.astype(F32) for part in parts]
    while len(parts) > 1:
        parts = [sum(parts[at + 1 : at + 2], parts[at]) for at in range(0, len(parts), 2)]
    return parts[0]


SMALL = 8


def split(values):
    high = values.astype(BF16).astype(F32)
    return high, (values - high).astype(BF16).astype(F32)


def small_sum(own, came):
    high, low = split(own)
    came = came.astype(F32)
    return (high + low) + (came[:SMALL] + came[SMALL:])


def put_small(message, at, values):
    message[at : at + 2 * SMALL] = jnp.concatenate(split(values), axis=0).astype(BF16)


BRIEF = 2 * 10**9


def merge(body, name, ins, outs, after=()):
    n_in = len(ins)

    def kernel(*refs):
        body(refs[:n_in], refs[n_in + len(after) :])

    return pl.pallas_call(
        kernel,
        name=name,
        out_shape=outs,
        in_specs=[pl.BlockSpec(memory_space=pltpu.VMEM)] * n_in
        + [pl.BlockSpec(memory_space=pl.ANY)] * len(after),
        out_specs=[pl.BlockSpec(memory_space=pltpu.VMEM)] * len(outs),
        compiler_params=pltpu.CompilerParams(vmem_limit_bytes=16 * 2**20),
        cost_estimate=pl.CostEstimate(flops=BRIEF, bytes_accessed=1, transcendentals=0),
    )(*ins, *after)


def exchange(name, jobs, small, after=()):
    rows = [keep.shape[0] // 2 for keep, _, _ in jobs]
    columns = min(keep.shape[1] for keep, _, _ in jobs)
    ins = []
    for keep, came, _ in jobs:
        ins += [keep, came]
    if small is not None:
        ins += [small[0], small[1]]

    def body(ins, outs):
        message = outs[-1]
        at = 0
        for job, (_, _, start) in enumerate(jobs):
            keep, came = ins[2 * job], ins[2 * job + 1]
            count = rows[job]
            sent = add(keep[count:], came[start + count : start + 2 * count])
            for column in range(0, keep.shape[1], columns):
                message[at : at + count] = sent[:, column : column + columns].astype(BF16)
                at += count
            outs[job][...] = add(keep[:count], came[start : start + count])
        if small is not None:
            values = small_sum(ins[-2][...], ins[-1][small[2] : small[2] + 2 * SMALL])
            outs[-2][...] = values
            put_small(message, at, values)

    wide = [keep.shape[1] for keep, _, _ in jobs]
    outs = [shape((count, width), F32) for count, width in zip(rows, wide)]
    height = sum(count * (width // columns) for count, width in zip(rows, wide))
    if small is not None:
        outs.append(shape(small[0].shape, F32))
        height += 2 * SMALL
    outs.append(shape((height, columns)))
    return merge(body, name, ins, outs, after)


def first_near(lengths, own, came, small=None, after=()):
    rows, columns = own.shape[0] // 2, own.shape[1]
    parts = 4
    size = rows // parts

    def body(lengths, loads, stores, scratch):
        out = stores[0]
        if small is not None:
            put_small(out.ref, rows, loads[2].ref()[...])
            out.send(pl.ds(rows, 2 * SMALL))
        for at in range(parts):
            cut = slice(at * size, (at + 1) * size)
            out.ref[cut] = add(loads[0].part(at)[cut], loads[1].part(at)[cut]).astype(BF16)
            out.send(pl.ds(at * size, size))

    ins = [Rows(own, rows, rows, parts), Rows(came, rows, rows, parts)]
    if small is not None:
        ins.append(small)
    rows_out = rows if small is None else rows + 2 * SMALL
    return call(body, "first_near", lengths, ins, [shape((rows_out, columns))], after=after)[0]


def kept_rows(own, came, near_came):
    rows = own.shape[0] // 2
    return [Rows(item, 0, rows, 4, True) for item in (own, came, near_came)]


def kept_sums(loads, stay, go):
    rows = loads[0].target.shape[0]
    size = rows // 4
    for at in range(4):
        start = (3 - at) * size
        cut = slice(start, start + size)
        own, came, near_came = (load.part(at)[cut] for load in loads)
        values = (add(own, came) + near_came.astype(F32)).astype(BF16)
        out, to = (go, start - rows // 2) if start >= rows // 2 else (stay, start)
        out.ref[to : to + size] = values
        out.send(pl.ds(to, size))


def second_low(lengths, own, came, near_came, after=()):
    rows, columns = own.shape[0] // 4, own.shape[1]

    def body(lengths, loads, stores, scratch):
        kept_sums(loads, *stores)

    return call(
        body,
        "second_low",
        lengths,
        kept_rows(own, came, near_came),
        [shape((rows, columns))] * 2,
        after=after,
    )


def second_far(lengths, own, came, near_came, down, low_came, small, after=()):
    rows, columns = own.shape[0] // 4, own.shape[1]
    less = down.shape[0] // 2

    def body(lengths, loads, stores, scratch):
        down, low_came, small_came, small = loads[:4]
        down_message, message, up_out, down_out, small_out = stores
        for at, (out, start) in enumerate(((down_message, less), (down_out, 0))):
            cut = slice(start, start + less)
            out.ref[...] = add(down.part(at)[cut], low_came.part(at)[cut]).astype(BF16)
            out.send()
        values = small_sum(small.ref()[...], small_came.ref()[...])
        put_small(message.ref, rows, values)
        message.send(pl.ds(rows, 2 * SMALL))
        small_out.ref[...] = values
        small_out.send()
        kept_sums(loads[4:], up_out, message)

    return call(
        body,
        "second_far",
        lengths,
        [Rows(down, 0, 2 * less, 2, True), Rows(low_came, 0, 2 * less, 2, True)]
        + [Rows(near_came, 2 * rows, 2 * SMALL), small, *kept_rows(own, came, near_came)],
        [
            shape((less, columns)),
            shape((rows + 2 * SMALL, columns)),
            shape((rows, columns)),
            shape((less, columns)),
            shape(small.shape, F32),
        ],
        after=after,
    )


def onward(lengths, name, jobs, small, after=()):
    rows = [keep.shape[0] // 2 for keep, _, _ in jobs]
    wide = [keep.shape[1] for keep, _, _ in jobs]
    columns = min(wide)
    height = sum(count * (width // columns) for count, width in zip(rows, wide))
    ins = []
    for (keep, came, start), count in zip(jobs, rows):
        ins += [Rows(keep, 0, 2 * count, 2, True), Rows(came, start, 2 * count, 2, True)]
    if small is not None:
        ins += [small[0], Rows(small[1], small[2], 2 * SMALL)]

    def body(lengths, loads, stores, scratch):
        message = stores[0]
        if small is not None:
            values = small_sum(loads[-2].ref()[...], loads[-1].ref()[...])
            stores[-1].ref[...] = values
            stores[-1].send()
            put_small(message.ref, height, values)
            message.send(pl.ds(height, 2 * SMALL))
        at = 0
        for job, count in enumerate(rows):
            keep, came = loads[2 * job], loads[2 * job + 1]
            for part, start in enumerate((count, 0)):
                cut = slice(start, start + count)
                values = add(keep.part(part)[cut], came.part(part)[cut]).astype(BF16)
                if part:
                    stores[1 + job].ref[...] = values
                    stores[1 + job].send()
                    continue
                first = at
                for column in range(0, wide[job], columns):
                    message.ref[at : at + count] = values[:, column : column + columns]
                    at += count
                message.send(pl.ds(first, at - first))

    outs = [shape((height + (2 * SMALL if small is not None else 0), columns))]
    outs += [shape((count, width)) for count, width in zip(rows, wide)]
    if small is not None:
        outs.append(shape(small[0].shape, F32))
    return call(body, name, lengths, ins, outs, after=after, cost=BRIEF)


def last_ffn(up, small, came, down, down_came, start):
    rows, columns = up.shape
    half = down_came.shape[1]

    def body(ins, outs):
        up, small, came, down, down_came = ins
        outs[0][...] = add(up[...], came[:rows])
        outs[2][...] = small_sum(small[...], came[rows:])
        for at in range(columns // half):
            cut = slice(at * half, (at + 1) * half)
            other = down_came[start + at * rows : start + (at + 1) * rows]
            outs[1][:, cut] = add(down[:, cut], other)

    return merge(
        body,
        "last_ffn",
        [up, small, came, down, down_came],
        [shape((rows, columns), F32), shape((rows, columns), F32), shape(small.shape, F32)],
    )


def last_heads(left, right, small, came):
    rows, columns = left.shape
    width = columns // 2

    def body(ins, outs):
        left, right, small, came = ins
        values = add(left[...], came[:rows])
        outs[0][...] = values[:, :width]
        outs[1][...] = values[:, width:]
        values = add(right[...], came[rows : 2 * rows])
        outs[2][...] = values[:, :width]
        outs[3][...] = values[:, width:]
        outs[4][...] = small_sum(small[...], came[2 * rows :])

    one = shape((rows, width), F32)
    return merge(
        body,
        "last_heads",
        [left, right, small, came],
        [one, one, one, one, shape(small.shape, F32)],
    )


def scatter(whole):
    return lax.psum_scatter(whole, "dp", scatter_dimension=0, tiled=True)


def local(
    tokens,
    seq_lengths,
    out_grad,
    w_query,
    bias_query,
    w_key,
    w_value,
    bias_value,
    w_out,
    bias_out,
    gain_one,
    shift_one,
    w_up,
    bias_up,
    w_down,
    bias_down,
    gain_two,
    shift_two,
):
    near = lax.axis_size("dp") == GROUPS
    SWAP[0] = near
    lengths = seq_lengths
    model = tokens.shape[1]
    length = tokens.shape[0] // seq_lengths.shape[0]
    width = w_query.shape[1]
    inner = w_up.shape[1]

    wo_b, wu_b, wd_b, bu_b = swap(w_out), swap(w_up), swap(w_down), swap(bias_up)
    query, keyed, valued, expo, att_own, att_other, inv, token_turned = attend(
        lengths, tokens, w_query, w_key, w_value, bias_query, bias_value, length
    )
    (
        normed,
        spread,
        hidden_turned,
        layer_own,
        grad_low,
        slope,
        slope_b,
        small_two,
        down_b,
        down_a,
    ) = middle(
        lengths,
        tokens,
        out_grad,
        (att_own, swap(att_other)),
        (w_out, wo_b),
        (bias_out, gain_one, shift_one, bias_down, gain_two, shift_two),
        (bias_up, bu_b),
        (w_up, wu_b),
        (w_down, wd_b),
        length,
    )
    down_came = swap(down_b)
    layer_other = swap(layer_own)
    up_b, back_b, bias_up_b = up_back(lengths, grad_low, wd_b, slope_b, hidden_turned, wu_b, length)
    up_came = swap(up_b)
    after = [back_b]
    if near:
        down_sent = first_near(lengths, down_a, down_came, after=after)
        near_down = flip(down_sent, NEAR)
        after = [down_sent]
    first_low, first_turned, small, up_a = up_own(
        lengths,
        grad_low,
        w_down,
        slope,
        w_up,
        back_b,
        normed,
        spread,
        gain_one,
        hidden_turned,
        (small_two, bias_up_b),
        length,
        after,
    )
    first_came = swap(first_low)
    after = []
    if near:
        up_sent = first_near(lengths, up_a, up_came, small)
        near_up = flip(up_sent, NEAR)
        down, down_sent = second_low(lengths, down_a, down_came, near_down, [up_sent])
        low_down = flip(down_sent, LOW)
        after = [down_sent]
    grads, small_heads, keep_p, send_p, keep_q, send_q, layer_output = attend_back(
        lengths,
        (first_low, first_came),
        first_turned,
        token_turned,
        w_out,
        (query, keyed, valued, expo, att_own, att_other, inv),
        [(layer_own, layer_other)],
        length,
        after,
    )
    after = []
    if near:
        came_p, came_q = flip(send_p, NEAR), flip(send_q, LOW)
        down_sent, sent, up, down, small = second_far(
            lengths, up_a, up_came, near_up, down, low_down, small, [keep_p]
        )
        high_down, far_came = flip(down_sent, HIGH), flip(sent, FAR)
        after = [sent]
    input_own, input_other = input_part(
        lengths, first_low, grads, (w_query, w_key, w_value), length, after
    )
    input_other = swap(input_other)
    if near:
        sent, heads_p, small_heads = onward(
            lengths,
            "heads_low",
            [(keep_p, came_p, 0)],
            (small_heads, came_p, model // 2),
            [input_own],
        )
        low_p = flip(sent, LOW)
        sent, heads_q = onward(lengths, "heads_near", [(keep_q, came_q, 0)], None, [sent])
        near_q = flip(sent, NEAR)
        sent, up, small = onward(
            lengths, "ffn_high", [(up, far_came, 0)], (small, far_came, up.shape[0]), [sent]
        )
        high_up = flip(sent, HIGH)
        sent, heads_p, heads_q, down, small_heads = onward(
            lengths,
            "heads_far",
            [(heads_p, low_p, 0), (heads_q, near_q, 0), (down, high_down, 0)],
            (small_heads, low_p, heads_p.shape[0]),
            [sent],
        )
        far_came = flip(sent, FAR)
        sent, up, small = onward(
            lengths, "ffn_low", [(up, high_up, 0)], (small, high_up, up.shape[0]), [sent]
        )
        low_up = flip(sent, LOW)
        input_other = together(input_other, sent)[0]
    input_own = (input_own.astype(F32) + input_other.astype(F32)).astype(BF16)
    (input_grad,) = call(
        lambda *_: None, "join", lengths, [], [], vmem=16, joins=[(input_own, swap(input_own))]
    )
    if near:
        rows = heads_p.shape[0]
        start = 2 * rows
        heads_p, heads_q, small_heads, sent = exchange(
            "heads_high",
            [(heads_p, far_came, 0), (heads_q, far_came, rows)],
            (small_heads, far_came, start + 2 * down.shape[0]),
            [input_own],
        )
        high_heads = flip(sent, HIGH)
        low_up = together(low_up, sent)[0]
        grad_up, grad_down, small = last_ffn(up, small, low_up, down, far_came, start)
        high_heads = together(high_heads, input_grad)[0]
        grad_query, grad_key, grad_value, grad_out, small_heads = last_heads(
            heads_p, heads_q, small_heads, high_heads
        )
    else:
        grad_down = scatter(total([down_a, down_came]))
        grad_up = scatter(total([up_a, up_came]))
        heads_p = scatter(jnp.concatenate([keep_p, send_p[: model // 2]], axis=0).astype(F32))
        heads_q = scatter(jnp.concatenate([keep_q, send_q], axis=0).astype(F32))
        small, small_heads = lax.psum((small, small_heads), "dp")
        grad_query, grad_key = heads_p[:, :width], heads_p[:, width:]
        grad_value, grad_out = heads_q[:, :width], heads_q[:, width:]
    small_other = together(swap(small), small_heads)[0]
    norms = (small[:3] + small_other[:3]).reshape(6, model)
    bias_up_grad = small[3] + small_other[4]
    bias_query_grad, bias_value_grad = small_heads[0, :width], small_heads[0, width:]
    gain_two_grad, shift_two_grad, bias_down_grad = norms[0], norms[1], norms[2]
    gain_one_grad, shift_one_grad, bias_out_grad = norms[3], norms[4], norms[5]
    return (
        layer_output,
        input_grad,
        grad_query,
        grad_key,
        grad_value,
        bias_query_grad,
        bias_value_grad,
        grad_out.T,
        bias_out_grad,
        gain_one_grad,
        shift_one_grad,
        grad_up,
        bias_up_grad,
        grad_down.T,
        bias_down_grad,
        gain_two_grad,
        shift_two_grad,
    )


def solution(mesh):
    return jax.shard_map(
        local,
        mesh=mesh,
        in_specs=(
            P("dp", None),
            P("dp"),
            P("dp", None),
            P(None, "tp"),
            P("tp"),
            P(None, "tp"),
            P(None, "tp"),
            P("tp"),
            P("tp", None),
            P(),
            P(),
            P(),
            P(None, "tp"),
            P("tp"),
            P("tp", None),
            P(),
            P(),
            P(),
        ),
        out_specs=(
            P("dp", None),
            P("dp", None),
            P("dp", "tp"),
            P("dp", "tp"),
            P("dp", "tp"),
            P("tp"),
            P("tp"),
            P("tp", "dp"),
            P(),
            P(),
            P(),
            P("dp", "tp"),
            P("tp"),
            P("tp", "dp"),
            P(),
            P(),
            P(),
        ),
        check_vma=False,
    )
```

```python
import jax
import jax.numpy as jnp
from jax import lax
from jax.experimental import pallas as pl
from jax.experimental.pallas import tpu as pltpu
from jax.sharding import PartitionSpec as P

HEAD = 64
PAIR = 128
EPS = 1e-05
GROUPS = 16
BF16 = jnp.bfloat16
F32 = jnp.float32
ROWS = 128
HIDDEN = 512


def nn(left, right):
    return lax.dot_general(left, right, (((1,), (0,)), ((), ())), preferred_element_type=F32)


def nt(left, right):
    return lax.dot_general(left, right, (((1,), (1,)), ((), ())), preferred_element_type=F32)


def tn(left, right):
    return lax.dot_general(left, right, (((0,), (0,)), ((), ())), preferred_element_type=F32)


def mean(values):
    return jnp.mean(values, axis=-1, keepdims=True)


def column_sum(values):
    return jnp.sum(values, axis=0, keepdims=True)


class Load:
    def __init__(self, source, target, sems, first, item):
        self.target, self.item = target, item
        self.source, self.sems, self.first = source, sems, first
        self.copies = []
        self.waited = set()
        if isinstance(item, Manual):
            return
        self.copies = [
            pltpu.make_async_copy(*item.ends(source, target, at), sems.at[first + at])
            for at in range(item.parts)
        ]

    def part(self, at):
        if at not in self.waited:
            self.copies[at].wait()
            self.waited.add(at)
        return self.target

    def columns(self, start, stop):
        if self.item.parts > 1:
            size = self.item.dims[self.item.axis] // self.item.parts
            for at in range(start // size, -(-stop // size)):
                self.part(at)
            return self.target
        return self.ref()

    def ref(self):
        for at in range(len(self.copies)):
            self.part(at)
        return self.target


class Store:
    def __init__(self, target, buffer, sems, first):
        self.target, self.ref, self.sems, self.next = target, buffer, sems, first
        self.copies = []
        self.manual = False

    def send(self, *index):
        source = self.ref.at[index] if index else self.ref
        target = self.target.at[index] if index else self.target
        copy = pltpu.make_async_copy(source, target, self.sems.at[self.next])
        copy.start()
        self.next += 1
        self.copies.append(copy)

    def finish(self):
        for copy in self.copies:
            copy.wait()


PARTS = 8


class Whole:
    def __init__(self, array, parts=1, axis=-1, late=False):
        self.array, self.dims = array, array.shape
        self.parts, self.axis, self.late = parts, axis % array.ndim, late

    def ends(self, source, target, at):
        if self.parts == 1:
            return source, target
        size = self.dims[self.axis] // self.parts
        cut = tuple(
            pl.ds(at * size, size) if axis == self.axis else pl.ds(0, dim)
            for axis, dim in enumerate(self.dims)
        )
        return source.at[cut], target.at[cut]


class Manual(Whole):
    pass


class OwnRows(Whole):
    def __init__(self, array, rows, late=False):
        super().__init__(array, late=late)
        self.dims = (rows,) + array.shape[1:]

    def ends(self, source, target, at):
        rows = self.dims[0]
        start = pl.multiple_of(lax.axis_index("tp") * rows, rows)
        return source.at[pl.ds(start, rows)], target


class Rows(Whole):
    def __init__(self, array, start, rows, parts=1, last=False):
        super().__init__(array, parts, 0)
        self.dims, self.start, self.last = (rows,) + array.shape[1:], start, last

    def ends(self, source, target, at):
        size = self.dims[0] // self.parts
        at = (self.parts - 1 - at if self.last else at) * size
        return source.at[pl.ds(self.start + at, size)], target.at[pl.ds(at, size)]


class BothRows(Whole):
    def __init__(self, array, rows):
        super().__init__(array, 2, 0)
        self.rows = rows

    def ends(self, source, target, at):
        core = lax.axis_index("tp")
        start = pl.multiple_of((core if at == 0 else 1 - core) * self.rows, self.rows)
        return source.at[pl.ds(start, self.rows)], target.at[pl.ds(at * self.rows, self.rows)]


class LateBoth(BothRows):
    def __init__(self, array, rows):
        super().__init__(array, rows)
        self.late = True


def call(body, name, lengths, ins, outs, scratch=(), vmem=64, after=(), joins=(), early=None, cost=1):
    ins = [item if isinstance(item, Whole) else Whole(item) for item in ins]
    n_in, n_out, n_after, n_join = len(ins), len(outs), len(after), len(joins)
    joined = [shape((2 * own.shape[0],) + own.shape[1:], own.dtype) for own, _ in joins]

    def kernel(lengths_ref, *refs):
        in_refs, refs = refs[:n_in], refs[n_in + n_after :]
        pair_refs, refs = refs[: 2 * n_join], refs[2 * n_join :]
        out_refs, refs = refs[:n_out], refs[n_out:]
        join_refs, refs = refs[:n_join], refs[n_join:]
        in_bufs, refs = refs[:n_in], refs[n_in:]
        out_bufs, refs = refs[:n_out], refs[n_out:]
        join_bufs, refs = refs[:n_join], refs[n_join:]
        in_sems, out_sems, join_sems, refs = refs[0], refs[1], refs[2], refs[3:]
        core = lax.axis_index("tp")
        copies = []
        for at in range(n_join):
            for side in range(2):
                source = pair_refs[2 * at + side]
                rows = source.shape[0]
                start = pl.multiple_of((core if side == 0 else 1 - core) * rows, rows)
                copies.append(
                    pltpu.make_async_copy(
                        source, join_bufs[at].at[pl.ds(start, rows)], join_sems.at[2 * at + side]
                    )
                )
        loads, first = [], 0
        for item, source, buffer in zip(ins, in_refs, in_bufs):
            loads.append(Load(source, buffer, in_sems, first, item))
            first += item.parts
        for late in (False, True):
            if late and early is not None:
                early(lengths_ref, loads)
            for at in range(max(item.parts for item in ins) if ins else 0):
                for load in loads:
                    if load.item.late == late and at < len(load.copies):
                        load.copies[at].start()
        stores = [
            Store(out_refs[at], out_bufs[at], out_sems, at * PARTS) for at in range(n_out)
        ]
        for copy in copies:
            copy.start()
        started = []

        def join():
            for copy in copies:
                copy.wait()
            for at in range(n_join):
                started.append(
                    pltpu.make_async_copy(join_bufs[at], join_refs[at], join_sems.at[2 * at])
                )
                started[-1].start()
            copies.clear()

        body(lengths_ref, loads, stores, (*refs, join))
        if copies:
            join()
        for store in stores:
            if not store.copies and not store.manual:
                store.send()
        for load in loads:
            load.ref()
        for store in stores:
            store.finish()
        for copy in started:
            copy.wait()

    return pl.pallas_call(
        kernel,
        name=name,
        out_shape=[*outs, *joined],
        in_specs=[pl.BlockSpec(memory_space=pltpu.SMEM)]
        + [pl.BlockSpec(memory_space=pl.ANY)] * (n_in + n_after + 2 * n_join),
        out_specs=[pl.BlockSpec(memory_space=pl.ANY)] * (n_out + n_join),
        scratch_shapes=[pltpu.VMEM(item.dims, item.array.dtype) for item in ins]
        + [pltpu.VMEM(out.shape, out.dtype) for out in [*outs, *joined]]
        + [
            pltpu.SemaphoreType.DMA((sum(item.parts for item in ins) + 1,)),
            pltpu.SemaphoreType.DMA((max(n_out, 1) * PARTS,)),
            pltpu.SemaphoreType.DMA((max(2 * n_join, 1),)),
        ]
        + list(scratch),
        compiler_params=pltpu.CompilerParams(vmem_limit_bytes=vmem * 2**20),
        cost_estimate=pl.CostEstimate(flops=cost, bytes_accessed=1, transcendentals=0),
    )(lengths, *(item.array for item in ins), *after, *(item for pair in joins for item in pair))


def line(load):
    ref = load.ref()
    return ref[...].astype(F32).reshape(1, ref.shape[0])


def length_of(lengths, at):
    core = lax.axis_index("tp")
    return lengths[core if at == 0 else 1 - core]


def places(order, partner=False):
    if not SWAP[0]:
        return list(range(GROUPS))
    place, core = lax.axis_index("dp"), lax.axis_index("tp")
    found = []
    for group in range(GROUPS):
        rel = jnp.bitwise_xor(place, group)
        bits = [rel % 2, (rel // 2) % 2, (rel // 4) % 2, rel // 8]
        near = jnp.where(core == (1 if partner else 0), bits[0], bits[1])
        bits[:2] = near, bits[0] + bits[1] - near
        found.append(sum(bit * (8 // 2**step) for bit, step in zip(bits, order)))
    return found


PLANE_FIRST = (0, 1, 2, 3)
Z_BETWEEN = (0, 2, 1, 3)


Z_FIRST = (1, 2, 0, 3)


def by_length(lengths, at, length, run):
    count = length_of(lengths, at)
    sizes = [size for size in (128, 256) if size < length] + [length]
    below = None
    for size in sizes:
        fits = count <= size
        if below is not None:
            fits = fits & (count > below)

        @pl.when(fits)
        def _(size=size):
            run(size)

        below = size


def shape(dims, dtype=BF16):
    return jax.ShapeDtypeStruct(dims, dtype)


def put_groups(target, place, values, columns):
    size = values.shape[0] // GROUPS
    for group in range(GROUPS):
        start = place[group] * size
        if not isinstance(start, int):
            start = pl.multiple_of(start, size)
        target[pl.ds(start, size), columns] = values[group * size : (group + 1) * size].astype(BF16)


def attend(lengths, tokens, w_query, w_key, w_value, bias_query, bias_value, length):
    width = w_query.shape[1]
    heads = width // HEAD

    def body(lengths, loads, stores, scratch):
        rows, wk, wq, wv, bq, bv = loads
        q_out, k_out, v_out, e_out, own_out, other_out, inv_out = stores
        (v_turned,) = scratch[:1]
        e_out.manual = True
        bq, bv = line(bq), line(bv)

        def lanes(head):
            return slice(head // 2 * PAIR, (head // 2 + 1) * PAIR)

        def sequence(at, size):
            near = slice(at * length, at * length + size)
            lane = lax.broadcasted_iota(jnp.int32, (size, PAIR), 1)
            row = lax.broadcasted_iota(jnp.int32, (size, PAIR), 0)
            count = length_of(lengths, at)
            masked = jnp.where((lane == 0) & (row >= count), -1e30, 0.0).astype(BF16)
            marker = jnp.where(lane == 0, 1.0, 0.0).astype(BF16)
            ones = jnp.ones((16, size), BF16)
            att_out = (own_out, other_out)[at]

            def scores(head):
                queries = q_out.ref[near, lanes(head)]
                own = jnp.where(lane // HEAD == head % 2, queries, jnp.zeros_like(queries))
                keys = jnp.concatenate([k_out.ref[near, lanes(head)], masked], axis=1)
                return nt(keys, jnp.concatenate([own, marker], axis=1))

            mixed, inverse = [], []

            def mix(head):
                values = v_turned[at, head * HEAD : (head + 1) * HEAD, :size]
                left = jnp.concatenate([values, ones], axis=0)
                sums = nn(left, e_out.ref[at * heads + head, :size, :size])
                inv = 1.0 / sums[HEAD : HEAD + 1]
                mixed.append(sums[:HEAD] * inv)
                inverse.append(jnp.broadcast_to(inv, (HEAD, size)))
                if head % 2:
                    att_out.ref[:size, lanes(head)] = (
                        jnp.concatenate(mixed, axis=0).astype(BF16).T
                    )
                    inv_out.ref[near, lanes(head)] = jnp.concatenate(inverse, axis=0).T
                    mixed.clear()
                    inverse.clear()

            now = scores(0)
            for head in range(heads):
                later = scores(head + 1) if head + 1 < heads else None
                top = jnp.max(now, axis=0, keepdims=True)
                e_out.ref[at * heads + head, :size, :size] = jnp.exp(now - top).astype(BF16)
                if head:
                    mix(head - 1)
                now = later
            mix(heads - 1)
            if size < length:
                att_out.ref[size:] = jnp.zeros((length - size, width), BF16)
            square(at, size).start()

        def square(at, size):
            cut = (pl.ds(at * heads, heads), pl.ds(0, size), pl.ds(0, size))
            return pltpu.make_async_copy(
                e_out.ref.at[cut], e_out.target.at[cut], e_out.sems.at[e_out.next + at]
            )

        for at in range(2):
            x = rows.part(at)
            near = slice(at * length, (at + 1) * length)
            k_out.ref[near] = nn(x[near], wk.ref()[...]).astype(BF16)
            q_out.ref[near] = (
                (nn(x[near], wq.ref()[...]) + bq).astype(BF16).astype(F32) * HEAD**-0.5
            ).astype(BF16)
            value = (nn(x[near], wv.ref()[...]) + bv).astype(BF16)
            v_out.ref[near] = value
            v_turned[at] = value.T
            by_length(lengths, at, length, lambda size: sequence(at, size))
            for out in (q_out, k_out, v_out, inv_out):
                out.send(pl.ds(at * length, length))
            (own_out, other_out)[at].send()
        for at in range(2):
            by_length(lengths, at, length, lambda size: square(at, size).wait())

    both = 2 * length
    return call(
        body,
        "attend",
        lengths,
        [BothRows(tokens, length), w_key, w_query, w_value, bias_query, bias_value],
        [
            shape((both, width)),
            shape((both, width)),
            shape((both, width)),
            shape((2 * heads, length, length)),
            shape((length, width)),
            shape((length, width)),
            shape((both, width), F32),
        ],
        scratch=[pltpu.VMEM((2, width, length), BF16)],
    )


def up_half(low, wu, bu, wd, act, slope, total, fresh):
    inner = act.shape[1]

    def project(start):
        return nn(low[...], wu[:, start : start + HIDDEN]) + bu[:, start : start + HIDDEN]

    now = project(0)
    for start in range(0, inner, HIDDEN):
        cut = slice(start, start + HIDDEN)
        later = project(start + HIDDEN) if start + HIDDEN < inner else None
        phi = 0.5 * (1.0 + lax.erf(now * (0.5**0.5)))
        act[:, cut] = (now * phi).astype(BF16)
        slope[:, cut] = (
            phi + now * (jnp.exp(-0.5 * now * now) * 0.3989422804014327)
        ).astype(BF16)
        part = nn(act[:, cut], wd[cut, :])
        if fresh and start == 0:
            total[...] = part
        else:
            total[...] += part
        now = later


def feed(lengths, tokens, out_grad, att, w_out, vectors, bias_up, w_up, w_down, length):
    model = tokens.shape[1]
    inner = w_up[0].shape[1]

    def body(lengths, loads, stores, scratch):
        att_a, wo_a, att_b, wo_b, rows, bo, g1, s1 = loads[:8]
        wu_a, bu_a, wd_a, wu_b, bu_b, wd_b, cot, bd, g2, s2 = loads[8:]
        first_out, layer_out, small, down_b, down_a, up_b, up_a = stores
        total, hidden, low, norm, spr, grad_low = scratch[:6]
        act_a, act_b, slope_a, slope_b, bias_a, bias_b = scratch[6:12]
        total[...] = nn(att_a.ref()[...], wo_a.ref()[...]) + nn(att_b.ref()[...], wo_b.ref()[...])
        x = rows.ref()
        bo, g1, s1 = line(bo), line(g1), line(s1)
        for start in range(0, length, ROWS):
            cut = slice(start, start + ROWS)
            value = x[cut].astype(F32) + (total[cut] + bo)
            centred = value - mean(value)
            spread = lax.rsqrt(mean(centred * centred) + EPS)
            normed = centred * spread
            norm[cut] = normed.astype(BF16)
            spr[cut] = jnp.broadcast_to(spread, (ROWS, 128))
            full = normed * g1 + s1
            hidden[cut] = full
            low[cut] = full.astype(BF16)
        for load in loads:
            load.ref()
        up_half(low, wu_a.ref(), line(bu_a), wd_a.ref(), act_a, slope_a, total, True)
        up_half(low, wu_b.ref(), line(bu_b), wd_b.ref(), act_b, slope_b, total, False)
        cot = cot.ref()
        bd, g2, s2 = line(bd), line(g2), line(s2)
        sums = [jnp.zeros((1, model), F32)] * 6
        for start in range(0, length, ROWS):
            cut = slice(start, start + ROWS)
            row = lax.broadcasted_iota(jnp.int32, (ROWS, model), 0) + start
            valid = jnp.where(row < length_of(lengths, 0), 1.0, 0.0)
            value = hidden[cut] + total[cut] + bd
            centred = value - mean(value)
            spread = lax.rsqrt(mean(centred * centred) + EPS)
            normed = centred * spread
            layer_out.ref[cut] = ((normed * g2 + s2) * valid).astype(BF16)
            grad = cot[cut].astype(F32) * valid
            scaled = grad * g2
            resid = spread * (scaled - mean(scaled) - normed * mean(scaled * normed))
            sums[0] += column_sum(grad * normed)
            sums[1] += column_sum(grad)
            sums[2] += column_sum(resid)
            grad_low[cut] = resid.astype(BF16)
        layer_out.send()
        slope_back(grad_low, wd_b.ref(), slope_b, bias_b)
        slope_back(grad_low, wd_a.ref(), slope_a, bias_a)
        total[...] = nt(slope_a[...], wu_a.ref()[...]) + nt(slope_b[...], wu_b.ref()[...])
        for start in range(0, length, ROWS):
            cut = slice(start, start + ROWS)
            value = grad_low[cut].astype(F32) + total[cut]
            normed = norm[cut].astype(F32)
            scaled = value * g1
            first = spr[cut, 0:1] * (scaled - mean(scaled) - normed * mean(scaled * normed))
            sums[3] += column_sum(value * normed)
            sums[4] += column_sum(value)
            sums[5] += column_sum(first)
            first_out.ref[cut] = first.astype(BF16)
        first_out.send()
        for at in range(3):
            small.ref[at : at + 1, :model] = sums[2 * at]
            small.ref[at : at + 1, model:] = sums[2 * at + 1]
        small.ref[3:4] = bias_a[0:1]
        small.ref[4:5] = bias_b[0:1]
        small.ref[5:8] = jnp.zeros((3, inner), F32)
        small.send()
        weight(down_b, grad_low, act_b, places(PLANE_FIRST, True))
        weight(up_b, low, slope_b, places(PLANE_FIRST, True))
        weight(down_a, grad_low, act_a, places(PLANE_FIRST))
        weight(up_a, low, slope_a, places(PLANE_FIRST))

    whole = shape((model, inner))
    half = pltpu.VMEM((length, inner), BF16)
    return call(
        body,
        "feed",
        lengths,
        [att[0], w_out[0], att[1], w_out[1], OwnRows(tokens, length), *vectors[:3]]
        + [w_up[0], bias_up[0], w_down[0], w_up[1], bias_up[1], w_down[1]]
        + [OwnRows(out_grad, length), *vectors[3:]],
        [shape((length, model)), shape((length, model)), shape((8, inner), F32)] + [whole] * 4,
        scratch=[
            pltpu.VMEM((length, model), F32),
            pltpu.VMEM((length, model), F32),
            pltpu.VMEM((length, model), BF16),
            pltpu.VMEM((length, model), BF16),
            pltpu.VMEM((length, 128), F32),
            pltpu.VMEM((length, model), BF16),
            half,
            half,
            half,
            half,
            pltpu.VMEM((8, inner), F32),
            pltpu.VMEM((8, inner), F32),
        ],
    )


SWAP = [True]


def weight(out, left, right, place):
    columns = right.shape[1]
    for start in range(0, columns, HIDDEN):
        cut = pl.ds(start, HIDDEN)
        put_groups(out.ref, place, tn(left[...], right[:, start : start + HIDDEN]), cut)
        out.send(slice(None), cut)


def slope_back(grad, wd, slope, bias):
    inner = slope.shape[1]

    def project(start):
        return nt(grad[...], wd[start : start + HIDDEN, :])

    now = project(0)
    for start in range(0, inner, HIDDEN):
        cut = slice(start, start + HIDDEN)
        later = project(start + HIDDEN) if start + HIDDEN < inner else None
        value = (now * slope[:, cut].astype(F32)).astype(BF16)
        slope[:, cut] = value
        bias[:, cut] = jnp.broadcast_to(column_sum(value.astype(F32)), (8, HIDDEN))
        now = later


def attend_back(
    lengths, low, tokens, w_out, saved, length, after=()
):
    query, keyed, valued, expo, att_own, att_other, inv = saved
    width, model = w_out.shape
    heads = width // HEAD
    both = 2 * length

    def square(e, at, size):
        cut = (pl.ds(at * heads, heads), pl.ds(0, size), pl.ds(0, size))
        return pltpu.make_async_copy(e.source.at[cut], e.target.at[cut], e.sems.at[e.first + at])

    def early(lengths, loads):
        for at in range(2):
            by_length(lengths, at, length, lambda size: square(loads[6], at, size).start())

    def body(lengths, loads, stores, scratch):
        grad_a, wo, k, v, inverse, att_a, e, q, grad_b, att_b = loads[:10]
        rows = loads[10]
        grads, small, *halves = stores
        dq, dk, dv = (grads.ref.at[:, pl.ds(at * width, width)] for at in range(3))
        mixed, k_turned, kept, first_p, first_q = scratch[:5]
        wo = wo.ref()
        atts = (att_a, att_b)

        def lanes(head):
            return slice(head // 2 * PAIR, (head // 2 + 1) * PAIR)

        def sequence(at, size):
            near = slice(at * length, at * length + size)
            lane = lax.broadcasted_iota(jnp.int32, (size, PAIR), 1)
            marker = jnp.where(lane < 2, 1.0, 0.0).astype(BF16)
            scaled_of, product_of = {}, {}

            def scores(head):
                cut, mine = lanes(head), lane // HEAD == head % 2
                if head % 2 == 0:
                    scaled = mixed[:size, cut].astype(F32) * inverse.target[near, cut]
                    product_of[head // 2] = scaled * atts[at].target[:size, cut].astype(F32)
                    scaled_of[head // 2] = scaled.astype(BF16)
                scaled, product = scaled_of[head // 2], product_of[head // 2]
                inner = -jnp.sum(jnp.where(mine, product, 0.0), axis=1, keepdims=True)
                high = inner.astype(BF16).astype(F32)
                extra = jnp.where(lane == 0, high, jnp.where(lane == 1, inner - high, 0.0))
                right = jnp.concatenate(
                    [jnp.where(mine, scaled, jnp.zeros_like(scaled)), extra.astype(BF16)], axis=1
                )
                return nt(jnp.concatenate([v.target[near, cut], marker], axis=1), right)

            dvs, dks, dqs = [], [], []

            def products(head):
                cut = lanes(head)
                grads = kept[head % 2, :size, :size]
                dks.append(nn(grads, q.target[near, cut]))
                dqs.append(nn(k_turned[head * HEAD : (head + 1) * HEAD, :size], grads))
                if head % 2:
                    dk[near, cut] = jnp.where(lane < HEAD, dks[0], dks[1]).astype(BF16)
                    dq[near, cut] = (jnp.concatenate(dqs, axis=0) * HEAD**-0.5).astype(BF16).T
                    dks.clear()
                    dqs.clear()

            square(e, at, size).wait()
            now = scores(0)
            for head in range(heads):
                later = scores(head + 1) if head + 1 < heads else None
                expo = e.target[at * heads + head, :size, :size]
                kept[head % 2, :size, :size] = (expo.astype(F32) * now).astype(BF16)
                dvs.append(nn(expo, scaled_of[head // 2]))
                if head % 2:
                    dv[near, lanes(head)] = jnp.where(lane < HEAD, dvs[0], dvs[1]).astype(BF16)
                    dvs.clear()
                if head:
                    products(head - 1)
                now = later
            products(heads - 1)
            if size < length:
                rest = slice(at * length + size, (at + 1) * length)
                grads.ref[rest] = jnp.zeros((length - size, 3 * width), BF16)

        for at, grad in enumerate((grad_a, grad_b)):
            near = slice(at * length, (at + 1) * length)
            mixed[...] = nt(grad.ref()[...], wo[...]).astype(BF16)
            k_turned[...] = k.part(at)[near].T
            for load in (inverse, v, q):
                load.part(at)
            atts[at].ref()
            by_length(lengths, at, length, lambda size: sequence(at, size))
            grads.send(pl.ds(at * length, length))
        sums = [column_sum(out[...].astype(F32)) for out in (dq, dv)]
        sums = jnp.concatenate(sums, axis=1)
        high = sums.astype(BF16).astype(F32)
        low = (sums - high).astype(BF16).astype(F32)
        first = lax.broadcasted_iota(jnp.int32, (8, 2 * width), 0) == 0
        small.ref[...] = jnp.where(first, high + low, 0.0)
        small.send()
        first_p[pl.ds(model, 2 * SMALL)] = jnp.concatenate(
            [jnp.where(first, high, 0.0), jnp.where(first, low, 0.0)], axis=0
        ).astype(BF16)
        x = rows.ref()
        for source, order, (keep, send), parts in (
            (first_p, Z_BETWEEN, halves[:2], (dq, dk)),
            (first_q, Z_FIRST, halves[2:], (dv, None)),
        ):
            place = places(order)
            for at, part in enumerate(parts):
                if part is None:
                    product = tn(grad_a.target[...], att_a.target[...])
                    product += tn(grad_b.target[...], att_b.target[...])
                else:
                    product = tn(x[...], part[...])
                put_groups(source, place, product, pl.ds(at * width, width))
            for out, start in ((send, model // 2), (keep, 0)):
                out.ref = source.at[pl.ds(start, out.target.shape[0])]
                out.send()

    half = shape((model // 2, 2 * width))
    return call(
        body,
        "attend_back",
        lengths,
        [low[0], w_out, *(Whole(item, 2, 0) for item in (keyed, valued, inv)), att_own]
        + [Manual(expo, 2, 0), Whole(query, 2, 0)]
        + [Whole(low[1], late=True), Whole(att_other, late=True), LateBoth(tokens, length)],
        [shape((both, 3 * width)), shape((8, 2 * width), F32), half, shape((model // 2 + 16, 2 * width))]
        + [half, half],
        scratch=[
            pltpu.VMEM((length, width), BF16),
            pltpu.VMEM((width, length), BF16),
            pltpu.VMEM((2, length, length), BF16),
            pltpu.VMEM((model + 2 * SMALL, 2 * width), BF16),
            pltpu.VMEM((model, 2 * width), BF16),
        ],
        after=after,
        early=early,
    )


def input_part(lengths, first, grads, weights, joins, length, after=()):
    model, width = weights[0].shape

    def body(lengths, loads, stores, scratch):
        side = scratch[0]
        copies = [
            pltpu.make_async_copy(
                load.source, side.at[:, pl.ds(at * width, width)], load.sems.at[load.first]
            )
            for at, load in enumerate(loads[1:4])
        ]
        for copy in copies:
            copy.start()
        for copy in copies:
            copy.wait()
        scratch[-1]()
        for at in (1, 0):
            near = slice(at * length, (at + 1) * length)
            total = nt(loads[0].part(at)[near], side[...])
            if not at:
                total += loads[4].ref()[...].astype(F32)
            stores[at].ref[...] = total.astype(BF16)
            stores[at].send()

    return call(
        body,
        "input_part",
        lengths,
        [Whole(grads, 2, 0), *(Manual(item) for item in weights), Whole(first, late=True)],
        [shape((length, model))] * 2,
        scratch=[pltpu.VMEM((model, 3 * width), BF16)],
        after=after,
        joins=joins,
    )


def swap(values):
    return lax.ppermute(values, "tp", [(0, 1), (1, 0)])


def together(*values):
    return lax.optimization_barrier(values)


def flip(values, bits):
    size = lax.axis_size("dp")
    perm = [(2 * d + c, 2 * (d ^ bits[c]) + c) for d in range(size) for c in range(2)]
    return lax.ppermute(values, ("dp", "tp"), perm)


NEAR, FAR, LOW, HIGH = (1, 2), (2, 1), (4, 4), (8, 8)


def add(left, right):
    return left.astype(F32) + right.astype(F32)


def total(parts):
    parts = [part.astype(F32) for part in parts]
    while len(parts) > 1:
        parts = [sum(parts[at + 1 : at + 2], parts[at]) for at in range(0, len(parts), 2)]
    return parts[0]


SMALL = 8


def split(values):
    high = values.astype(BF16).astype(F32)
    return high, (values - high).astype(BF16).astype(F32)


def small_sum(own, came):
    high, low = split(own)
    came = came.astype(F32)
    return (high + low) + (came[:SMALL] + came[SMALL:])


def put_small(message, at, values):
    message[at : at + 2 * SMALL] = jnp.concatenate(split(values), axis=0).astype(BF16)


BRIEF, LONG = 2 * 10**9, 2 * 10**10


def merge(body, name, ins, outs, after=()):
    n_in = len(ins)

    def kernel(*refs):
        body(refs[:n_in], refs[n_in + len(after) :])

    return pl.pallas_call(
        kernel,
        name=name,
        out_shape=outs,
        in_specs=[pl.BlockSpec(memory_space=pltpu.VMEM)] * n_in
        + [pl.BlockSpec(memory_space=pl.ANY)] * len(after),
        out_specs=[pl.BlockSpec(memory_space=pltpu.VMEM)] * len(outs),
        compiler_params=pltpu.CompilerParams(vmem_limit_bytes=16 * 2**20),
        cost_estimate=pl.CostEstimate(flops=BRIEF, bytes_accessed=1, transcendentals=0),
    )(*ins, *after)


def exchange(name, jobs, small, after=()):
    rows = [keep.shape[0] // 2 for keep, _, _ in jobs]
    columns = min(keep.shape[1] for keep, _, _ in jobs)
    ins = []
    for keep, came, _ in jobs:
        ins += [keep, came]
    if small is not None:
        ins += [small[0], small[1]]

    def body(ins, outs):
        message = outs[-1]
        at = 0
        for job, (_, _, start) in enumerate(jobs):
            keep, came = ins[2 * job], ins[2 * job + 1]
            count = rows[job]
            sent = add(keep[count:], came[start + count : start + 2 * count])
            for column in range(0, keep.shape[1], columns):
                message[at : at + count] = sent[:, column : column + columns].astype(BF16)
                at += count
            outs[job][...] = add(keep[:count], came[start : start + count])
        if small is not None:
            values = small_sum(ins[-2][...], ins[-1][small[2] : small[2] + 2 * SMALL])
            outs[-2][...] = values
            put_small(message, at, values)

    wide = [keep.shape[1] for keep, _, _ in jobs]
    outs = [shape((count, width), F32) for count, width in zip(rows, wide)]
    height = sum(count * (width // columns) for count, width in zip(rows, wide))
    if small is not None:
        outs.append(shape(small[0].shape, F32))
        height += 2 * SMALL
    outs.append(shape((height, columns)))
    return merge(body, name, ins, outs, after)


def first_near(lengths, own, came, small=None, after=()):
    rows, columns = own.shape[0] // 2, own.shape[1]
    parts = 4
    size = rows // parts

    def body(lengths, loads, stores, scratch):
        out = stores[0]
        if small is not None:
            put_small(out.ref, rows, loads[2].ref()[...])
            out.send(pl.ds(rows, 2 * SMALL))
        for at in range(parts):
            cut = slice(at * size, (at + 1) * size)
            out.ref[cut] = add(loads[0].part(at)[cut], loads[1].part(at)[cut]).astype(BF16)
            out.send(pl.ds(at * size, size))

    ins = [Rows(own, rows, rows, parts), Rows(came, rows, rows, parts)]
    if small is not None:
        ins.append(small)
    rows_out = rows if small is None else rows + 2 * SMALL
    return call(body, "first_near", lengths, ins, [shape((rows_out, columns))], after=after, cost=LONG)[0]


def kept_rows(own, came, near_came):
    rows = own.shape[0] // 2
    return [Rows(item, 0, rows, 4, True) for item in (own, came, near_came)]


def kept_sums(loads, stay, go):
    rows = loads[0].target.shape[0]
    size = rows // 4
    for at in range(4):
        start = (3 - at) * size
        cut = slice(start, start + size)
        own, came, near_came = (load.part(at)[cut] for load in loads)
        values = (add(own, came) + near_came.astype(F32)).astype(BF16)
        out, to = (go, start - rows // 2) if start >= rows // 2 else (stay, start)
        out.ref[to : to + size] = values
        out.send(pl.ds(to, size))


def second(lengths, name, own, came, near_came, small=None, after=()):
    rows, columns = own.shape[0] // 4, own.shape[1]

    def body(lengths, loads, stores, scratch):
        message, stay = stores[:2]
        if small is not None:
            values = small_sum(loads[-2].ref()[...], loads[-1].ref()[...])
            put_small(message.ref, rows, values)
            message.send(pl.ds(rows, 2 * SMALL))
            stores[2].ref[...] = values
            stores[2].send()
        kept_sums(loads[:3], stay, message)

    ins = kept_rows(own, came, near_came)
    outs = [shape((rows + (2 * SMALL if small is not None else 0), columns)), shape((rows, columns))]
    if small is not None:
        ins += [small, Rows(near_came, 2 * rows, 2 * SMALL)]
        outs.append(shape(small.shape, F32))
    return call(body, name, lengths, ins, outs, after=after, cost=BRIEF)


def onward(name, jobs, small, after=()):
    rows = [keep.shape[0] // 2 for keep, _, _ in jobs]
    columns = jobs[0][0].shape[1]
    height = sum(rows)
    ins = []
    for keep, came, _ in jobs:
        ins += [keep, came]
    if small is not None:
        ins += small[:2]

    def body(ins, outs):
        message = outs[0]
        at = 0
        for job, (count, (_, _, start)) in enumerate(zip(rows, jobs)):
            keep, came = ins[2 * job], ins[2 * job + 1]
            sent = add(keep[count:], came[start + count : start + 2 * count])
            message[at : at + count] = sent.astype(BF16)
            outs[1 + job][...] = add(keep[:count], came[start : start + count]).astype(BF16)
            at += count
        if small is not None:
            values = small_sum(ins[-2][...], ins[-1][small[2] : small[2] + 2 * SMALL])
            outs[-1][...] = values
            put_small(message, at, values)

    outs = [shape((height + (2 * SMALL if small is not None else 0), columns))]
    outs += [shape((count, columns)) for count in rows]
    if small is not None:
        outs.append(shape(small[0].shape, F32))
    return merge(body, name, ins, outs, after)


def last_up(up, small, came):
    rows = up.shape[0]

    def body(ins, outs):
        up, small, came = ins
        outs[0][...] = add(up[...], came[:rows])
        outs[1][...] = small_sum(small[...], came[rows:])

    return merge(
        body, "last_up", [up, small, came], [shape(up.shape, F32), shape(small.shape, F32)]
    )


def last_heads(left, right, small, came):
    rows, columns = left.shape
    width = columns // 2

    def body(ins, outs):
        left, right, small, came = ins
        values = add(left[...], came[:rows])
        outs[0][...] = values[:, :width]
        outs[1][...] = values[:, width:]
        values = add(right[...], came[rows : 2 * rows])
        outs[2][...] = values[:, :width]
        outs[3][...] = values[:, width:]
        outs[4][...] = small_sum(small[...], came[2 * rows :])

    one = shape((rows, width), F32)
    return merge(
        body,
        "last_heads",
        [left, right, small, came],
        [one, one, one, one, shape(small.shape, F32)],
    )


def scatter(whole):
    return lax.psum_scatter(whole, "dp", scatter_dimension=0, tiled=True)


def local(
    tokens,
    seq_lengths,
    out_grad,
    w_query,
    bias_query,
    w_key,
    w_value,
    bias_value,
    w_out,
    bias_out,
    gain_one,
    shift_one,
    w_up,
    bias_up,
    w_down,
    bias_down,
    gain_two,
    shift_two,
):
    near = lax.axis_size("dp") == GROUPS
    SWAP[0] = near
    lengths = seq_lengths
    model = tokens.shape[1]
    length = tokens.shape[0] // seq_lengths.shape[0]
    width = w_query.shape[1]
    inner = w_up.shape[1]

    wo_b, wu_b, wd_b, bu_b = swap(w_out), swap(w_up), swap(w_down), swap(bias_up)
    query, keyed, valued, expo, att_own, att_other, inv = attend(
        lengths, tokens, w_query, w_key, w_value, bias_query, bias_value, length
    )
    first_low, layer_own, small, down_b, down_a, up_b, up_a = feed(
        lengths,
        tokens,
        out_grad,
        (att_own, swap(att_other)),
        (w_out, wo_b),
        (bias_out, gain_one, shift_one, bias_down, gain_two, shift_two),
        (bias_up, bu_b),
        (w_up, wu_b),
        (w_down, wd_b),
        length,
    )
    first_came = swap(first_low)
    down_came = swap(down_b)
    up_came = swap(up_b)
    layer_other = swap(layer_own)
    if near:
        down_sent = first_near(lengths, down_a, down_came, after=[first_came])
        near_down = flip(down_sent, NEAR)
    after = []
    if near:
        up_sent = first_near(lengths, up_a, up_came, small, [down_sent])
        near_up = flip(up_sent, NEAR)
        after = [up_sent]
    grads, small_heads, keep_p, send_p, keep_q, send_q = attend_back(
        lengths,
        (first_low, first_came),
        tokens,
        w_out,
        (query, keyed, valued, expo, att_own, att_other, inv),
        length,
        after,
    )
    after = []
    if near:
        came_p, came_q = flip(send_p, NEAR), flip(send_q, LOW)
        sent, down = second(
            lengths, "down_far", down_a, down_came, near_down, after=[keep_p]
        )
        far_down = flip(sent, FAR)
        sent, up, small = second(
            lengths, "up_far", up_a, up_came, near_up, small, [sent]
        )
        far_up = flip(sent, FAR)
        after = [sent]
    input_own, input_other, layer_output = input_part(
        lengths,
        first_low,
        grads,
        (w_query, w_key, w_value),
        [(layer_own, layer_other)],
        length,
        after,
    )
    input_other = swap(input_other)
    if near:
        came_p = together(came_p, input_own)[0]
        sent, heads_p, small_heads = onward(
            "heads_low",
            [(keep_p, came_p, 0)],
            (small_heads, came_p, model // 2),
        )
        low_p = flip(sent, LOW)
        sent, heads_q = onward("heads_near", [(keep_q, came_q, 0)], None, [sent])
        near_q = flip(sent, NEAR)
        sent, down = onward("down_low", [(down, far_down, 0)], None, [sent])
        low_down = flip(sent, LOW)
        sent, up, small = onward(
            "up_low", [(up, far_up, 0)], (small, far_up, up.shape[0]), [sent]
        )
        low_up = flip(sent, LOW)
        sent, heads_p, heads_q, small_heads = onward(
            "heads_far",
            [(heads_p, low_p, 0), (heads_q, near_q, 0)],
            (small_heads, low_p, heads_p.shape[0]),
            [sent],
        )
        far_heads = flip(sent, FAR)
        sent, down = onward("down_high", [(down, low_down, 0)], None, [sent])
        high_down = flip(sent, HIGH)
        input_other = together(input_other, sent)[0]
    input_own = (input_own.astype(F32) + input_other.astype(F32)).astype(BF16)
    (input_grad,) = call(
        lambda *_: None, "join", lengths, [], [], vmem=16, joins=[(input_own, swap(input_own))]
    )
    if near:
        rows = heads_p.shape[0]
        sent, heads_p, heads_q, small_heads = onward(
            "heads_high",
            [(heads_p, far_heads, 0), (heads_q, far_heads, rows)],
            (small_heads, far_heads, 2 * rows),
            [input_own],
        )
        high_heads = flip(sent, HIGH)
        sent, up, small = onward(
            "up_high", [(up, low_up, 0)], (small, low_up, up.shape[0]), [sent]
        )
        high_up = flip(sent, HIGH)
        grad_down = add(down, high_down)
        grad_up, small = last_up(up, small, high_up)
        high_heads = together(high_heads, input_grad)[0]
        grad_query, grad_key, grad_value, grad_out, small_heads = last_heads(
            heads_p, heads_q, small_heads, high_heads
        )
    else:
        grad_down = scatter(total([down_a, down_came]))
        grad_up = scatter(total([up_a, up_came]))
        heads_p = scatter(jnp.concatenate([keep_p, send_p[: model // 2]], axis=0).astype(F32))
        heads_q = scatter(jnp.concatenate([keep_q, send_q], axis=0).astype(F32))
        small, small_heads = lax.psum((small, small_heads), "dp")
        grad_query, grad_key = heads_p[:, :width], heads_p[:, width:]
        grad_value, grad_out = heads_q[:, :width], heads_q[:, width:]
    small_other = together(swap(small), small_heads)[0]
    norms = (small[:3] + small_other[:3]).reshape(6, model)
    bias_up_grad = small[3] + small_other[4]
    bias_query_grad, bias_value_grad = small_heads[0, :width], small_heads[0, width:]
    gain_two_grad, shift_two_grad, bias_down_grad = norms[0], norms[1], norms[2]
    gain_one_grad, shift_one_grad, bias_out_grad = norms[3], norms[4], norms[5]
    return (
        layer_output,
        input_grad,
        grad_query,
        grad_key,
        grad_value,
        bias_query_grad,
        bias_value_grad,
        grad_out.T,
        bias_out_grad,
        gain_one_grad,
        shift_one_grad,
        grad_up,
        bias_up_grad,
        grad_down.T,
        bias_down_grad,
        gain_two_grad,
        shift_two_grad,
    )


def solution(mesh):
    return jax.shard_map(
        local,
        mesh=mesh,
        in_specs=(
            P("dp", None),
            P("dp"),
            P("dp", None),
            P(None, "tp"),
            P("tp"),
            P(None, "tp"),
            P(None, "tp"),
            P("tp"),
            P("tp", None),
            P(),
            P(),
            P(),
            P(None, "tp"),
            P("tp"),
            P("tp", None),
            P(),
            P(),
            P(),
        ),
        out_specs=(
            P("dp", None),
            P("dp", None),
            P("dp", "tp"),
            P("dp", "tp"),
            P("dp", "tp"),
            P("tp"),
            P("tp"),
            P("tp", "dp"),
            P(),
            P(),
            P(),
            P("dp", "tp"),
            P("tp"),
            P("tp", "dp"),
            P(),
            P(),
            P(),
        ),
        check_vma=False,
    )
```

```python
import jax
import jax.numpy as jnp
from jax import lax
from jax.experimental import pallas as pl
from jax.experimental.pallas import tpu as pltpu
from jax.sharding import PartitionSpec as P

HEAD = 64
PAIR = 128
EPS = 1e-05
GROUPS = 16
BF16 = jnp.bfloat16
F32 = jnp.float32
ROWS = 128
HIDDEN = 512


def nn(left, right):
    return lax.dot_general(left, right, (((1,), (0,)), ((), ())), preferred_element_type=F32)


def nt(left, right):
    return lax.dot_general(left, right, (((1,), (1,)), ((), ())), preferred_element_type=F32)


def tn(left, right):
    return lax.dot_general(left, right, (((0,), (0,)), ((), ())), preferred_element_type=F32)


def mean(values):
    return jnp.mean(values, axis=-1, keepdims=True)


def column_sum(values):
    return jnp.sum(values, axis=0, keepdims=True)


class Load:
    def __init__(self, source, target, sems, first, item):
        self.target, self.item = target, item
        self.source, self.sems, self.first = source, sems, first
        self.copies = []
        self.waited = set()
        if isinstance(item, Manual):
            return
        self.copies = [
            pltpu.make_async_copy(*item.ends(source, target, at), sems.at[first + at])
            for at in range(item.parts)
        ]

    def part(self, at):
        if at not in self.waited:
            self.copies[at].wait()
            self.waited.add(at)
        return self.target

    def columns(self, start, stop):
        if self.item.parts > 1:
            size = self.item.dims[self.item.axis] // self.item.parts
            for at in range(start // size, -(-stop // size)):
                self.part(at)
            return self.target
        return self.ref()

    def ref(self):
        for at in range(len(self.copies)):
            self.part(at)
        return self.target


class Store:
    def __init__(self, target, buffer, sems, first):
        self.target, self.ref, self.sems, self.next = target, buffer, sems, first
        self.copies = []
        self.manual = False

    def send(self, *index):
        source = self.ref.at[index] if index else self.ref
        target = self.target.at[index] if index else self.target
        copy = pltpu.make_async_copy(source, target, self.sems.at[self.next])
        copy.start()
        self.next += 1
        self.copies.append(copy)

    def finish(self):
        for copy in self.copies:
            copy.wait()


PARTS = 8


class Whole:
    def __init__(self, array, parts=1, axis=-1, late=False):
        self.array, self.dims = array, array.shape
        self.parts, self.axis, self.late = parts, axis % array.ndim, late

    def ends(self, source, target, at):
        if self.parts == 1:
            return source, target
        size = self.dims[self.axis] // self.parts
        cut = tuple(
            pl.ds(at * size, size) if axis == self.axis else pl.ds(0, dim)
            for axis, dim in enumerate(self.dims)
        )
        return source.at[cut], target.at[cut]


class Manual(Whole):
    pass


class OwnRows(Whole):
    def __init__(self, array, rows, late=False):
        super().__init__(array, late=late)
        self.dims = (rows,) + array.shape[1:]

    def ends(self, source, target, at):
        rows = self.dims[0]
        start = pl.multiple_of(lax.axis_index("tp") * rows, rows)
        return source.at[pl.ds(start, rows)], target


class Rows(Whole):
    def __init__(self, array, start, rows, parts=1, last=False):
        super().__init__(array, parts, 0)
        self.dims, self.start, self.last = (rows,) + array.shape[1:], start, last

    def ends(self, source, target, at):
        size = self.dims[0] // self.parts
        at = (self.parts - 1 - at if self.last else at) * size
        return source.at[pl.ds(self.start + at, size)], target.at[pl.ds(at, size)]


class BothRows(Whole):
    def __init__(self, array, rows):
        super().__init__(array, 2, 0)
        self.rows = rows

    def ends(self, source, target, at):
        core = lax.axis_index("tp")
        start = pl.multiple_of((core if at == 0 else 1 - core) * self.rows, self.rows)
        return source.at[pl.ds(start, self.rows)], target.at[pl.ds(at * self.rows, self.rows)]


class LateBoth(BothRows):
    def __init__(self, array, rows):
        super().__init__(array, rows)
        self.late = True


def call(body, name, lengths, ins, outs, scratch=(), vmem=64, after=(), joins=(), early=None, cost=1):
    ins = [item if isinstance(item, Whole) else Whole(item) for item in ins]
    n_in, n_out, n_after, n_join = len(ins), len(outs), len(after), len(joins)
    joined = [shape((2 * own.shape[0],) + own.shape[1:], own.dtype) for own, _ in joins]

    def kernel(lengths_ref, *refs):
        in_refs, refs = refs[:n_in], refs[n_in + n_after :]
        pair_refs, refs = refs[: 2 * n_join], refs[2 * n_join :]
        out_refs, refs = refs[:n_out], refs[n_out:]
        join_refs, refs = refs[:n_join], refs[n_join:]
        in_bufs, refs = refs[:n_in], refs[n_in:]
        out_bufs, refs = refs[:n_out], refs[n_out:]
        join_bufs, refs = refs[:n_join], refs[n_join:]
        in_sems, out_sems, join_sems, refs = refs[0], refs[1], refs[2], refs[3:]
        core = lax.axis_index("tp")
        copies = []
        for at in range(n_join):
            for side in range(2):
                source = pair_refs[2 * at + side]
                rows = source.shape[0]
                start = pl.multiple_of((core if side == 0 else 1 - core) * rows, rows)
                copies.append(
                    pltpu.make_async_copy(
                        source, join_bufs[at].at[pl.ds(start, rows)], join_sems.at[2 * at + side]
                    )
                )
        loads, first = [], 0
        for item, source, buffer in zip(ins, in_refs, in_bufs):
            loads.append(Load(source, buffer, in_sems, first, item))
            first += item.parts
        for late in (False, True):
            if late and early is not None:
                early(lengths_ref, loads)
            for at in range(max(item.parts for item in ins) if ins else 0):
                for load in loads:
                    if load.item.late == late and at < len(load.copies):
                        load.copies[at].start()
        stores = [
            Store(out_refs[at], out_bufs[at], out_sems, at * PARTS) for at in range(n_out)
        ]
        for copy in copies:
            copy.start()
        started = []

        def join():
            for copy in copies:
                copy.wait()
            for at in range(n_join):
                started.append(
                    pltpu.make_async_copy(join_bufs[at], join_refs[at], join_sems.at[2 * at])
                )
                started[-1].start()
            copies.clear()

        body(lengths_ref, loads, stores, (*refs, join))
        if copies:
            join()
        for store in stores:
            if not store.copies and not store.manual:
                store.send()
        for load in loads:
            load.ref()
        for store in stores:
            store.finish()
        for copy in started:
            copy.wait()

    return pl.pallas_call(
        kernel,
        name=name,
        out_shape=[*outs, *joined],
        in_specs=[pl.BlockSpec(memory_space=pltpu.SMEM)]
        + [pl.BlockSpec(memory_space=pl.ANY)] * (n_in + n_after + 2 * n_join),
        out_specs=[pl.BlockSpec(memory_space=pl.ANY)] * (n_out + n_join),
        scratch_shapes=[pltpu.VMEM(item.dims, item.array.dtype) for item in ins]
        + [pltpu.VMEM(out.shape, out.dtype) for out in [*outs, *joined]]
        + [
            pltpu.SemaphoreType.DMA((sum(item.parts for item in ins) + 1,)),
            pltpu.SemaphoreType.DMA((max(n_out, 1) * PARTS,)),
            pltpu.SemaphoreType.DMA((max(2 * n_join, 1),)),
        ]
        + list(scratch),
        compiler_params=pltpu.CompilerParams(vmem_limit_bytes=vmem * 2**20),
        cost_estimate=pl.CostEstimate(flops=cost, bytes_accessed=1, transcendentals=0),
    )(lengths, *(item.array for item in ins), *after, *(item for pair in joins for item in pair))


def line(load):
    ref = load.ref()
    return ref[...].astype(F32).reshape(1, ref.shape[0])


def length_of(lengths, at):
    core = lax.axis_index("tp")
    return lengths[core if at == 0 else 1 - core]


def places(order, partner=False):
    if not SWAP[0]:
        return list(range(GROUPS))
    place, core = lax.axis_index("dp"), lax.axis_index("tp")
    found = []
    for group in range(GROUPS):
        rel = jnp.bitwise_xor(place, group)
        bits = [rel % 2, (rel // 2) % 2, (rel // 4) % 2, rel // 8]
        near = jnp.where(core == (1 if partner else 0), bits[0], bits[1])
        bits[:2] = near, bits[0] + bits[1] - near
        found.append(sum(bit * (8 // 2**step) for bit, step in zip(bits, order)))
    return found


PLANE_FIRST = (0, 1, 2, 3)
Z_BETWEEN = (0, 2, 1, 3)


Z_FIRST = (1, 2, 0, 3)


def by_length(lengths, at, length, run):
    count = length_of(lengths, at)
    sizes = [size for size in (128, 256) if size < length] + [length]
    below = None
    for size in sizes:
        fits = count <= size
        if below is not None:
            fits = fits & (count > below)

        @pl.when(fits)
        def _(size=size):
            run(size)

        below = size


def shape(dims, dtype=BF16):
    return jax.ShapeDtypeStruct(dims, dtype)


def put_groups(target, place, values, columns):
    size = values.shape[0] // GROUPS
    for group in range(GROUPS):
        start = place[group] * size
        if not isinstance(start, int):
            start = pl.multiple_of(start, size)
        target[pl.ds(start, size), columns] = values[group * size : (group + 1) * size].astype(BF16)


def attend(lengths, tokens, w_query, w_key, w_value, bias_query, bias_value, length):
    width = w_query.shape[1]
    heads = width // HEAD

    def body(lengths, loads, stores, scratch):
        rows, wk, wq, wv, bq, bv = loads
        q_out, k_out, v_out, e_out, own_out, other_out, inv_out = stores
        (v_turned,) = scratch[:1]
        e_out.manual = True
        bq, bv = line(bq), line(bv)

        def lanes(head):
            return slice(head // 2 * PAIR, (head // 2 + 1) * PAIR)

        def sequence(at, size):
            near = slice(at * length, at * length + size)
            lane = lax.broadcasted_iota(jnp.int32, (size, PAIR), 1)
            row = lax.broadcasted_iota(jnp.int32, (size, PAIR), 0)
            count = length_of(lengths, at)
            masked = jnp.where((lane == 0) & (row >= count), -1e30, 0.0).astype(BF16)
            marker = jnp.where(lane == 0, 1.0, 0.0).astype(BF16)
            ones = jnp.ones((16, size), BF16)
            att_out = (own_out, other_out)[at]

            def scores(head):
                queries = q_out.ref[near, lanes(head)]
                own = jnp.where(lane // HEAD == head % 2, queries, jnp.zeros_like(queries))
                keys = jnp.concatenate([k_out.ref[near, lanes(head)], masked], axis=1)
                return nt(keys, jnp.concatenate([own, marker], axis=1))

            mixed, inverse = [], []

            def mix(head):
                values = v_turned[at, head * HEAD : (head + 1) * HEAD, :size]
                left = jnp.concatenate([values, ones], axis=0)
                sums = nn(left, e_out.ref[at * heads + head, :size, :size])
                inv = 1.0 / sums[HEAD : HEAD + 1]
                mixed.append(sums[:HEAD] * inv)
                inverse.append(jnp.broadcast_to(inv, (HEAD, size)))
                if head % 2:
                    att_out.ref[:size, lanes(head)] = (
                        jnp.concatenate(mixed, axis=0).astype(BF16).T
                    )
                    inv_out.ref[near, lanes(head)] = jnp.concatenate(inverse, axis=0).T
                    mixed.clear()
                    inverse.clear()

            now = scores(0)
            for head in range(heads):
                later = scores(head + 1) if head + 1 < heads else None
                top = jnp.max(now, axis=0, keepdims=True)
                e_out.ref[at * heads + head, :size, :size] = jnp.exp(now - top).astype(BF16)
                if head:
                    mix(head - 1)
                now = later
            mix(heads - 1)
            if size < length:
                att_out.ref[size:] = jnp.zeros((length - size, width), BF16)
            square(at, size).start()

        def square(at, size):
            cut = (pl.ds(at * heads, heads), pl.ds(0, size), pl.ds(0, size))
            return pltpu.make_async_copy(
                e_out.ref.at[cut], e_out.target.at[cut], e_out.sems.at[e_out.next + at]
            )

        for at in range(2):
            x = rows.part(at)
            near = slice(at * length, (at + 1) * length)
            k_out.ref[near] = nn(x[near], wk.ref()[...]).astype(BF16)
            q_out.ref[near] = (
                (nn(x[near], wq.ref()[...]) + bq).astype(BF16).astype(F32) * HEAD**-0.5
            ).astype(BF16)
            value = (nn(x[near], wv.ref()[...]) + bv).astype(BF16)
            v_out.ref[near] = value
            v_turned[at] = value.T
            by_length(lengths, at, length, lambda size: sequence(at, size))
            for out in (q_out, k_out, v_out, inv_out):
                out.send(pl.ds(at * length, length))
            (own_out, other_out)[at].send()
        for at in range(2):
            by_length(lengths, at, length, lambda size: square(at, size).wait())

    both = 2 * length
    return call(
        body,
        "attend",
        lengths,
        [BothRows(tokens, length), w_key, w_query, w_value, bias_query, bias_value],
        [
            shape((both, width)),
            shape((both, width)),
            shape((both, width)),
            shape((2 * heads, length, length)),
            shape((length, width)),
            shape((length, width)),
            shape((both, width), F32),
        ],
        scratch=[pltpu.VMEM((2, width, length), BF16)],
    )


def up_half(low, wu, bu, wd, act, slope, total, fresh):
    inner = act.shape[1]

    def project(start):
        return nn(low[...], wu[:, start : start + HIDDEN]) + bu[:, start : start + HIDDEN]

    now = project(0)
    for start in range(0, inner, HIDDEN):
        cut = slice(start, start + HIDDEN)
        later = project(start + HIDDEN) if start + HIDDEN < inner else None
        phi = 0.5 * (1.0 + lax.erf(now * (0.5**0.5)))
        act[:, cut] = (now * phi).astype(BF16)
        slope[:, cut] = (
            phi + now * (jnp.exp(-0.5 * now * now) * 0.3989422804014327)
        ).astype(BF16)
        part = nn(act[:, cut], wd[cut, :])
        if fresh and start == 0:
            total[...] = part
        else:
            total[...] += part
        now = later


def feed(lengths, tokens, out_grad, att, w_out, vectors, bias_up, w_up, w_down, length):
    model = tokens.shape[1]
    inner = w_up[0].shape[1]

    def body(lengths, loads, stores, scratch):
        att_a, wo_a, att_b, wo_b, rows, bo, g1, s1 = loads[:8]
        wu_a, bu_a, wd_a, wu_b, bu_b, wd_b, cot, bd, g2, s2 = loads[8:]
        first_out, layer_out, small, down_b, down_a, up_b, up_a = stores
        total, hidden, low, norm, spr, grad_low = scratch[:6]
        act_a, act_b, slope_a, slope_b, bias_a, bias_b = scratch[6:12]
        total[...] = nn(att_a.ref()[...], wo_a.ref()[...]) + nn(att_b.ref()[...], wo_b.ref()[...])
        x = rows.ref()
        bo, g1, s1 = line(bo), line(g1), line(s1)
        for start in range(0, length, ROWS):
            cut = slice(start, start + ROWS)
            value = x[cut].astype(F32) + (total[cut] + bo)
            centred = value - mean(value)
            spread = lax.rsqrt(mean(centred * centred) + EPS)
            normed = centred * spread
            norm[cut] = normed.astype(BF16)
            spr[cut] = jnp.broadcast_to(spread, (ROWS, 128))
            full = normed * g1 + s1
            hidden[cut] = full
            low[cut] = full.astype(BF16)
        for load in loads[:11]:
            load.ref()
        up_half(low, wu_a.ref(), line(bu_a), wd_a.ref(), act_a, slope_a, total, True)
        for load in loads:
            load.ref()
        up_half(low, wu_b.ref(), line(bu_b), wd_b.ref(), act_b, slope_b, total, False)
        cot = cot.ref()
        bd, g2, s2 = line(bd), line(g2), line(s2)
        sums = [jnp.zeros((1, model), F32)] * 6
        for start in range(0, length, ROWS):
            cut = slice(start, start + ROWS)
            row = lax.broadcasted_iota(jnp.int32, (ROWS, model), 0) + start
            valid = jnp.where(row < length_of(lengths, 0), 1.0, 0.0)
            value = hidden[cut] + total[cut] + bd
            centred = value - mean(value)
            spread = lax.rsqrt(mean(centred * centred) + EPS)
            normed = centred * spread
            layer_out.ref[cut] = ((normed * g2 + s2) * valid).astype(BF16)
            grad = cot[cut].astype(F32) * valid
            scaled = grad * g2
            resid = spread * (scaled - mean(scaled) - normed * mean(scaled * normed))
            sums[0] += column_sum(grad * normed)
            sums[1] += column_sum(grad)
            sums[2] += column_sum(resid)
            grad_low[cut] = resid.astype(BF16)
        layer_out.send()
        slope_back(grad_low, wd_b.ref(), slope_b, bias_b)
        slope_back(grad_low, wd_a.ref(), slope_a, bias_a)
        total[...] = nt(slope_a[...], wu_a.ref()[...]) + nt(slope_b[...], wu_b.ref()[...])
        for start in range(0, length, ROWS):
            cut = slice(start, start + ROWS)
            value = grad_low[cut].astype(F32) + total[cut]
            normed = norm[cut].astype(F32)
            scaled = value * g1
            first = spr[cut, 0:1] * (scaled - mean(scaled) - normed * mean(scaled * normed))
            sums[3] += column_sum(value * normed)
            sums[4] += column_sum(value)
            sums[5] += column_sum(first)
            first_out.ref[cut] = first.astype(BF16)
        first_out.send()
        for at in range(3):
            small.ref[at : at + 1, :model] = sums[2 * at]
            small.ref[at : at + 1, model:] = sums[2 * at + 1]
        small.ref[3:4] = bias_a[0:1]
        small.ref[4:5] = bias_b[0:1]
        small.ref[5:8] = jnp.zeros((3, inner), F32)
        small.send()
        weight(down_b, grad_low, act_b, places(PLANE_FIRST, True))
        weight(up_b, low, slope_b, places(PLANE_FIRST, True))
        weight(down_a, grad_low, act_a, places(PLANE_FIRST))
        weight(up_a, low, slope_a, places(PLANE_FIRST))

    whole = shape((model, inner))
    half = pltpu.VMEM((length, inner), BF16)
    return call(
        body,
        "feed",
        lengths,
        [att[0], w_out[0], att[1], w_out[1], OwnRows(tokens, length), *vectors[:3]]
        + [w_up[0], bias_up[0], w_down[0], w_up[1], bias_up[1], w_down[1]]
        + [OwnRows(out_grad, length), *vectors[3:]],
        [shape((length, model)), shape((length, model)), shape((8, inner), F32)] + [whole] * 4,
        scratch=[
            pltpu.VMEM((length, model), F32),
            pltpu.VMEM((length, model), F32),
            pltpu.VMEM((length, model), BF16),
            pltpu.VMEM((length, model), BF16),
            pltpu.VMEM((length, 128), F32),
            pltpu.VMEM((length, model), BF16),
            half,
            half,
            half,
            half,
            pltpu.VMEM((8, inner), F32),
            pltpu.VMEM((8, inner), F32),
        ],
    )


SWAP = [True]


def weight(out, left, right, place):
    columns = right.shape[1]
    for start in range(0, columns, HIDDEN):
        cut = pl.ds(start, HIDDEN)
        put_groups(out.ref, place, tn(left[...], right[:, start : start + HIDDEN]), cut)
        out.send(slice(None), cut)


def slope_back(grad, wd, slope, bias):
    inner = slope.shape[1]

    def project(start):
        return nt(grad[...], wd[start : start + HIDDEN, :])

    now = project(0)
    for start in range(0, inner, HIDDEN):
        cut = slice(start, start + HIDDEN)
        later = project(start + HIDDEN) if start + HIDDEN < inner else None
        value = (now * slope[:, cut].astype(F32)).astype(BF16)
        slope[:, cut] = value
        bias[:, cut] = jnp.broadcast_to(column_sum(value.astype(F32)), (8, HIDDEN))
        now = later


def attend_back(
    lengths, low, tokens, w_out, saved, length, after=()
):
    query, keyed, valued, expo, att_own, att_other, inv = saved
    width, model = w_out.shape
    heads = width // HEAD
    both = 2 * length

    def square(e, at, size):
        cut = (pl.ds(at * heads, heads), pl.ds(0, size), pl.ds(0, size))
        return pltpu.make_async_copy(e.source.at[cut], e.target.at[cut], e.sems.at[e.first + at])

    def early(lengths, loads):
        for at in range(2):
            by_length(lengths, at, length, lambda size: square(loads[6], at, size).start())

    def body(lengths, loads, stores, scratch):
        grad_a, wo, k, v, inverse, att_a, e, q, grad_b, att_b = loads[:10]
        rows = loads[10]
        grads, small, *halves = stores
        dq, dk, dv = (grads.ref.at[:, pl.ds(at * width, width)] for at in range(3))
        mixed, k_turned, kept, first_p, first_q = scratch[:5]
        wo = wo.ref()
        atts = (att_a, att_b)

        def lanes(head):
            return slice(head // 2 * PAIR, (head // 2 + 1) * PAIR)

        def sequence(at, size):
            near = slice(at * length, at * length + size)
            lane = lax.broadcasted_iota(jnp.int32, (size, PAIR), 1)
            marker = jnp.where(lane < 2, 1.0, 0.0).astype(BF16)
            scaled_of, product_of = {}, {}

            def scores(head):
                cut, mine = lanes(head), lane // HEAD == head % 2
                if head % 2 == 0:
                    scaled = mixed[:size, cut].astype(F32) * inverse.target[near, cut]
                    product_of[head // 2] = scaled * atts[at].target[:size, cut].astype(F32)
                    scaled_of[head // 2] = scaled.astype(BF16)
                scaled, product = scaled_of[head // 2], product_of[head // 2]
                inner = -jnp.sum(jnp.where(mine, product, 0.0), axis=1, keepdims=True)
                high = inner.astype(BF16).astype(F32)
                extra = jnp.where(lane == 0, high, jnp.where(lane == 1, inner - high, 0.0))
                right = jnp.concatenate(
                    [jnp.where(mine, scaled, jnp.zeros_like(scaled)), extra.astype(BF16)], axis=1
                )
                return nt(jnp.concatenate([v.target[near, cut], marker], axis=1), right)

            dvs, dks, dqs = [], [], []

            def products(head):
                cut = lanes(head)
                grads = kept[head % 2, :size, :size]
                dks.append(nn(grads, q.target[near, cut]))
                dqs.append(nn(k_turned[head * HEAD : (head + 1) * HEAD, :size], grads))
                if head % 2:
                    dk[near, cut] = jnp.where(lane < HEAD, dks[0], dks[1]).astype(BF16)
                    dq[near, cut] = (jnp.concatenate(dqs, axis=0) * HEAD**-0.5).astype(BF16).T
                    dks.clear()
                    dqs.clear()

            square(e, at, size).wait()
            now = scores(0)
            for head in range(heads):
                later = scores(head + 1) if head + 1 < heads else None
                expo = e.target[at * heads + head, :size, :size]
                kept[head % 2, :size, :size] = (expo.astype(F32) * now).astype(BF16)
                dvs.append(nn(expo, scaled_of[head // 2]))
                if head % 2:
                    dv[near, lanes(head)] = jnp.where(lane < HEAD, dvs[0], dvs[1]).astype(BF16)
                    dvs.clear()
                if head:
                    products(head - 1)
                now = later
            products(heads - 1)
            if size < length:
                rest = slice(at * length + size, (at + 1) * length)
                grads.ref[rest] = jnp.zeros((length - size, 3 * width), BF16)

        for at, grad in enumerate((grad_a, grad_b)):
            near = slice(at * length, (at + 1) * length)
            mixed[...] = nt(grad.ref()[...], wo[...]).astype(BF16)
            k_turned[...] = k.part(at)[near].T
            for load in (inverse, v, q):
                load.part(at)
            atts[at].ref()
            by_length(lengths, at, length, lambda size: sequence(at, size))
            grads.send(pl.ds(at * length, length))
        sums = [column_sum(out[...].astype(F32)) for out in (dq, dv)]
        sums = jnp.concatenate(sums, axis=1)
        high = sums.astype(BF16).astype(F32)
        low = (sums - high).astype(BF16).astype(F32)
        first = lax.broadcasted_iota(jnp.int32, (8, 2 * width), 0) == 0
        small.ref[...] = jnp.where(first, high + low, 0.0)
        small.send()
        first_p[pl.ds(model, 2 * SMALL)] = jnp.concatenate(
            [jnp.where(first, high, 0.0), jnp.where(first, low, 0.0)], axis=0
        ).astype(BF16)
        x = rows.ref()
        for source, order, (keep, send), parts in (
            (first_p, Z_BETWEEN, halves[:2], (dq, dk)),
            (first_q, Z_FIRST, halves[2:], (dv, None)),
        ):
            place = places(order)
            for at, part in enumerate(parts):
                if part is None:
                    product = tn(grad_a.target[...], att_a.target[...])
                    product += tn(grad_b.target[...], att_b.target[...])
                else:
                    product = tn(x[...], part[...])
                put_groups(source, place, product, pl.ds(at * width, width))
            for out, start in ((send, model // 2), (keep, 0)):
                out.ref = source.at[pl.ds(start, out.target.shape[0])]
                out.send()

    half = shape((model // 2, 2 * width))
    return call(
        body,
        "attend_back",
        lengths,
        [low[0], w_out, *(Whole(item, 2, 0) for item in (keyed, valued, inv)), att_own]
        + [Manual(expo, 2, 0), Whole(query, 2, 0)]
        + [Whole(low[1], late=True), Whole(att_other, late=True), LateBoth(tokens, length)],
        [shape((both, 3 * width)), shape((8, 2 * width), F32), half, shape((model // 2 + 16, 2 * width))]
        + [half, half],
        scratch=[
            pltpu.VMEM((length, width), BF16),
            pltpu.VMEM((width, length), BF16),
            pltpu.VMEM((2, length, length), BF16),
            pltpu.VMEM((model + 2 * SMALL, 2 * width), BF16),
            pltpu.VMEM((model, 2 * width), BF16),
        ],
        after=after,
        early=early,
    )


def input_part(lengths, first, grads, weights, joins, length, after=()):
    model, width = weights[0].shape

    def body(lengths, loads, stores, scratch):
        side = scratch[0]
        copies = [
            pltpu.make_async_copy(
                load.source, side.at[:, pl.ds(at * width, width)], load.sems.at[load.first]
            )
            for at, load in enumerate(loads[1:4])
        ]
        for copy in copies:
            copy.start()
        for copy in copies:
            copy.wait()
        scratch[-1]()
        for at in (1, 0):
            near = slice(at * length, (at + 1) * length)
            total = nt(loads[0].part(at)[near], side[...])
            if not at:
                total += loads[4].ref()[...].astype(F32)
            stores[at].ref[...] = total.astype(BF16)
            stores[at].send()

    return call(
        body,
        "input_part",
        lengths,
        [Whole(grads, 2, 0), *(Manual(item) for item in weights), Whole(first, late=True)],
        [shape((length, model))] * 2,
        scratch=[pltpu.VMEM((model, 3 * width), BF16)],
        after=after,
        joins=joins,
    )


def swap(values):
    return lax.ppermute(values, "tp", [(0, 1), (1, 0)])


def together(*values):
    return lax.optimization_barrier(values)


def flip(values, bits):
    size = lax.axis_size("dp")
    perm = [(2 * d + c, 2 * (d ^ bits[c]) + c) for d in range(size) for c in range(2)]
    return lax.ppermute(values, ("dp", "tp"), perm)


NEAR, FAR, LOW, HIGH = (1, 2), (2, 1), (4, 4), (8, 8)


def add(left, right):
    return left.astype(F32) + right.astype(F32)


def total(parts):
    parts = [part.astype(F32) for part in parts]
    while len(parts) > 1:
        parts = [sum(parts[at + 1 : at + 2], parts[at]) for at in range(0, len(parts), 2)]
    return parts[0]


SMALL = 8


def split(values):
    high = values.astype(BF16).astype(F32)
    return high, (values - high).astype(BF16).astype(F32)


def small_sum(own, came):
    high, low = split(own)
    came = came.astype(F32)
    return (high + low) + (came[:SMALL] + came[SMALL:])


def put_small(message, at, values):
    message[at : at + 2 * SMALL] = jnp.concatenate(split(values), axis=0).astype(BF16)


BRIEF, LONG = 2 * 10**9, 2 * 10**10


def merge(body, name, ins, outs, after=()):
    n_in = len(ins)

    def kernel(*refs):
        body(refs[:n_in], refs[n_in + len(after) :])

    return pl.pallas_call(
        kernel,
        name=name,
        out_shape=outs,
        in_specs=[pl.BlockSpec(memory_space=pltpu.VMEM)] * n_in
        + [pl.BlockSpec(memory_space=pl.ANY)] * len(after),
        out_specs=[pl.BlockSpec(memory_space=pltpu.VMEM)] * len(outs),
        compiler_params=pltpu.CompilerParams(vmem_limit_bytes=16 * 2**20),
        cost_estimate=pl.CostEstimate(flops=BRIEF, bytes_accessed=1, transcendentals=0),
    )(*ins, *after)


def exchange(name, jobs, small, after=()):
    rows = [keep.shape[0] // 2 for keep, _, _ in jobs]
    columns = min(keep.shape[1] for keep, _, _ in jobs)
    ins = []
    for keep, came, _ in jobs:
        ins += [keep, came]
    if small is not None:
        ins += [small[0], small[1]]

    def body(ins, outs):
        message = outs[-1]
        at = 0
        for job, (_, _, start) in enumerate(jobs):
            keep, came = ins[2 * job], ins[2 * job + 1]
            count = rows[job]
            sent = add(keep[count:], came[start + count : start + 2 * count])
            for column in range(0, keep.shape[1], columns):
                message[at : at + count] = sent[:, column : column + columns].astype(BF16)
                at += count
            outs[job][...] = add(keep[:count], came[start : start + count])
        if small is not None:
            values = small_sum(ins[-2][...], ins[-1][small[2] : small[2] + 2 * SMALL])
            outs[-2][...] = values
            put_small(message, at, values)

    wide = [keep.shape[1] for keep, _, _ in jobs]
    outs = [shape((count, width), F32) for count, width in zip(rows, wide)]
    height = sum(count * (width // columns) for count, width in zip(rows, wide))
    if small is not None:
        outs.append(shape(small[0].shape, F32))
        height += 2 * SMALL
    outs.append(shape((height, columns)))
    return merge(body, name, ins, outs, after)


def first_near(lengths, own, came, small=None, after=()):
    rows, columns = own.shape[0] // 2, own.shape[1]
    parts = 4
    size = rows // parts

    def body(lengths, loads, stores, scratch):
        out = stores[0]
        if small is not None:
            put_small(out.ref, rows, loads[2].ref()[...])
            out.send(pl.ds(rows, 2 * SMALL))
        for at in range(parts):
            cut = slice(at * size, (at + 1) * size)
            out.ref[cut] = add(loads[0].part(at)[cut], loads[1].part(at)[cut]).astype(BF16)
            out.send(pl.ds(at * size, size))

    ins = [Rows(own, rows, rows, parts), Rows(came, rows, rows, parts)]
    if small is not None:
        ins.append(small)
    rows_out = rows if small is None else rows + 2 * SMALL
    return call(body, "first_near", lengths, ins, [shape((rows_out, columns))], after=after, cost=LONG)[0]


def kept_rows(own, came, near_came):
    rows = own.shape[0] // 2
    return [Rows(item, 0, rows, 4, True) for item in (own, came, near_came)]


def kept_sums(loads, stay, go):
    rows = loads[0].target.shape[0]
    size = rows // 4
    for at in range(4):
        start = (3 - at) * size
        cut = slice(start, start + size)
        own, came, near_came = (load.part(at)[cut] for load in loads)
        values = (add(own, came) + near_came.astype(F32)).astype(BF16)
        out, to = (go, start - rows // 2) if start >= rows // 2 else (stay, start)
        out.ref[to : to + size] = values
        out.send(pl.ds(to, size))


def second(lengths, name, own, came, near_came, small=None, after=()):
    rows, columns = own.shape[0] // 4, own.shape[1]

    def body(lengths, loads, stores, scratch):
        message, stay = stores[:2]
        if small is not None:
            values = small_sum(loads[-2].ref()[...], loads[-1].ref()[...])
            put_small(message.ref, rows, values)
            message.send(pl.ds(rows, 2 * SMALL))
            stores[2].ref[...] = values
            stores[2].send()
        kept_sums(loads[:3], stay, message)

    ins = kept_rows(own, came, near_came)
    outs = [shape((rows + (2 * SMALL if small is not None else 0), columns)), shape((rows, columns))]
    if small is not None:
        ins += [small, Rows(near_came, 2 * rows, 2 * SMALL)]
        outs.append(shape(small.shape, F32))
    return call(body, name, lengths, ins, outs, after=after, cost=BRIEF)


def onward(name, jobs, small, after=()):
    rows = [keep.shape[0] // 2 for keep, _, _ in jobs]
    columns = jobs[0][0].shape[1]
    height = sum(rows)
    ins = []
    for keep, came, _ in jobs:
        ins += [keep, came]
    if small is not None:
        ins += small[:2]

    def body(ins, outs):
        message = outs[0]
        at = 0
        for job, (count, (_, _, start)) in enumerate(zip(rows, jobs)):
            keep, came = ins[2 * job], ins[2 * job + 1]
            sent = add(keep[count:], came[start + count : start + 2 * count])
            message[at : at + count] = sent.astype(BF16)
            outs[1 + job][...] = add(keep[:count], came[start : start + count]).astype(BF16)
            at += count
        if small is not None:
            values = small_sum(ins[-2][...], ins[-1][small[2] : small[2] + 2 * SMALL])
            outs[-1][...] = values
            put_small(message, at, values)

    outs = [shape((height + (2 * SMALL if small is not None else 0), columns))]
    outs += [shape((count, columns)) for count in rows]
    if small is not None:
        outs.append(shape(small[0].shape, F32))
    return merge(body, name, ins, outs, after)


def last_up(up, small, came):
    rows = up.shape[0]

    def body(ins, outs):
        up, small, came = ins
        outs[0][...] = add(up[...], came[:rows])
        outs[1][...] = small_sum(small[...], came[rows:])

    return merge(
        body, "last_up", [up, small, came], [shape(up.shape, F32), shape(small.shape, F32)]
    )


def last_heads(left, right, small, came):
    rows, columns = left.shape
    width = columns // 2

    def body(ins, outs):
        left, right, small, came = ins
        values = add(left[...], came[:rows])
        outs[0][...] = values[:, :width]
        outs[1][...] = values[:, width:]
        values = add(right[...], came[rows : 2 * rows])
        outs[2][...] = values[:, :width]
        outs[3][...] = values[:, width:]
        outs[4][...] = small_sum(small[...], came[2 * rows :])

    one = shape((rows, width), F32)
    return merge(
        body,
        "last_heads",
        [left, right, small, came],
        [one, one, one, one, shape(small.shape, F32)],
    )


def scatter(whole):
    return lax.psum_scatter(whole, "dp", scatter_dimension=0, tiled=True)


def local(
    tokens,
    seq_lengths,
    out_grad,
    w_query,
    bias_query,
    w_key,
    w_value,
    bias_value,
    w_out,
    bias_out,
    gain_one,
    shift_one,
    w_up,
    bias_up,
    w_down,
    bias_down,
    gain_two,
    shift_two,
):
    near = lax.axis_size("dp") == GROUPS
    SWAP[0] = near
    lengths = seq_lengths
    model = tokens.shape[1]
    length = tokens.shape[0] // seq_lengths.shape[0]
    width = w_query.shape[1]
    inner = w_up.shape[1]

    wo_b, wu_b, wd_b, bu_b = swap(w_out), swap(w_up), swap(w_down), swap(bias_up)
    query, keyed, valued, expo, att_own, att_other, inv = attend(
        lengths, tokens, w_query, w_key, w_value, bias_query, bias_value, length
    )
    first_low, layer_own, small, down_b, down_a, up_b, up_a = feed(
        lengths,
        tokens,
        out_grad,
        (att_own, swap(att_other)),
        (w_out, wo_b),
        (bias_out, gain_one, shift_one, bias_down, gain_two, shift_two),
        (bias_up, bu_b),
        (w_up, wu_b),
        (w_down, wd_b),
        length,
    )
    first_came = swap(first_low)
    down_came = swap(down_b)
    up_came = swap(up_b)
    layer_other = swap(layer_own)
    if near:
        down_sent = first_near(lengths, down_a, down_came, after=[first_came])
        near_down = flip(down_sent, NEAR)
    after = []
    if near:
        up_sent = first_near(lengths, up_a, up_came, small, [down_sent])
        near_up = flip(up_sent, NEAR)
        after = [up_sent]
    grads, small_heads, keep_p, send_p, keep_q, send_q = attend_back(
        lengths,
        (first_low, first_came),
        tokens,
        w_out,
        (query, keyed, valued, expo, att_own, att_other, inv),
        length,
        after,
    )
    after = []
    if near:
        came_p, came_q = flip(send_p, NEAR), flip(send_q, LOW)
        sent, down = second(
            lengths, "down_far", down_a, down_came, near_down, after=[keep_p]
        )
        far_down = flip(sent, FAR)
        sent, up, small = second(
            lengths, "up_far", up_a, up_came, near_up, small, [sent]
        )
        far_up = flip(sent, FAR)
        after = [sent]
    input_own, input_other, layer_output = input_part(
        lengths,
        first_low,
        grads,
        (w_query, w_key, w_value),
        [(layer_own, layer_other)],
        length,
        after,
    )
    input_other = swap(input_other)
    if near:
        came_p = together(came_p, input_own)[0]
        sent, heads_p, small_heads = onward(
            "heads_low",
            [(keep_p, came_p, 0)],
            (small_heads, came_p, model // 2),
        )
        low_p = flip(sent, LOW)
        sent, heads_q = onward("heads_near", [(keep_q, came_q, 0)], None, [sent])
        near_q = flip(sent, NEAR)
        sent, down = onward("down_low", [(down, far_down, 0)], None, [sent])
        low_down = flip(sent, LOW)
        sent, up, small = onward(
            "up_low", [(up, far_up, 0)], (small, far_up, up.shape[0]), [sent]
        )
        low_up = flip(sent, LOW)
        sent, heads_p, heads_q, small_heads = onward(
            "heads_far",
            [(heads_p, low_p, 0), (heads_q, near_q, 0)],
            (small_heads, low_p, heads_p.shape[0]),
            [sent],
        )
        far_heads = flip(sent, FAR)
        sent, down = onward("down_high", [(down, low_down, 0)], None, [sent])
        high_down = flip(sent, HIGH)
        input_other = together(input_other, sent)[0]
    input_own = (input_own.astype(F32) + input_other.astype(F32)).astype(BF16)
    (input_grad,) = call(
        lambda *_: None, "join", lengths, [], [], vmem=16, joins=[(input_own, swap(input_own))]
    )
    if near:
        rows = heads_p.shape[0]
        sent, heads_p, heads_q, small_heads = onward(
            "heads_high",
            [(heads_p, far_heads, 0), (heads_q, far_heads, rows)],
            (small_heads, far_heads, 2 * rows),
            [input_own],
        )
        high_heads = flip(sent, HIGH)
        sent, up, small = onward(
            "up_high", [(up, low_up, 0)], (small, low_up, up.shape[0]), [sent]
        )
        high_up = flip(sent, HIGH)
        grad_down = add(down, high_down)
        high_up = together(high_up, input_grad)[0]
        grad_up, small = last_up(up, small, high_up)
        high_heads = together(high_heads, input_grad)[0]
        grad_query, grad_key, grad_value, grad_out, small_heads = last_heads(
            heads_p, heads_q, small_heads, high_heads
        )
    else:
        grad_down = scatter(total([down_a, down_came]))
        grad_up = scatter(total([up_a, up_came]))
        heads_p = scatter(jnp.concatenate([keep_p, send_p[: model // 2]], axis=0).astype(F32))
        heads_q = scatter(jnp.concatenate([keep_q, send_q], axis=0).astype(F32))
        small, small_heads = lax.psum((small, small_heads), "dp")
        grad_query, grad_key = heads_p[:, :width], heads_p[:, width:]
        grad_value, grad_out = heads_q[:, :width], heads_q[:, width:]
    small_other = together(swap(small), small_heads)[0]
    norms = (small[:3] + small_other[:3]).reshape(6, model)
    bias_up_grad = small[3] + small_other[4]
    bias_query_grad, bias_value_grad = small_heads[0, :width], small_heads[0, width:]
    gain_two_grad, shift_two_grad, bias_down_grad = norms[0], norms[1], norms[2]
    gain_one_grad, shift_one_grad, bias_out_grad = norms[3], norms[4], norms[5]
    return (
        layer_output,
        input_grad,
        grad_query,
        grad_key,
        grad_value,
        bias_query_grad,
        bias_value_grad,
        grad_out.T,
        bias_out_grad,
        gain_one_grad,
        shift_one_grad,
        grad_up,
        bias_up_grad,
        grad_down.T,
        bias_down_grad,
        gain_two_grad,
        shift_two_grad,
    )


def solution(mesh):
    return jax.shard_map(
        local,
        mesh=mesh,
        in_specs=(
            P("dp", None),
            P("dp"),
            P("dp", None),
            P(None, "tp"),
            P("tp"),
            P(None, "tp"),
            P(None, "tp"),
            P("tp"),
            P("tp", None),
            P(),
            P(),
            P(),
            P(None, "tp"),
            P("tp"),
            P("tp", None),
            P(),
            P(),
            P(),
        ),
        out_specs=(
            P("dp", None),
            P("dp", None),
            P("dp", "tp"),
            P("dp", "tp"),
            P("dp", "tp"),
            P("tp"),
            P("tp"),
            P("tp", "dp"),
            P(),
            P(),
            P(),
            P("dp", "tp"),
            P("tp"),
            P("tp", "dp"),
            P(),
            P(),
            P(),
        ),
        check_vma=False,
    )
```

```python
import jax
import jax.numpy as jnp
from jax import lax
from jax.experimental import pallas as pl
from jax.experimental.pallas import tpu as pltpu
from jax.sharding import PartitionSpec as P

HEAD = 64
PAIR = 128
EPS = 1e-05
GROUPS = 16
BF16 = jnp.bfloat16
F32 = jnp.float32
ROWS = 128
HIDDEN = 512


def nn(left, right):
    return lax.dot_general(left, right, (((1,), (0,)), ((), ())), preferred_element_type=F32)


def nt(left, right):
    return lax.dot_general(left, right, (((1,), (1,)), ((), ())), preferred_element_type=F32)


def tn(left, right):
    return lax.dot_general(left, right, (((0,), (0,)), ((), ())), preferred_element_type=F32)


def mean(values):
    return jnp.mean(values, axis=-1, keepdims=True)


def column_sum(values):
    return jnp.sum(values, axis=0, keepdims=True)


class Load:
    def __init__(self, source, target, sems, first, item):
        self.target, self.item = target, item
        self.source, self.sems, self.first = source, sems, first
        self.copies = []
        self.waited = set()
        if isinstance(item, Manual):
            return
        self.copies = [
            pltpu.make_async_copy(*item.ends(source, target, at), sems.at[first + at])
            for at in range(item.parts)
        ]

    def part(self, at):
        if at not in self.waited:
            self.copies[at].wait()
            self.waited.add(at)
        return self.target

    def columns(self, start, stop):
        if self.item.parts > 1:
            size = self.item.dims[self.item.axis] // self.item.parts
            for at in range(start // size, -(-stop // size)):
                self.part(at)
            return self.target
        return self.ref()

    def ref(self):
        for at in range(len(self.copies)):
            self.part(at)
        return self.target


class Store:
    def __init__(self, target, buffer, sems, first):
        self.target, self.ref, self.sems, self.next = target, buffer, sems, first
        self.copies = []
        self.manual = False

    def send(self, *index):
        source = self.ref.at[index] if index else self.ref
        target = self.target.at[index] if index else self.target
        copy = pltpu.make_async_copy(source, target, self.sems.at[self.next])
        copy.start()
        self.next += 1
        self.copies.append(copy)

    def finish(self):
        for copy in self.copies:
            copy.wait()


PARTS = 8


class Whole:
    def __init__(self, array, parts=1, axis=-1, late=False):
        self.array, self.dims = array, array.shape
        self.parts, self.axis, self.late = parts, axis % array.ndim, late

    def ends(self, source, target, at):
        if self.parts == 1:
            return source, target
        size = self.dims[self.axis] // self.parts
        cut = tuple(
            pl.ds(at * size, size) if axis == self.axis else pl.ds(0, dim)
            for axis, dim in enumerate(self.dims)
        )
        return source.at[cut], target.at[cut]


class Manual(Whole):
    pass


class OwnRows(Whole):
    def __init__(self, array, rows, late=False):
        super().__init__(array, late=late)
        self.dims = (rows,) + array.shape[1:]

    def ends(self, source, target, at):
        rows = self.dims[0]
        start = pl.multiple_of(lax.axis_index("tp") * rows, rows)
        return source.at[pl.ds(start, rows)], target


class Rows(Whole):
    def __init__(self, array, start, rows, parts=1, last=False):
        super().__init__(array, parts, 0)
        self.dims, self.start, self.last = (rows,) + array.shape[1:], start, last

    def ends(self, source, target, at):
        size = self.dims[0] // self.parts
        at = (self.parts - 1 - at if self.last else at) * size
        return source.at[pl.ds(self.start + at, size)], target.at[pl.ds(at, size)]


class BothRows(Whole):
    def __init__(self, array, rows):
        super().__init__(array, 2, 0)
        self.rows = rows

    def ends(self, source, target, at):
        core = lax.axis_index("tp")
        start = pl.multiple_of((core if at == 0 else 1 - core) * self.rows, self.rows)
        return source.at[pl.ds(start, self.rows)], target.at[pl.ds(at * self.rows, self.rows)]


class LateBoth(BothRows):
    def __init__(self, array, rows):
        super().__init__(array, rows)
        self.late = True


def call(body, name, lengths, ins, outs, scratch=(), vmem=64, after=(), joins=(), early=None, cost=1):
    ins = [item if isinstance(item, Whole) else Whole(item) for item in ins]
    n_in, n_out, n_after, n_join = len(ins), len(outs), len(after), len(joins)
    joined = [shape((2 * own.shape[0],) + own.shape[1:], own.dtype) for own, _ in joins]

    def kernel(lengths_ref, *refs):
        in_refs, refs = refs[:n_in], refs[n_in + n_after :]
        pair_refs, refs = refs[: 2 * n_join], refs[2 * n_join :]
        out_refs, refs = refs[:n_out], refs[n_out:]
        join_refs, refs = refs[:n_join], refs[n_join:]
        in_bufs, refs = refs[:n_in], refs[n_in:]
        out_bufs, refs = refs[:n_out], refs[n_out:]
        join_bufs, refs = refs[:n_join], refs[n_join:]
        in_sems, out_sems, join_sems, refs = refs[0], refs[1], refs[2], refs[3:]
        core = lax.axis_index("tp")
        copies = []
        for at in range(n_join):
            for side in range(2):
                source = pair_refs[2 * at + side]
                rows = source.shape[0]
                start = pl.multiple_of((core if side == 0 else 1 - core) * rows, rows)
                copies.append(
                    pltpu.make_async_copy(
                        source, join_bufs[at].at[pl.ds(start, rows)], join_sems.at[2 * at + side]
                    )
                )
        loads, first = [], 0
        for item, source, buffer in zip(ins, in_refs, in_bufs):
            loads.append(Load(source, buffer, in_sems, first, item))
            first += item.parts
        for late in (False, True):
            if late and early is not None:
                early(lengths_ref, loads)
            for at in range(max(item.parts for item in ins) if ins else 0):
                for load in loads:
                    if load.item.late == late and at < len(load.copies):
                        load.copies[at].start()
        stores = [
            Store(out_refs[at], out_bufs[at], out_sems, at * PARTS) for at in range(n_out)
        ]
        for copy in copies:
            copy.start()
        started = []

        def join():
            for copy in copies:
                copy.wait()
            for at in range(n_join):
                started.append(
                    pltpu.make_async_copy(join_bufs[at], join_refs[at], join_sems.at[2 * at])
                )
                started[-1].start()
            copies.clear()

        body(lengths_ref, loads, stores, (*refs, join))
        if copies:
            join()
        for store in stores:
            if not store.copies and not store.manual:
                store.send()
        for load in loads:
            load.ref()
        for store in stores:
            store.finish()
        for copy in started:
            copy.wait()

    return pl.pallas_call(
        kernel,
        name=name,
        out_shape=[*outs, *joined],
        in_specs=[pl.BlockSpec(memory_space=pltpu.SMEM)]
        + [pl.BlockSpec(memory_space=pl.ANY)] * (n_in + n_after + 2 * n_join),
        out_specs=[pl.BlockSpec(memory_space=pl.ANY)] * (n_out + n_join),
        scratch_shapes=[pltpu.VMEM(item.dims, item.array.dtype) for item in ins]
        + [pltpu.VMEM(out.shape, out.dtype) for out in [*outs, *joined]]
        + [
            pltpu.SemaphoreType.DMA((sum(item.parts for item in ins) + 1,)),
            pltpu.SemaphoreType.DMA((max(n_out, 1) * PARTS,)),
            pltpu.SemaphoreType.DMA((max(2 * n_join, 1),)),
        ]
        + list(scratch),
        compiler_params=pltpu.CompilerParams(vmem_limit_bytes=vmem * 2**20),
        cost_estimate=pl.CostEstimate(flops=cost, bytes_accessed=1, transcendentals=0),
    )(lengths, *(item.array for item in ins), *after, *(item for pair in joins for item in pair))


def line(load):
    ref = load.ref()
    return ref[...].astype(F32).reshape(1, ref.shape[0])


def length_of(lengths, at):
    core = lax.axis_index("tp")
    return lengths[core if at == 0 else 1 - core]


def places(order, partner=False):
    if not SWAP[0]:
        return list(range(GROUPS))
    place, core = lax.axis_index("dp"), lax.axis_index("tp")
    found = []
    for group in range(GROUPS):
        rel = jnp.bitwise_xor(place, group)
        bits = [rel % 2, (rel // 2) % 2, (rel // 4) % 2, rel // 8]
        near = jnp.where(core == (1 if partner else 0), bits[0], bits[1])
        bits[:2] = near, bits[0] + bits[1] - near
        found.append(sum(bit * (8 // 2**step) for bit, step in zip(bits, order)))
    return found


PLANE_FIRST = (0, 1, 2, 3)
Z_BETWEEN = (0, 2, 1, 3)


Z_FIRST = (1, 2, 0, 3)


def by_length(lengths, at, length, run):
    count = length_of(lengths, at)
    sizes = [size for size in (128, 256) if size < length] + [length]
    below = None
    for size in sizes:
        fits = count <= size
        if below is not None:
            fits = fits & (count > below)

        @pl.when(fits)
        def _(size=size):
            run(size)

        below = size


def shape(dims, dtype=BF16):
    return jax.ShapeDtypeStruct(dims, dtype)


def put_groups(target, place, values, columns):
    size = values.shape[0] // GROUPS
    for group in range(GROUPS):
        start = place[group] * size
        if not isinstance(start, int):
            start = pl.multiple_of(start, size)
        target[pl.ds(start, size), columns] = values[group * size : (group + 1) * size].astype(BF16)


def attend(lengths, tokens, w_query, w_key, w_value, bias_query, bias_value, length):
    width = w_query.shape[1]
    heads = width // HEAD

    def body(lengths, loads, stores, scratch):
        rows, wk, wq, wv, bq, bv = loads
        q_out, k_out, v_out, e_out, own_out, other_out, inv_out = stores
        (v_turned,) = scratch[:1]
        e_out.manual = True
        bq, bv = line(bq), line(bv)

        def lanes(head):
            return slice(head // 2 * PAIR, (head // 2 + 1) * PAIR)

        def sequence(at, size):
            near = slice(at * length, at * length + size)
            lane = lax.broadcasted_iota(jnp.int32, (size, PAIR), 1)
            row = lax.broadcasted_iota(jnp.int32, (size, PAIR), 0)
            count = length_of(lengths, at)
            masked = jnp.where((lane == 0) & (row >= count), -1e30, 0.0).astype(BF16)
            marker = jnp.where(lane == 0, 1.0, 0.0).astype(BF16)
            ones = jnp.ones((16, size), BF16)
            att_out = (own_out, other_out)[at]

            def scores(head):
                queries = q_out.ref[near, lanes(head)]
                own = jnp.where(lane // HEAD == head % 2, queries, jnp.zeros_like(queries))
                keys = jnp.concatenate([k_out.ref[near, lanes(head)], masked], axis=1)
                return nt(keys, jnp.concatenate([own, marker], axis=1))

            mixed, inverse = [], []

            def mix(head):
                values = v_turned[at, head * HEAD : (head + 1) * HEAD, :size]
                left = jnp.concatenate([values, ones], axis=0)
                sums = nn(left, e_out.ref[at * heads + head, :size, :size])
                inv = 1.0 / sums[HEAD : HEAD + 1]
                mixed.append(sums[:HEAD] * inv)
                inverse.append(jnp.broadcast_to(inv, (HEAD, size)))
                if head % 2:
                    att_out.ref[:size, lanes(head)] = (
                        jnp.concatenate(mixed, axis=0).astype(BF16).T
                    )
                    inv_out.ref[near, lanes(head)] = jnp.concatenate(inverse, axis=0).T
                    mixed.clear()
                    inverse.clear()

            now = scores(0)
            for head in range(heads):
                later = scores(head + 1) if head + 1 < heads else None
                top = jnp.max(now, axis=0, keepdims=True)
                e_out.ref[at * heads + head, :size, :size] = jnp.exp(now - top).astype(BF16)
                if head:
                    mix(head - 1)
                now = later
            mix(heads - 1)
            if size < length:
                att_out.ref[size:] = jnp.zeros((length - size, width), BF16)
            square(at, size).start()

        def square(at, size):
            cut = (pl.ds(at * heads, heads), pl.ds(0, size), pl.ds(0, size))
            return pltpu.make_async_copy(
                e_out.ref.at[cut], e_out.target.at[cut], e_out.sems.at[e_out.next + at]
            )

        for at in range(2):
            x = rows.part(at)
            near = slice(at * length, (at + 1) * length)
            k_out.ref[near] = nn(x[near], wk.ref()[...]).astype(BF16)
            q_out.ref[near] = (
                (nn(x[near], wq.ref()[...]) + bq).astype(BF16).astype(F32) * HEAD**-0.5
            ).astype(BF16)
            value = (nn(x[near], wv.ref()[...]) + bv).astype(BF16)
            v_out.ref[near] = value
            v_turned[at] = value.T
            by_length(lengths, at, length, lambda size: sequence(at, size))
            for out in (q_out, k_out, v_out, inv_out):
                out.send(pl.ds(at * length, length))
            (own_out, other_out)[at].send()
        for at in range(2):
            by_length(lengths, at, length, lambda size: square(at, size).wait())

    both = 2 * length
    return call(
        body,
        "attend",
        lengths,
        [BothRows(tokens, length), w_key, w_query, w_value, bias_query, bias_value],
        [
            shape((both, width)),
            shape((both, width)),
            shape((both, width)),
            shape((2 * heads, length, length)),
            shape((length, width)),
            shape((length, width)),
            shape((both, width), F32),
        ],
        scratch=[pltpu.VMEM((2, width, length), BF16)],
    )


def up_half(low, wu, bu, wd, act, slope, total, fresh):
    inner = act.shape[1]

    def project(start):
        return nn(low[...], wu[:, start : start + HIDDEN]) + bu[:, start : start + HIDDEN]

    now = project(0)
    for start in range(0, inner, HIDDEN):
        cut = slice(start, start + HIDDEN)
        later = project(start + HIDDEN) if start + HIDDEN < inner else None
        phi = 0.5 * (1.0 + lax.erf(now * (0.5**0.5)))
        act[:, cut] = (now * phi).astype(BF16)
        slope[:, cut] = (
            phi + now * (jnp.exp(-0.5 * now * now) * 0.3989422804014327)
        ).astype(BF16)
        part = nn(act[:, cut], wd[cut, :])
        if fresh and start == 0:
            total[...] = part
        else:
            total[...] += part
        now = later


def feed(lengths, tokens, out_grad, att, w_out, vectors, bias_up, w_up, w_down, length):
    model = tokens.shape[1]
    inner = w_up[0].shape[1]

    def body(lengths, loads, stores, scratch):
        att_a, wo_a, att_b, wo_b, rows, bo, g1, s1 = loads[:8]
        wu_a, bu_a, wd_a, wu_b, bu_b, wd_b, cot, bd, g2, s2 = loads[8:]
        first_out, layer_out, small, down_a, up_a, *halves = stores
        total, hidden, low, norm, spr, grad_low = scratch[:6]
        act_a, act_b, slope_a, slope_b, bias_a, bias_b, down_b, up_b = scratch[6:14]
        total[...] = nn(att_a.ref()[...], wo_a.ref()[...]) + nn(att_b.ref()[...], wo_b.ref()[...])
        x = rows.ref()
        bo, g1, s1 = line(bo), line(g1), line(s1)
        for start in range(0, length, ROWS):
            cut = slice(start, start + ROWS)
            value = x[cut].astype(F32) + (total[cut] + bo)
            centred = value - mean(value)
            spread = lax.rsqrt(mean(centred * centred) + EPS)
            normed = centred * spread
            norm[cut] = normed.astype(BF16)
            spr[cut] = jnp.broadcast_to(spread, (ROWS, 128))
            full = normed * g1 + s1
            hidden[cut] = full
            low[cut] = full.astype(BF16)
        for load in loads[:11]:
            load.ref()
        up_half(low, wu_a.ref(), line(bu_a), wd_a.ref(), act_a, slope_a, total, True)
        for load in loads:
            load.ref()
        up_half(low, wu_b.ref(), line(bu_b), wd_b.ref(), act_b, slope_b, total, False)
        cot = cot.ref()
        bd, g2, s2 = line(bd), line(g2), line(s2)
        sums = [jnp.zeros((1, model), F32)] * 6
        for start in range(0, length, ROWS):
            cut = slice(start, start + ROWS)
            row = lax.broadcasted_iota(jnp.int32, (ROWS, model), 0) + start
            valid = jnp.where(row < length_of(lengths, 0), 1.0, 0.0)
            value = hidden[cut] + total[cut] + bd
            centred = value - mean(value)
            spread = lax.rsqrt(mean(centred * centred) + EPS)
            normed = centred * spread
            layer_out.ref[cut] = ((normed * g2 + s2) * valid).astype(BF16)
            grad = cot[cut].astype(F32) * valid
            scaled = grad * g2
            resid = spread * (scaled - mean(scaled) - normed * mean(scaled * normed))
            sums[0] += column_sum(grad * normed)
            sums[1] += column_sum(grad)
            sums[2] += column_sum(resid)
            grad_low[cut] = resid.astype(BF16)
        layer_out.send()
        slope_back(grad_low, wd_b.ref(), slope_b, bias_b)
        slope_back(grad_low, wd_a.ref(), slope_a, bias_a)
        total[...] = nt(slope_a[...], wu_a.ref()[...]) + nt(slope_b[...], wu_b.ref()[...])
        for start in range(0, length, ROWS):
            cut = slice(start, start + ROWS)
            value = grad_low[cut].astype(F32) + total[cut]
            normed = norm[cut].astype(F32)
            scaled = value * g1
            first = spr[cut, 0:1] * (scaled - mean(scaled) - normed * mean(scaled * normed))
            sums[3] += column_sum(value * normed)
            sums[4] += column_sum(value)
            sums[5] += column_sum(first)
            first_out.ref[cut] = first.astype(BF16)
        first_out.send()
        for at in range(3):
            small.ref[at : at + 1, :model] = sums[2 * at]
            small.ref[at : at + 1, model:] = sums[2 * at + 1]
        small.ref[3:4] = bias_a[0:1]
        small.ref[4:5] = bias_b[0:1]
        small.ref[5:8] = jnp.zeros((3, inner), F32)
        small.send()
        weight_halves(*halves[:2], down_b, grad_low, act_b, places(PLANE_FIRST, True))
        weight_halves(*halves[2:], up_b, low, slope_b, places(PLANE_FIRST, True))
        weight(down_a, grad_low, act_a, places(PLANE_FIRST))
        weight(up_a, low, slope_a, places(PLANE_FIRST))

    whole = shape((model, inner))
    half = pltpu.VMEM((length, inner), BF16)
    return call(
        body,
        "feed",
        lengths,
        [att[0], w_out[0], att[1], w_out[1], OwnRows(tokens, length), *vectors[:3]]
        + [w_up[0], bias_up[0], w_down[0], w_up[1], bias_up[1], w_down[1]]
        + [OwnRows(out_grad, length), *vectors[3:]],
        [shape((length, model)), shape((length, model)), shape((8, inner), F32), whole, whole]
        + [shape((model // 2, inner))] * 4,
        scratch=[
            pltpu.VMEM((length, model), F32),
            pltpu.VMEM((length, model), F32),
            pltpu.VMEM((length, model), BF16),
            pltpu.VMEM((length, model), BF16),
            pltpu.VMEM((length, 128), F32),
            pltpu.VMEM((length, model), BF16),
            half,
            half,
            half,
            half,
            pltpu.VMEM((8, inner), F32),
            pltpu.VMEM((8, inner), F32),
            pltpu.VMEM((model, inner), BF16),
            pltpu.VMEM((model, inner), BF16),
        ],
    )


SWAP = [True]


def weight(out, left, right, place):
    columns = right.shape[1]
    for start in range(0, columns, HIDDEN):
        cut = pl.ds(start, HIDDEN)
        put_groups(out.ref, place, tn(left[...], right[:, start : start + HIDDEN]), cut)
        out.send(slice(None), cut)


def weight_halves(keep, send, buffer, left, right, place):
    columns = right.shape[1]
    rows = buffer.shape[0] // 2
    keep.ref, send.ref = buffer.at[pl.ds(0, rows)], buffer.at[pl.ds(rows, rows)]
    for start in range(0, columns, HIDDEN):
        cut = pl.ds(start, HIDDEN)
        put_groups(buffer, place, tn(left[...], right[:, start : start + HIDDEN]), cut)
        for out in (send, keep):
            out.send(slice(None), cut)


def slope_back(grad, wd, slope, bias):
    inner = slope.shape[1]

    def project(start):
        return nt(grad[...], wd[start : start + HIDDEN, :])

    now = project(0)
    for start in range(0, inner, HIDDEN):
        cut = slice(start, start + HIDDEN)
        later = project(start + HIDDEN) if start + HIDDEN < inner else None
        value = (now * slope[:, cut].astype(F32)).astype(BF16)
        slope[:, cut] = value
        bias[:, cut] = jnp.broadcast_to(column_sum(value.astype(F32)), (8, HIDDEN))
        now = later


def attend_back(
    lengths, low, tokens, w_out, saved, length, after=()
):
    query, keyed, valued, expo, att_own, att_other, inv = saved
    width, model = w_out.shape
    heads = width // HEAD
    both = 2 * length

    def square(e, at, size):
        cut = (pl.ds(at * heads, heads), pl.ds(0, size), pl.ds(0, size))
        return pltpu.make_async_copy(e.source.at[cut], e.target.at[cut], e.sems.at[e.first + at])

    def early(lengths, loads):
        for at in range(2):
            by_length(lengths, at, length, lambda size: square(loads[6], at, size).start())

    def body(lengths, loads, stores, scratch):
        grad_a, wo, k, v, inverse, att_a, e, q, grad_b, att_b = loads[:10]
        rows = loads[10]
        grads, small, *halves = stores
        dq, dk, dv = (grads.ref.at[:, pl.ds(at * width, width)] for at in range(3))
        mixed, k_turned, kept, first_p, first_q = scratch[:5]
        wo = wo.ref()
        atts = (att_a, att_b)

        def lanes(head):
            return slice(head // 2 * PAIR, (head // 2 + 1) * PAIR)

        def sequence(at, size):
            near = slice(at * length, at * length + size)
            lane = lax.broadcasted_iota(jnp.int32, (size, PAIR), 1)
            marker = jnp.where(lane < 2, 1.0, 0.0).astype(BF16)
            scaled_of, product_of = {}, {}

            def scores(head):
                cut, mine = lanes(head), lane // HEAD == head % 2
                if head % 2 == 0:
                    scaled = mixed[:size, cut].astype(F32) * inverse.target[near, cut]
                    product_of[head // 2] = scaled * atts[at].target[:size, cut].astype(F32)
                    scaled_of[head // 2] = scaled.astype(BF16)
                scaled, product = scaled_of[head // 2], product_of[head // 2]
                inner = -jnp.sum(jnp.where(mine, product, 0.0), axis=1, keepdims=True)
                high = inner.astype(BF16).astype(F32)
                extra = jnp.where(lane == 0, high, jnp.where(lane == 1, inner - high, 0.0))
                right = jnp.concatenate(
                    [jnp.where(mine, scaled, jnp.zeros_like(scaled)), extra.astype(BF16)], axis=1
                )
                return nt(jnp.concatenate([v.target[near, cut], marker], axis=1), right)

            dvs, dks, dqs = [], [], []

            def products(head):
                cut = lanes(head)
                grads = kept[head % 2, :size, :size]
                dks.append(nn(grads, q.target[near, cut]))
                dqs.append(nn(k_turned[head * HEAD : (head + 1) * HEAD, :size], grads))
                if head % 2:
                    dk[near, cut] = jnp.where(lane < HEAD, dks[0], dks[1]).astype(BF16)
                    dq[near, cut] = (jnp.concatenate(dqs, axis=0) * HEAD**-0.5).astype(BF16).T
                    dks.clear()
                    dqs.clear()

            square(e, at, size).wait()
            now = scores(0)
            for head in range(heads):
                later = scores(head + 1) if head + 1 < heads else None
                expo = e.target[at * heads + head, :size, :size]
                kept[head % 2, :size, :size] = (expo.astype(F32) * now).astype(BF16)
                dvs.append(nn(expo, scaled_of[head // 2]))
                if head % 2:
                    dv[near, lanes(head)] = jnp.where(lane < HEAD, dvs[0], dvs[1]).astype(BF16)
                    dvs.clear()
                if head:
                    products(head - 1)
                now = later
            products(heads - 1)
            if size < length:
                rest = slice(at * length + size, (at + 1) * length)
                grads.ref[rest] = jnp.zeros((length - size, 3 * width), BF16)

        for at, grad in enumerate((grad_a, grad_b)):
            near = slice(at * length, (at + 1) * length)
            mixed[...] = nt(grad.ref()[...], wo[...]).astype(BF16)
            k_turned[...] = k.part(at)[near].T
            for load in (inverse, v, q):
                load.part(at)
            atts[at].ref()
            by_length(lengths, at, length, lambda size: sequence(at, size))
            grads.send(pl.ds(at * length, length))
        sums = [column_sum(out[...].astype(F32)) for out in (dq, dv)]
        sums = jnp.concatenate(sums, axis=1)
        high = sums.astype(BF16).astype(F32)
        low = (sums - high).astype(BF16).astype(F32)
        first = lax.broadcasted_iota(jnp.int32, (8, 2 * width), 0) == 0
        small.ref[...] = jnp.where(first, high + low, 0.0)
        small.send()
        first_p[pl.ds(model, 2 * SMALL)] = jnp.concatenate(
            [jnp.where(first, high, 0.0), jnp.where(first, low, 0.0)], axis=0
        ).astype(BF16)
        x = rows.ref()
        for source, order, (keep, send), parts in (
            (first_p, Z_BETWEEN, halves[:2], (dq, dk)),
            (first_q, Z_FIRST, halves[2:], (dv, None)),
        ):
            place = places(order)
            for at, part in enumerate(parts):
                if part is None:
                    product = tn(grad_a.target[...], att_a.target[...])
                    product += tn(grad_b.target[...], att_b.target[...])
                else:
                    product = tn(x[...], part[...])
                put_groups(source, place, product, pl.ds(at * width, width))
            for out, start in ((send, model // 2), (keep, 0)):
                out.ref = source.at[pl.ds(start, out.target.shape[0])]
                out.send()

    half = shape((model // 2, 2 * width))
    return call(
        body,
        "attend_back",
        lengths,
        [low[0], w_out, *(Whole(item, 2, 0) for item in (keyed, valued, inv)), att_own]
        + [Manual(expo, 2, 0), Whole(query, 2, 0)]
        + [Whole(low[1], late=True), Whole(att_other, late=True), LateBoth(tokens, length)],
        [shape((both, 3 * width)), shape((8, 2 * width), F32), half, shape((model // 2 + 16, 2 * width))]
        + [half, half],
        scratch=[
            pltpu.VMEM((length, width), BF16),
            pltpu.VMEM((width, length), BF16),
            pltpu.VMEM((2, length, length), BF16),
            pltpu.VMEM((model + 2 * SMALL, 2 * width), BF16),
            pltpu.VMEM((model, 2 * width), BF16),
        ],
        after=after,
        early=early,
    )


def input_part(lengths, first, grads, weights, joins, length, after=()):
    model, width = weights[0].shape

    def body(lengths, loads, stores, scratch):
        side = scratch[0]
        copies = [
            pltpu.make_async_copy(
                load.source, side.at[:, pl.ds(at * width, width)], load.sems.at[load.first]
            )
            for at, load in enumerate(loads[1:4])
        ]
        for copy in copies:
            copy.start()
        for copy in copies:
            copy.wait()
        scratch[-1]()
        for at in (1, 0):
            near = slice(at * length, (at + 1) * length)
            total = nt(loads[0].part(at)[near], side[...])
            if not at:
                total += loads[4].ref()[...].astype(F32)
            stores[at].ref[...] = total.astype(BF16)
            stores[at].send()

    return call(
        body,
        "input_part",
        lengths,
        [Whole(grads, 2, 0), *(Manual(item) for item in weights), Whole(first, late=True)],
        [shape((length, model))] * 2,
        scratch=[pltpu.VMEM((model, 3 * width), BF16)],
        after=after,
        joins=joins,
    )


def swap(values):
    return lax.ppermute(values, "tp", [(0, 1), (1, 0)])


def together(*values):
    return lax.optimization_barrier(values)


def flip(values, bits):
    size = lax.axis_size("dp")
    perm = [(2 * d + c, 2 * (d ^ bits[c]) + c) for d in range(size) for c in range(2)]
    return lax.ppermute(values, ("dp", "tp"), perm)


NEAR, FAR, LOW, HIGH = (1, 2), (2, 1), (4, 4), (8, 8)


def add(left, right):
    return left.astype(F32) + right.astype(F32)


def total(parts):
    parts = [part.astype(F32) for part in parts]
    while len(parts) > 1:
        parts = [sum(parts[at + 1 : at + 2], parts[at]) for at in range(0, len(parts), 2)]
    return parts[0]


SMALL = 8


def split(values):
    high = values.astype(BF16).astype(F32)
    return high, (values - high).astype(BF16).astype(F32)


def small_sum(own, came):
    high, low = split(own)
    came = came.astype(F32)
    return (high + low) + (came[:SMALL] + came[SMALL:])


def put_small(message, at, values):
    message[at : at + 2 * SMALL] = jnp.concatenate(split(values), axis=0).astype(BF16)


BRIEF, LONG = 2 * 10**9, 2 * 10**10


def merge(body, name, ins, outs, after=()):
    n_in = len(ins)

    def kernel(*refs):
        body(refs[:n_in], refs[n_in + len(after) :])

    return pl.pallas_call(
        kernel,
        name=name,
        out_shape=outs,
        in_specs=[pl.BlockSpec(memory_space=pltpu.VMEM)] * n_in
        + [pl.BlockSpec(memory_space=pl.ANY)] * len(after),
        out_specs=[pl.BlockSpec(memory_space=pltpu.VMEM)] * len(outs),
        compiler_params=pltpu.CompilerParams(vmem_limit_bytes=16 * 2**20),
        cost_estimate=pl.CostEstimate(flops=BRIEF, bytes_accessed=1, transcendentals=0),
    )(*ins, *after)


def exchange(name, jobs, small, after=()):
    rows = [keep.shape[0] // 2 for keep, _, _ in jobs]
    columns = min(keep.shape[1] for keep, _, _ in jobs)
    ins = []
    for keep, came, _ in jobs:
        ins += [keep, came]
    if small is not None:
        ins += [small[0], small[1]]

    def body(ins, outs):
        message = outs[-1]
        at = 0
        for job, (_, _, start) in enumerate(jobs):
            keep, came = ins[2 * job], ins[2 * job + 1]
            count = rows[job]
            sent = add(keep[count:], came[start + count : start + 2 * count])
            for column in range(0, keep.shape[1], columns):
                message[at : at + count] = sent[:, column : column + columns].astype(BF16)
                at += count
            outs[job][...] = add(keep[:count], came[start : start + count])
        if small is not None:
            values = small_sum(ins[-2][...], ins[-1][small[2] : small[2] + 2 * SMALL])
            outs[-2][...] = values
            put_small(message, at, values)

    wide = [keep.shape[1] for keep, _, _ in jobs]
    outs = [shape((count, width), F32) for count, width in zip(rows, wide)]
    height = sum(count * (width // columns) for count, width in zip(rows, wide))
    if small is not None:
        outs.append(shape(small[0].shape, F32))
        height += 2 * SMALL
    outs.append(shape((height, columns)))
    return merge(body, name, ins, outs, after)


def first_near(lengths, own, came, small=None, after=()):
    rows, columns = own.shape[0] // 2, own.shape[1]
    parts = 4
    size = rows // parts

    def body(lengths, loads, stores, scratch):
        out = stores[0]
        if small is not None:
            put_small(out.ref, rows, loads[2].ref()[...])
            out.send(pl.ds(rows, 2 * SMALL))
        for at in range(parts):
            cut = slice(at * size, (at + 1) * size)
            out.ref[cut] = add(loads[0].part(at)[cut], loads[1].part(at)[cut]).astype(BF16)
            out.send(pl.ds(at * size, size))

    ins = [Rows(own, rows, rows, parts), Rows(came, 0, rows, parts)]
    if small is not None:
        ins.append(small)
    rows_out = rows if small is None else rows + 2 * SMALL
    return call(body, "first_near", lengths, ins, [shape((rows_out, columns))], after=after, cost=LONG)[0]


def kept_rows(own, came, near_came):
    rows = own.shape[0] // 2
    return [Rows(item, 0, rows, 4, True) for item in (own, came, near_came)]


def kept_sums(loads, stay, go):
    rows = loads[0].target.shape[0]
    size = rows // 4
    for at in range(4):
        start = (3 - at) * size
        cut = slice(start, start + size)
        own, came, near_came = (load.part(at)[cut] for load in loads)
        values = (add(own, came) + near_came.astype(F32)).astype(BF16)
        out, to = (go, start - rows // 2) if start >= rows // 2 else (stay, start)
        out.ref[to : to + size] = values
        out.send(pl.ds(to, size))


def second(lengths, name, own, came, near_came, small=None, after=()):
    rows, columns = own.shape[0] // 4, own.shape[1]

    def body(lengths, loads, stores, scratch):
        message, stay = stores[:2]
        if small is not None:
            values = small_sum(loads[-2].ref()[...], loads[-1].ref()[...])
            put_small(message.ref, rows, values)
            message.send(pl.ds(rows, 2 * SMALL))
            stores[2].ref[...] = values
            stores[2].send()
        kept_sums(loads[:3], stay, message)

    ins = kept_rows(own, came, near_came)
    outs = [shape((rows + (2 * SMALL if small is not None else 0), columns)), shape((rows, columns))]
    if small is not None:
        ins += [small, Rows(near_came, 2 * rows, 2 * SMALL)]
        outs.append(shape(small.shape, F32))
    return call(body, name, lengths, ins, outs, after=after, cost=BRIEF)


def onward(name, jobs, small, after=()):
    rows = [keep.shape[0] // 2 for keep, _, _ in jobs]
    columns = jobs[0][0].shape[1]
    height = sum(rows)
    ins = []
    for keep, came, _ in jobs:
        ins += [keep, came]
    if small is not None:
        ins += small[:2]

    def body(ins, outs):
        message = outs[0]
        at = 0
        for job, (count, (_, _, start)) in enumerate(zip(rows, jobs)):
            keep, came = ins[2 * job], ins[2 * job + 1]
            sent = add(keep[count:], came[start + count : start + 2 * count])
            message[at : at + count] = sent.astype(BF16)
            outs[1 + job][...] = add(keep[:count], came[start : start + count]).astype(BF16)
            at += count
        if small is not None:
            values = small_sum(ins[-2][...], ins[-1][small[2] : small[2] + 2 * SMALL])
            outs[-1][...] = values
            put_small(message, at, values)

    outs = [shape((height + (2 * SMALL if small is not None else 0), columns))]
    outs += [shape((count, columns)) for count in rows]
    if small is not None:
        outs.append(shape(small[0].shape, F32))
    return merge(body, name, ins, outs, after)


def last_up(up, small, came):
    rows = up.shape[0]

    def body(ins, outs):
        up, small, came = ins
        outs[0][...] = add(up[...], came[:rows])
        outs[1][...] = small_sum(small[...], came[rows:])

    return merge(
        body, "last_up", [up, small, came], [shape(up.shape, F32), shape(small.shape, F32)]
    )


def last_heads(left, right, small, came):
    rows, columns = left.shape
    width = columns // 2

    def body(ins, outs):
        left, right, small, came = ins
        values = add(left[...], came[:rows])
        outs[0][...] = values[:, :width]
        outs[1][...] = values[:, width:]
        values = add(right[...], came[rows : 2 * rows])
        outs[2][...] = values[:, :width]
        outs[3][...] = values[:, width:]
        outs[4][...] = small_sum(small[...], came[2 * rows :])

    one = shape((rows, width), F32)
    return merge(
        body,
        "last_heads",
        [left, right, small, came],
        [one, one, one, one, shape(small.shape, F32)],
    )


def scatter(whole):
    return lax.psum_scatter(whole, "dp", scatter_dimension=0, tiled=True)


def local(
    tokens,
    seq_lengths,
    out_grad,
    w_query,
    bias_query,
    w_key,
    w_value,
    bias_value,
    w_out,
    bias_out,
    gain_one,
    shift_one,
    w_up,
    bias_up,
    w_down,
    bias_down,
    gain_two,
    shift_two,
):
    near = lax.axis_size("dp") == GROUPS
    SWAP[0] = near
    lengths = seq_lengths
    model = tokens.shape[1]
    length = tokens.shape[0] // seq_lengths.shape[0]
    width = w_query.shape[1]
    inner = w_up.shape[1]

    wo_b, wu_b, wd_b, bu_b = swap(w_out), swap(w_up), swap(w_down), swap(bias_up)
    query, keyed, valued, expo, att_own, att_other, inv = attend(
        lengths, tokens, w_query, w_key, w_value, bias_query, bias_value, length
    )
    first_low, layer_own, small, down_a, up_a, *halves = feed(
        lengths,
        tokens,
        out_grad,
        (att_own, swap(att_other)),
        (w_out, wo_b),
        (bias_out, gain_one, shift_one, bias_down, gain_two, shift_two),
        (bias_up, bu_b),
        (w_up, wu_b),
        (w_down, wd_b),
        length,
    )
    first_came = swap(first_low)
    down_kept, down_gone, up_kept, up_gone = (swap(half) for half in halves)
    layer_other = swap(layer_own)
    if near:
        down_sent = first_near(lengths, down_a, down_gone, after=[first_came])
        near_down = flip(down_sent, NEAR)
    after = []
    if near:
        up_sent = first_near(lengths, up_a, up_gone, small, [down_sent])
        near_up = flip(up_sent, NEAR)
        after = [up_sent]
    grads, small_heads, keep_p, send_p, keep_q, send_q = attend_back(
        lengths,
        (first_low, first_came),
        tokens,
        w_out,
        (query, keyed, valued, expo, att_own, att_other, inv),
        length,
        after,
    )
    after = []
    if near:
        came_p, came_q = flip(send_p, NEAR), flip(send_q, LOW)
        sent, down = second(
            lengths, "down_far", down_a, down_kept, near_down, after=[keep_p]
        )
        far_down = flip(sent, FAR)
        sent, up, small = second(
            lengths, "up_far", up_a, up_kept, near_up, small, [sent]
        )
        far_up = flip(sent, FAR)
        after = [sent]
    input_own, input_other, layer_output = input_part(
        lengths,
        first_low,
        grads,
        (w_query, w_key, w_value),
        [(layer_own, layer_other)],
        length,
        after,
    )
    input_other = swap(input_other)
    if near:
        came_p = together(came_p, input_own)[0]
        sent, heads_p, small_heads = onward(
            "heads_low",
            [(keep_p, came_p, 0)],
            (small_heads, came_p, model // 2),
        )
        low_p = flip(sent, LOW)
        sent, heads_q = onward("heads_near", [(keep_q, came_q, 0)], None, [sent])
        near_q = flip(sent, NEAR)
        sent, down = onward("down_low", [(down, far_down, 0)], None, [sent])
        low_down = flip(sent, LOW)
        sent, up, small = onward(
            "up_low", [(up, far_up, 0)], (small, far_up, up.shape[0]), [sent]
        )
        low_up = flip(sent, LOW)
        sent, heads_p, heads_q, small_heads = onward(
            "heads_far",
            [(heads_p, low_p, 0), (heads_q, near_q, 0)],
            (small_heads, low_p, heads_p.shape[0]),
            [sent],
        )
        far_heads = flip(sent, FAR)
        sent, down = onward("down_high", [(down, low_down, 0)], None, [sent])
        high_down = flip(sent, HIGH)
        input_other = together(input_other, sent)[0]
    input_own = (input_own.astype(F32) + input_other.astype(F32)).astype(BF16)
    (input_grad,) = call(
        lambda *_: None, "join", lengths, [], [], vmem=16, joins=[(input_own, swap(input_own))]
    )
    if near:
        rows = heads_p.shape[0]
        sent, heads_p, heads_q, small_heads = onward(
            "heads_high",
            [(heads_p, far_heads, 0), (heads_q, far_heads, rows)],
            (small_heads, far_heads, 2 * rows),
            [input_own],
        )
        high_heads = flip(sent, HIGH)
        sent, up, small = onward(
            "up_high", [(up, low_up, 0)], (small, low_up, up.shape[0]), [sent]
        )
        high_up = flip(sent, HIGH)
        grad_down = add(down, high_down)
        high_up = together(high_up, input_grad)[0]
        grad_up, small = last_up(up, small, high_up)
        high_heads = together(high_heads, input_grad)[0]
        grad_query, grad_key, grad_value, grad_out, small_heads = last_heads(
            heads_p, heads_q, small_heads, high_heads
        )
    else:
        grad_down = scatter(total([down_a, jnp.concatenate([down_kept, down_gone], axis=0)]))
        grad_up = scatter(total([up_a, jnp.concatenate([up_kept, up_gone], axis=0)]))
        heads_p = scatter(jnp.concatenate([keep_p, send_p[: model // 2]], axis=0).astype(F32))
        heads_q = scatter(jnp.concatenate([keep_q, send_q], axis=0).astype(F32))
        small, small_heads = lax.psum((small, small_heads), "dp")
        grad_query, grad_key = heads_p[:, :width], heads_p[:, width:]
        grad_value, grad_out = heads_q[:, :width], heads_q[:, width:]
    small_other = together(swap(small), small_heads)[0]
    norms = (small[:3] + small_other[:3]).reshape(6, model)
    bias_up_grad = small[3] + small_other[4]
    bias_query_grad, bias_value_grad = small_heads[0, :width], small_heads[0, width:]
    gain_two_grad, shift_two_grad, bias_down_grad = norms[0], norms[1], norms[2]
    gain_one_grad, shift_one_grad, bias_out_grad = norms[3], norms[4], norms[5]
    return (
        layer_output,
        input_grad,
        grad_query,
        grad_key,
        grad_value,
        bias_query_grad,
        bias_value_grad,
        grad_out.T,
        bias_out_grad,
        gain_one_grad,
        shift_one_grad,
        grad_up,
        bias_up_grad,
        grad_down.T,
        bias_down_grad,
        gain_two_grad,
        shift_two_grad,
    )


def solution(mesh):
    return jax.shard_map(
        local,
        mesh=mesh,
        in_specs=(
            P("dp", None),
            P("dp"),
            P("dp", None),
            P(None, "tp"),
            P("tp"),
            P(None, "tp"),
            P(None, "tp"),
            P("tp"),
            P("tp", None),
            P(),
            P(),
            P(),
            P(None, "tp"),
            P("tp"),
            P("tp", None),
            P(),
            P(),
            P(),
        ),
        out_specs=(
            P("dp", None),
            P("dp", None),
            P("dp", "tp"),
            P("dp", "tp"),
            P("dp", "tp"),
            P("tp"),
            P("tp"),
            P("tp", "dp"),
            P(),
            P(),
            P(),
            P("dp", "tp"),
            P("tp"),
            P("tp", "dp"),
            P(),
            P(),
            P(),
        ),
        check_vma=False,
    )
```

```python
import jax
import jax.numpy as jnp
from jax import lax
from jax.experimental import pallas as pl
from jax.experimental.pallas import tpu as pltpu
from jax.sharding import PartitionSpec as P

HEAD = 64
PAIR = 128
EPS = 1e-05
GROUPS = 16
BF16 = jnp.bfloat16
F32 = jnp.float32
ROWS = 128
HIDDEN = 512


def nn(left, right):
    return lax.dot_general(left, right, (((1,), (0,)), ((), ())), preferred_element_type=F32)


def nt(left, right):
    return lax.dot_general(left, right, (((1,), (1,)), ((), ())), preferred_element_type=F32)


def tn(left, right):
    return lax.dot_general(left, right, (((0,), (0,)), ((), ())), preferred_element_type=F32)


def mean(values):
    return jnp.mean(values, axis=-1, keepdims=True)


def column_sum(values):
    return jnp.sum(values, axis=0, keepdims=True)


class Load:
    def __init__(self, source, target, sems, first, item):
        self.target, self.item = target, item
        self.source, self.sems, self.first = source, sems, first
        self.copies = []
        self.waited = set()
        if isinstance(item, Manual):
            return
        self.copies = [
            pltpu.make_async_copy(*item.ends(source, target, at), sems.at[first + at])
            for at in range(item.parts)
        ]

    def part(self, at):
        if at not in self.waited:
            self.copies[at].wait()
            self.waited.add(at)
        return self.target

    def columns(self, start, stop):
        if self.item.parts > 1:
            size = self.item.dims[self.item.axis] // self.item.parts
            for at in range(start // size, -(-stop // size)):
                self.part(at)
            return self.target
        return self.ref()

    def ref(self):
        for at in range(len(self.copies)):
            self.part(at)
        return self.target


class Store:
    def __init__(self, target, buffer, sems, first):
        self.target, self.ref, self.sems, self.next = target, buffer, sems, first
        self.copies = []
        self.manual = False

    def send(self, *index):
        source = self.ref.at[index] if index else self.ref
        target = self.target.at[index] if index else self.target
        copy = pltpu.make_async_copy(source, target, self.sems.at[self.next])
        copy.start()
        self.next += 1
        self.copies.append(copy)

    def finish(self):
        for copy in self.copies:
            copy.wait()


PARTS = 8


class Whole:
    def __init__(self, array, parts=1, axis=-1, late=False):
        self.array, self.dims = array, array.shape
        self.parts, self.axis, self.late = parts, axis % array.ndim, late

    def ends(self, source, target, at):
        if self.parts == 1:
            return source, target
        size = self.dims[self.axis] // self.parts
        cut = tuple(
            pl.ds(at * size, size) if axis == self.axis else pl.ds(0, dim)
            for axis, dim in enumerate(self.dims)
        )
        return source.at[cut], target.at[cut]


class Manual(Whole):
    pass


class OwnRows(Whole):
    def __init__(self, array, rows, late=False):
        super().__init__(array, late=late)
        self.dims = (rows,) + array.shape[1:]

    def ends(self, source, target, at):
        rows = self.dims[0]
        start = pl.multiple_of(lax.axis_index("tp") * rows, rows)
        return source.at[pl.ds(start, rows)], target


class Rows(Whole):
    def __init__(self, array, start, rows, parts=1, last=False):
        super().__init__(array, parts, 0)
        self.dims, self.start, self.last = (rows,) + array.shape[1:], start, last

    def ends(self, source, target, at):
        size = self.dims[0] // self.parts
        at = (self.parts - 1 - at if self.last else at) * size
        return source.at[pl.ds(self.start + at, size)], target.at[pl.ds(at, size)]


class BothRows(Whole):
    def __init__(self, array, rows):
        super().__init__(array, 2, 0)
        self.rows = rows

    def ends(self, source, target, at):
        core = lax.axis_index("tp")
        start = pl.multiple_of((core if at == 0 else 1 - core) * self.rows, self.rows)
        return source.at[pl.ds(start, self.rows)], target.at[pl.ds(at * self.rows, self.rows)]


class LateBoth(BothRows):
    def __init__(self, array, rows):
        super().__init__(array, rows)
        self.late = True


def call(body, name, lengths, ins, outs, scratch=(), vmem=64, after=(), joins=(), early=None, cost=1):
    ins = [item if isinstance(item, Whole) else Whole(item) for item in ins]
    n_in, n_out, n_after, n_join = len(ins), len(outs), len(after), len(joins)
    joined = [shape((2 * own.shape[0],) + own.shape[1:], own.dtype) for own, _ in joins]

    def kernel(lengths_ref, *refs):
        in_refs, refs = refs[:n_in], refs[n_in + n_after :]
        pair_refs, refs = refs[: 2 * n_join], refs[2 * n_join :]
        out_refs, refs = refs[:n_out], refs[n_out:]
        join_refs, refs = refs[:n_join], refs[n_join:]
        in_bufs, refs = refs[:n_in], refs[n_in:]
        out_bufs, refs = refs[:n_out], refs[n_out:]
        join_bufs, refs = refs[:n_join], refs[n_join:]
        in_sems, out_sems, join_sems, refs = refs[0], refs[1], refs[2], refs[3:]
        core = lax.axis_index("tp")
        copies = []
        for at in range(n_join):
            for side in range(2):
                source = pair_refs[2 * at + side]
                rows = source.shape[0]
                start = pl.multiple_of((core if side == 0 else 1 - core) * rows, rows)
                copies.append(
                    pltpu.make_async_copy(
                        source, join_bufs[at].at[pl.ds(start, rows)], join_sems.at[2 * at + side]
                    )
                )
        loads, first = [], 0
        for item, source, buffer in zip(ins, in_refs, in_bufs):
            loads.append(Load(source, buffer, in_sems, first, item))
            first += item.parts
        for late in (False, True):
            if late and early is not None:
                early(lengths_ref, loads)
            for at in range(max(item.parts for item in ins) if ins else 0):
                for load in loads:
                    if load.item.late == late and at < len(load.copies):
                        load.copies[at].start()
        stores = [
            Store(out_refs[at], out_bufs[at], out_sems, at * PARTS) for at in range(n_out)
        ]
        for copy in copies:
            copy.start()
        started = []

        def join():
            for copy in copies:
                copy.wait()
            for at in range(n_join):
                started.append(
                    pltpu.make_async_copy(join_bufs[at], join_refs[at], join_sems.at[2 * at])
                )
                started[-1].start()
            copies.clear()

        body(lengths_ref, loads, stores, (*refs, join))
        if copies:
            join()
        for store in stores:
            if not store.copies and not store.manual:
                store.send()
        for load in loads:
            load.ref()
        for store in stores:
            store.finish()
        for copy in started:
            copy.wait()

    return pl.pallas_call(
        kernel,
        name=name,
        out_shape=[*outs, *joined],
        in_specs=[pl.BlockSpec(memory_space=pltpu.SMEM)]
        + [pl.BlockSpec(memory_space=pl.ANY)] * (n_in + n_after + 2 * n_join),
        out_specs=[pl.BlockSpec(memory_space=pl.ANY)] * (n_out + n_join),
        scratch_shapes=[pltpu.VMEM(item.dims, item.array.dtype) for item in ins]
        + [pltpu.VMEM(out.shape, out.dtype) for out in [*outs, *joined]]
        + [
            pltpu.SemaphoreType.DMA((sum(item.parts for item in ins) + 1,)),
            pltpu.SemaphoreType.DMA((max(n_out, 1) * PARTS,)),
            pltpu.SemaphoreType.DMA((max(2 * n_join, 1),)),
        ]
        + list(scratch),
        compiler_params=pltpu.CompilerParams(vmem_limit_bytes=vmem * 2**20),
        cost_estimate=pl.CostEstimate(flops=cost, bytes_accessed=1, transcendentals=0),
    )(lengths, *(item.array for item in ins), *after, *(item for pair in joins for item in pair))


def line(load):
    ref = load.ref()
    return ref[...].astype(F32).reshape(1, ref.shape[0])


def length_of(lengths, at):
    core = lax.axis_index("tp")
    return lengths[core if at == 0 else 1 - core]


def places(order, partner=False):
    if not SWAP[0]:
        return list(range(GROUPS))
    place, core = lax.axis_index("dp"), lax.axis_index("tp")
    found = []
    for group in range(GROUPS):
        rel = jnp.bitwise_xor(place, group)
        bits = [rel % 2, (rel // 2) % 2, (rel // 4) % 2, rel // 8]
        near = jnp.where(core == (1 if partner else 0), bits[0], bits[1])
        bits[:2] = near, bits[0] + bits[1] - near
        found.append(sum(bit * (8 // 2**step) for bit, step in zip(bits, order)))
    return found


PLANE_FIRST = (0, 1, 2, 3)
Z_BETWEEN = (0, 2, 1, 3)


Z_FIRST = (1, 2, 0, 3)


def by_length(lengths, at, length, run):
    count = length_of(lengths, at)
    sizes = [size for size in (128, 256) if size < length] + [length]
    below = None
    for size in sizes:
        fits = count <= size
        if below is not None:
            fits = fits & (count > below)

        @pl.when(fits)
        def _(size=size):
            run(size)

        below = size


def shape(dims, dtype=BF16):
    return jax.ShapeDtypeStruct(dims, dtype)


def put_groups(target, place, values, columns):
    size = values.shape[0] // GROUPS
    for group in range(GROUPS):
        start = place[group] * size
        if not isinstance(start, int):
            start = pl.multiple_of(start, size)
        target[pl.ds(start, size), columns] = values[group * size : (group + 1) * size].astype(BF16)


def attend(lengths, tokens, w_query, w_key, w_value, bias_query, bias_value, length):
    width = w_query.shape[1]
    heads = width // HEAD

    def body(lengths, loads, stores, scratch):
        rows, wk, wq, wv, bq, bv = loads
        q_out, k_out, v_out, e_out, own_out, other_out, inv_out = stores
        (v_turned,) = scratch[:1]
        e_out.manual = True
        bq, bv = line(bq), line(bv)

        def lanes(head):
            return slice(head // 2 * PAIR, (head // 2 + 1) * PAIR)

        def sequence(at, size):
            near = slice(at * length, at * length + size)
            lane = lax.broadcasted_iota(jnp.int32, (size, PAIR), 1)
            row = lax.broadcasted_iota(jnp.int32, (size, PAIR), 0)
            count = length_of(lengths, at)
            masked = jnp.where((lane == 0) & (row >= count), -1e30, 0.0).astype(BF16)
            marker = jnp.where(lane == 0, 1.0, 0.0).astype(BF16)
            ones = jnp.ones((16, size), BF16)
            att_out = (own_out, other_out)[at]

            def scores(head):
                queries = q_out.ref[near, lanes(head)]
                own = jnp.where(lane // HEAD == head % 2, queries, jnp.zeros_like(queries))
                keys = jnp.concatenate([k_out.ref[near, lanes(head)], masked], axis=1)
                return nt(keys, jnp.concatenate([own, marker], axis=1))

            mixed, inverse = [], []

            def mix(head):
                values = v_turned[at, head * HEAD : (head + 1) * HEAD, :size]
                left = jnp.concatenate([values, ones], axis=0)
                sums = nn(left, e_out.ref[at * heads + head, :size, :size])
                inv = 1.0 / sums[HEAD : HEAD + 1]
                mixed.append(sums[:HEAD] * inv)
                inverse.append(jnp.broadcast_to(inv, (HEAD, size)))
                if head % 2:
                    att_out.ref[:size, lanes(head)] = (
                        jnp.concatenate(mixed, axis=0).astype(BF16).T
                    )
                    inv_out.ref[near, lanes(head)] = jnp.concatenate(inverse, axis=0).T
                    mixed.clear()
                    inverse.clear()

            now = scores(0)
            for head in range(heads):
                later = scores(head + 1) if head + 1 < heads else None
                top = jnp.max(now, axis=0, keepdims=True)
                e_out.ref[at * heads + head, :size, :size] = jnp.exp(now - top).astype(BF16)
                if head:
                    mix(head - 1)
                now = later
            mix(heads - 1)
            if size < length:
                att_out.ref[size:] = jnp.zeros((length - size, width), BF16)
            square(at, size).start()

        def square(at, size):
            cut = (pl.ds(at * heads, heads), pl.ds(0, size), pl.ds(0, size))
            return pltpu.make_async_copy(
                e_out.ref.at[cut], e_out.target.at[cut], e_out.sems.at[e_out.next + at]
            )

        for at in range(2):
            x = rows.part(at)
            near = slice(at * length, (at + 1) * length)
            k_out.ref[near] = nn(x[near], wk.ref()[...]).astype(BF16)
            q_out.ref[near] = (
                (nn(x[near], wq.ref()[...]) + bq).astype(BF16).astype(F32) * HEAD**-0.5
            ).astype(BF16)
            value = (nn(x[near], wv.ref()[...]) + bv).astype(BF16)
            v_out.ref[near] = value
            v_turned[at] = value.T
            by_length(lengths, at, length, lambda size: sequence(at, size))
            for out in (q_out, k_out, v_out, inv_out):
                out.send(pl.ds(at * length, length))
            (own_out, other_out)[at].send()
        for at in range(2):
            by_length(lengths, at, length, lambda size: square(at, size).wait())

    both = 2 * length
    return call(
        body,
        "attend",
        lengths,
        [BothRows(tokens, length), w_key, w_query, w_value, bias_query, bias_value],
        [
            shape((both, width)),
            shape((both, width)),
            shape((both, width)),
            shape((2 * heads, length, length)),
            shape((length, width)),
            shape((length, width)),
            shape((both, width), F32),
        ],
        scratch=[pltpu.VMEM((2, width, length), BF16)],
    )


def up_half(low, wu, bu, wd, act, slope, total, fresh):
    inner = act.shape[1]

    def project(start):
        return nn(low[...], wu[:, start : start + HIDDEN]) + bu[:, start : start + HIDDEN]

    now = project(0)
    for start in range(0, inner, HIDDEN):
        cut = slice(start, start + HIDDEN)
        later = project(start + HIDDEN) if start + HIDDEN < inner else None
        phi = 0.5 * (1.0 + lax.erf(now * (0.5**0.5)))
        act[:, cut] = (now * phi).astype(BF16)
        slope[:, cut] = (
            phi + now * (jnp.exp(-0.5 * now * now) * 0.3989422804014327)
        ).astype(BF16)
        part = nn(act[:, cut], wd[cut, :])
        if fresh and start == 0:
            total[...] = part
        else:
            total[...] += part
        now = later


def feed(lengths, tokens, out_grad, att, w_out, vectors, bias_up, w_up, w_down, length):
    model = tokens.shape[1]
    inner = w_up[0].shape[1]

    def body(lengths, loads, stores, scratch):
        att_a, wo_a, att_b, wo_b, rows, bo, g1, s1 = loads[:8]
        wu_a, bu_a, wd_a, wu_b, bu_b, wd_b, cot, bd, g2, s2 = loads[8:]
        first_out, layer_out, small, down_a, up_a, *halves = stores
        total, hidden, low, norm, spr, grad_low = scratch[:6]
        act_a, act_b, slope_a, slope_b, bias_a, bias_b, down_b, up_b = scratch[6:14]
        total[...] = nn(att_a.ref()[...], wo_a.ref()[...]) + nn(att_b.ref()[...], wo_b.ref()[...])
        x = rows.ref()
        bo, g1, s1 = line(bo), line(g1), line(s1)
        for start in range(0, length, ROWS):
            cut = slice(start, start + ROWS)
            value = x[cut].astype(F32) + (total[cut] + bo)
            centred = value - mean(value)
            spread = lax.rsqrt(mean(centred * centred) + EPS)
            normed = centred * spread
            norm[cut] = normed.astype(BF16)
            spr[cut] = jnp.broadcast_to(spread, (ROWS, 128))
            full = normed * g1 + s1
            hidden[cut] = full
            low[cut] = full.astype(BF16)
        for load in loads[:11]:
            load.ref()
        up_half(low, wu_a.ref(), line(bu_a), wd_a.ref(), act_a, slope_a, total, True)
        for load in loads:
            load.ref()
        up_half(low, wu_b.ref(), line(bu_b), wd_b.ref(), act_b, slope_b, total, False)
        cot = cot.ref()
        bd, g2, s2 = line(bd), line(g2), line(s2)
        sums = [jnp.zeros((1, model), F32)] * 6
        for start in range(0, length, ROWS):
            cut = slice(start, start + ROWS)
            row = lax.broadcasted_iota(jnp.int32, (ROWS, model), 0) + start
            valid = jnp.where(row < length_of(lengths, 0), 1.0, 0.0)
            value = hidden[cut] + total[cut] + bd
            centred = value - mean(value)
            spread = lax.rsqrt(mean(centred * centred) + EPS)
            normed = centred * spread
            layer_out.ref[cut] = ((normed * g2 + s2) * valid).astype(BF16)
            grad = cot[cut].astype(F32) * valid
            scaled = grad * g2
            resid = spread * (scaled - mean(scaled) - normed * mean(scaled * normed))
            sums[0] += column_sum(grad * normed)
            sums[1] += column_sum(grad)
            sums[2] += column_sum(resid)
            grad_low[cut] = resid.astype(BF16)
        layer_out.send()
        slope_back(grad_low, wd_b.ref(), slope_b, bias_b)
        slope_back(grad_low, wd_a.ref(), slope_a, bias_a)
        total[...] = nt(slope_a[...], wu_a.ref()[...]) + nt(slope_b[...], wu_b.ref()[...])
        for start in range(0, length, ROWS):
            cut = slice(start, start + ROWS)
            value = grad_low[cut].astype(F32) + total[cut]
            normed = norm[cut].astype(F32)
            scaled = value * g1
            first = spr[cut, 0:1] * (scaled - mean(scaled) - normed * mean(scaled * normed))
            sums[3] += column_sum(value * normed)
            sums[4] += column_sum(value)
            sums[5] += column_sum(first)
            first_out.ref[cut] = first.astype(BF16)
        first_out.send()
        for at in range(3):
            small.ref[at : at + 1, :model] = sums[2 * at]
            small.ref[at : at + 1, model:] = sums[2 * at + 1]
        small.ref[3:4] = bias_a[0:1]
        small.ref[4:5] = bias_b[0:1]
        small.ref[5:8] = jnp.zeros((3, inner), F32)
        small.send()
        weight_halves(*halves[:2], down_b, grad_low, act_b, places(PLANE_FIRST, True))
        weight_halves(*halves[2:], up_b, low, slope_b, places(PLANE_FIRST, True))
        weight(down_a, grad_low, act_a, places(PLANE_FIRST))
        weight(up_a, low, slope_a, places(PLANE_FIRST))

    whole = shape((model, inner))
    half = pltpu.VMEM((length, inner), BF16)
    return call(
        body,
        "feed",
        lengths,
        [att[0], w_out[0], att[1], w_out[1], OwnRows(tokens, length), *vectors[:3]]
        + [w_up[0], bias_up[0], w_down[0], w_up[1], bias_up[1], w_down[1]]
        + [OwnRows(out_grad, length), *vectors[3:]],
        [shape((length, model)), shape((length, model)), shape((8, inner), F32), whole, whole]
        + [shape((model // 2, inner))] * 4,
        scratch=[
            pltpu.VMEM((length, model), F32),
            pltpu.VMEM((length, model), F32),
            pltpu.VMEM((length, model), BF16),
            pltpu.VMEM((length, model), BF16),
            pltpu.VMEM((length, 128), F32),
            pltpu.VMEM((length, model), BF16),
            half,
            half,
            half,
            half,
            pltpu.VMEM((8, inner), F32),
            pltpu.VMEM((8, inner), F32),
            pltpu.VMEM((model, inner), BF16),
            pltpu.VMEM((model, inner), BF16),
        ],
    )


SWAP = [True]


def weight(out, left, right, place):
    columns = right.shape[1]
    for start in range(0, columns, HIDDEN):
        cut = pl.ds(start, HIDDEN)
        put_groups(out.ref, place, tn(left[...], right[:, start : start + HIDDEN]), cut)
        out.send(slice(None), cut)


def weight_halves(keep, send, buffer, left, right, place):
    columns = right.shape[1]
    rows = buffer.shape[0] // 2
    keep.ref, send.ref = buffer.at[pl.ds(0, rows)], buffer.at[pl.ds(rows, rows)]
    for start in range(0, columns, HIDDEN):
        cut = pl.ds(start, HIDDEN)
        put_groups(buffer, place, tn(left[...], right[:, start : start + HIDDEN]), cut)
        for out in (send, keep):
            out.send(slice(None), cut)


def slope_back(grad, wd, slope, bias):
    inner = slope.shape[1]

    def project(start):
        return nt(grad[...], wd[start : start + HIDDEN, :])

    now = project(0)
    for start in range(0, inner, HIDDEN):
        cut = slice(start, start + HIDDEN)
        later = project(start + HIDDEN) if start + HIDDEN < inner else None
        value = (now * slope[:, cut].astype(F32)).astype(BF16)
        slope[:, cut] = value
        bias[:, cut] = jnp.broadcast_to(column_sum(value.astype(F32)), (8, HIDDEN))
        now = later


def attend_back(
    lengths, low, tokens, w_out, saved, length, after=()
):
    query, keyed, valued, expo, att_own, att_other, inv = saved
    width, model = w_out.shape
    heads = width // HEAD
    both = 2 * length

    def square(e, at, size):
        cut = (pl.ds(at * heads, heads), pl.ds(0, size), pl.ds(0, size))
        return pltpu.make_async_copy(e.source.at[cut], e.target.at[cut], e.sems.at[e.first + at])

    def early(lengths, loads):
        for at in range(2):
            by_length(lengths, at, length, lambda size: square(loads[6], at, size).start())

    def body(lengths, loads, stores, scratch):
        grad_a, wo, k, v, inverse, att_a, e, q, grad_b, att_b = loads[:10]
        rows = loads[10]
        grads, small, *halves = stores
        dq, dk, dv = (grads.ref.at[:, pl.ds(at * width, width)] for at in range(3))
        mixed, k_turned, kept, first_p, first_q = scratch[:5]
        wo = wo.ref()
        atts = (att_a, att_b)

        def sequence(at, size):
            rows_at = pl.ds(at * length, size)
            lane = lax.broadcasted_iota(jnp.int32, (size, PAIR), 1)
            marker = jnp.where(lane < 2, 1.0, 0.0).astype(BF16)
            square(e, at, size).wait()

            def two_heads(pair, carry):
                cut = pl.ds(pl.multiple_of(pair * PAIR, PAIR), PAIR)
                scaled = mixed[:size, cut].astype(F32) * inverse.target[rows_at, cut]
                product = scaled * atts[at].target[:size, cut].astype(F32)
                scaled = scaled.astype(BF16)
                values = jnp.concatenate([v.target[rows_at, cut], marker], axis=1)
                queries = q.target[rows_at, cut]

                def scores(half):
                    mine = lane // HEAD == half
                    inner = -jnp.sum(jnp.where(mine, product, 0.0), axis=1, keepdims=True)
                    high = inner.astype(BF16).astype(F32)
                    extra = jnp.where(lane == 0, high, jnp.where(lane == 1, inner - high, 0.0))
                    own = jnp.where(mine, scaled, jnp.zeros_like(scaled))
                    return nt(values, jnp.concatenate([own, extra.astype(BF16)], axis=1))

                now = [scores(0), scores(1)]
                dvs, dks, dqs = [], [], []
                for half in range(2):
                    expo = e.target[at * heads + 2 * pair + half, :size, :size]
                    kept[half, :size, :size] = (expo.astype(F32) * now[half]).astype(BF16)
                    dvs.append(nn(expo, scaled))
                for half in range(2):
                    grads_half = kept[half, :size, :size]
                    dks.append(nn(grads_half, queries))
                    at_row = pl.multiple_of(pair * PAIR + half * HEAD, HEAD)
                    dqs.append(nn(k_turned[pl.ds(at_row, HEAD), :size], grads_half))
                dv[rows_at, cut] = jnp.where(lane < HEAD, dvs[0], dvs[1]).astype(BF16)
                dk[rows_at, cut] = jnp.where(lane < HEAD, dks[0], dks[1]).astype(BF16)
                dq[rows_at, cut] = (jnp.concatenate(dqs, axis=0) * HEAD**-0.5).astype(BF16).T
                return carry

            lax.fori_loop(0, heads // 2, two_heads, 0)
            if size < length:
                rest = slice(at * length + size, (at + 1) * length)
                grads.ref[rest] = jnp.zeros((length - size, 3 * width), BF16)

        for at, grad in enumerate((grad_a, grad_b)):
            near = slice(at * length, (at + 1) * length)
            mixed[...] = nt(grad.ref()[...], wo[...]).astype(BF16)
            k_turned[...] = k.part(at)[near].T
            for load in (inverse, v, q):
                load.part(at)
            atts[at].ref()
            by_length(lengths, at, length, lambda size: sequence(at, size))
            grads.send(pl.ds(at * length, length))
        sums = [column_sum(out[...].astype(F32)) for out in (dq, dv)]
        sums = jnp.concatenate(sums, axis=1)
        high = sums.astype(BF16).astype(F32)
        low = (sums - high).astype(BF16).astype(F32)
        first = lax.broadcasted_iota(jnp.int32, (8, 2 * width), 0) == 0
        small.ref[...] = jnp.where(first, high + low, 0.0)
        small.send()
        first_p[pl.ds(model, 2 * SMALL)] = jnp.concatenate(
            [jnp.where(first, high, 0.0), jnp.where(first, low, 0.0)], axis=0
        ).astype(BF16)
        x = rows.ref()
        for source, order, (keep, send), parts in (
            (first_p, Z_BETWEEN, halves[:2], (dq, dk)),
            (first_q, Z_FIRST, halves[2:], (dv, None)),
        ):
            place = places(order)
            for at, part in enumerate(parts):
                if part is None:
                    product = tn(grad_a.target[...], att_a.target[...])
                    product += tn(grad_b.target[...], att_b.target[...])
                else:
                    product = tn(x[...], part[...])
                put_groups(source, place, product, pl.ds(at * width, width))
            for out, start in ((send, model // 2), (keep, 0)):
                out.ref = source.at[pl.ds(start, out.target.shape[0])]
                out.send()

    half = shape((model // 2, 2 * width))
    return call(
        body,
        "attend_back",
        lengths,
        [low[0], w_out, *(Whole(item, 2, 0) for item in (keyed, valued, inv)), att_own]
        + [Manual(expo, 2, 0), Whole(query, 2, 0)]
        + [Whole(low[1], late=True), Whole(att_other, late=True), LateBoth(tokens, length)],
        [shape((both, 3 * width)), shape((8, 2 * width), F32), half, shape((model // 2 + 16, 2 * width))]
        + [half, half],
        scratch=[
            pltpu.VMEM((length, width), BF16),
            pltpu.VMEM((width, length), BF16),
            pltpu.VMEM((2, length, length), BF16),
            pltpu.VMEM((model + 2 * SMALL, 2 * width), BF16),
            pltpu.VMEM((model, 2 * width), BF16),
        ],
        after=after,
        early=early,
    )


def input_part(lengths, first, grads, weights, joins, length, after=()):
    model, width = weights[0].shape

    def body(lengths, loads, stores, scratch):
        side = scratch[0]
        copies = [
            pltpu.make_async_copy(
                load.source, side.at[:, pl.ds(at * width, width)], load.sems.at[load.first]
            )
            for at, load in enumerate(loads[1:4])
        ]
        for copy in copies:
            copy.start()
        for copy in copies:
            copy.wait()
        scratch[-1]()
        for at in (1, 0):
            near = slice(at * length, (at + 1) * length)
            total = nt(loads[0].part(at)[near], side[...])
            if not at:
                total += loads[4].ref()[...].astype(F32)
            stores[at].ref[...] = total.astype(BF16)
            stores[at].send()

    return call(
        body,
        "input_part",
        lengths,
        [Whole(grads, 2, 0), *(Manual(item) for item in weights), Whole(first, late=True)],
        [shape((length, model))] * 2,
        scratch=[pltpu.VMEM((model, 3 * width), BF16)],
        after=after,
        joins=joins,
    )


def swap(values):
    return lax.ppermute(values, "tp", [(0, 1), (1, 0)])


def together(*values):
    return lax.optimization_barrier(values)


def flip(values, bits):
    size = lax.axis_size("dp")
    perm = [(2 * d + c, 2 * (d ^ bits[c]) + c) for d in range(size) for c in range(2)]
    return lax.ppermute(values, ("dp", "tp"), perm)


NEAR, FAR, LOW, HIGH = (1, 2), (2, 1), (4, 4), (8, 8)


def add(left, right):
    return left.astype(F32) + right.astype(F32)


def total(parts):
    parts = [part.astype(F32) for part in parts]
    while len(parts) > 1:
        parts = [sum(parts[at + 1 : at + 2], parts[at]) for at in range(0, len(parts), 2)]
    return parts[0]


SMALL = 8


def split(values):
    high = values.astype(BF16).astype(F32)
    return high, (values - high).astype(BF16).astype(F32)


def small_sum(own, came):
    high, low = split(own)
    came = came.astype(F32)
    return (high + low) + (came[:SMALL] + came[SMALL:])


def put_small(message, at, values):
    message[at : at + 2 * SMALL] = jnp.concatenate(split(values), axis=0).astype(BF16)


BRIEF, LONG = 2 * 10**9, 2 * 10**10


def merge(body, name, ins, outs, after=()):
    n_in = len(ins)

    def kernel(*refs):
        body(refs[:n_in], refs[n_in + len(after) :])

    return pl.pallas_call(
        kernel,
        name=name,
        out_shape=outs,
        in_specs=[pl.BlockSpec(memory_space=pltpu.VMEM)] * n_in
        + [pl.BlockSpec(memory_space=pl.ANY)] * len(after),
        out_specs=[pl.BlockSpec(memory_space=pltpu.VMEM)] * len(outs),
        compiler_params=pltpu.CompilerParams(vmem_limit_bytes=16 * 2**20),
        cost_estimate=pl.CostEstimate(flops=BRIEF, bytes_accessed=1, transcendentals=0),
    )(*ins, *after)


def exchange(name, jobs, small, after=()):
    rows = [keep.shape[0] // 2 for keep, _, _ in jobs]
    columns = min(keep.shape[1] for keep, _, _ in jobs)
    ins = []
    for keep, came, _ in jobs:
        ins += [keep, came]
    if small is not None:
        ins += [small[0], small[1]]

    def body(ins, outs):
        message = outs[-1]
        at = 0
        for job, (_, _, start) in enumerate(jobs):
            keep, came = ins[2 * job], ins[2 * job + 1]
            count = rows[job]
            sent = add(keep[count:], came[start + count : start + 2 * count])
            for column in range(0, keep.shape[1], columns):
                message[at : at + count] = sent[:, column : column + columns].astype(BF16)
                at += count
            outs[job][...] = add(keep[:count], came[start : start + count])
        if small is not None:
            values = small_sum(ins[-2][...], ins[-1][small[2] : small[2] + 2 * SMALL])
            outs[-2][...] = values
            put_small(message, at, values)

    wide = [keep.shape[1] for keep, _, _ in jobs]
    outs = [shape((count, width), F32) for count, width in zip(rows, wide)]
    height = sum(count * (width // columns) for count, width in zip(rows, wide))
    if small is not None:
        outs.append(shape(small[0].shape, F32))
        height += 2 * SMALL
    outs.append(shape((height, columns)))
    return merge(body, name, ins, outs, after)


def first_near(lengths, own, came, small=None, after=()):
    rows, columns = own.shape[0] // 2, own.shape[1]
    parts = 4
    size = rows // parts

    def body(lengths, loads, stores, scratch):
        out = stores[0]
        if small is not None:
            put_small(out.ref, rows, loads[2].ref()[...])
            out.send(pl.ds(rows, 2 * SMALL))
        for at in range(parts):
            cut = slice(at * size, (at + 1) * size)
            out.ref[cut] = add(loads[0].part(at)[cut], loads[1].part(at)[cut]).astype(BF16)
            out.send(pl.ds(at * size, size))

    ins = [Rows(own, rows, rows, parts), Rows(came, 0, rows, parts)]
    if small is not None:
        ins.append(small)
    rows_out = rows if small is None else rows + 2 * SMALL
    return call(body, "first_near", lengths, ins, [shape((rows_out, columns))], after=after, cost=LONG)[0]


def kept_rows(own, came, near_came):
    rows = own.shape[0] // 2
    return [Rows(item, 0, rows, 4, True) for item in (own, came, near_came)]


def kept_sums(loads, stay, go):
    rows = loads[0].target.shape[0]
    size = rows // 4
    for at in range(4):
        start = (3 - at) * size
        cut = slice(start, start + size)
        own, came, near_came = (load.part(at)[cut] for load in loads)
        values = (add(own, came) + near_came.astype(F32)).astype(BF16)
        out, to = (go, start - rows // 2) if start >= rows // 2 else (stay, start)
        out.ref[to : to + size] = values
        out.send(pl.ds(to, size))


def second(lengths, name, own, came, near_came, small=None, after=()):
    rows, columns = own.shape[0] // 4, own.shape[1]

    def body(lengths, loads, stores, scratch):
        message, stay = stores[:2]
        if small is not None:
            values = small_sum(loads[-2].ref()[...], loads[-1].ref()[...])
            put_small(message.ref, rows, values)
            message.send(pl.ds(rows, 2 * SMALL))
            stores[2].ref[...] = values
            stores[2].send()
        kept_sums(loads[:3], stay, message)

    ins = kept_rows(own, came, near_came)
    outs = [shape((rows + (2 * SMALL if small is not None else 0), columns)), shape((rows, columns))]
    if small is not None:
        ins += [small, Rows(near_came, 2 * rows, 2 * SMALL)]
        outs.append(shape(small.shape, F32))
    return call(body, name, lengths, ins, outs, after=after, cost=BRIEF)


def onward(name, jobs, small, after=()):
    rows = [keep.shape[0] // 2 for keep, _, _ in jobs]
    columns = jobs[0][0].shape[1]
    height = sum(rows)
    ins = []
    for keep, came, _ in jobs:
        ins += [keep, came]
    if small is not None:
        ins += small[:2]

    def body(ins, outs):
        message = outs[0]
        at = 0
        for job, (count, (_, _, start)) in enumerate(zip(rows, jobs)):
            keep, came = ins[2 * job], ins[2 * job + 1]
            sent = add(keep[count:], came[start + count : start + 2 * count])
            message[at : at + count] = sent.astype(BF16)
            outs[1 + job][...] = add(keep[:count], came[start : start + count]).astype(BF16)
            at += count
        if small is not None:
            values = small_sum(ins[-2][...], ins[-1][small[2] : small[2] + 2 * SMALL])
            outs[-1][...] = values
            put_small(message, at, values)

    outs = [shape((height + (2 * SMALL if small is not None else 0), columns))]
    outs += [shape((count, columns)) for count in rows]
    if small is not None:
        outs.append(shape(small[0].shape, F32))
    return merge(body, name, ins, outs, after)


def last_up(up, small, came):
    rows = up.shape[0]

    def body(ins, outs):
        up, small, came = ins
        outs[0][...] = add(up[...], came[:rows])
        outs[1][...] = small_sum(small[...], came[rows:])

    return merge(
        body, "last_up", [up, small, came], [shape(up.shape, F32), shape(small.shape, F32)]
    )


def last_heads(left, right, small, came):
    rows, columns = left.shape
    width = columns // 2

    def body(ins, outs):
        left, right, small, came = ins
        values = add(left[...], came[:rows])
        outs[0][...] = values[:, :width]
        outs[1][...] = values[:, width:]
        values = add(right[...], came[rows : 2 * rows])
        outs[2][...] = values[:, :width]
        outs[3][...] = values[:, width:]
        outs[4][...] = small_sum(small[...], came[2 * rows :])

    one = shape((rows, width), F32)
    return merge(
        body,
        "last_heads",
        [left, right, small, came],
        [one, one, one, one, shape(small.shape, F32)],
    )


def scatter(whole):
    return lax.psum_scatter(whole, "dp", scatter_dimension=0, tiled=True)


def local(
    tokens,
    seq_lengths,
    out_grad,
    w_query,
    bias_query,
    w_key,
    w_value,
    bias_value,
    w_out,
    bias_out,
    gain_one,
    shift_one,
    w_up,
    bias_up,
    w_down,
    bias_down,
    gain_two,
    shift_two,
):
    near = lax.axis_size("dp") == GROUPS
    SWAP[0] = near
    lengths = seq_lengths
    model = tokens.shape[1]
    length = tokens.shape[0] // seq_lengths.shape[0]
    width = w_query.shape[1]
    inner = w_up.shape[1]

    wo_b, wu_b, wd_b, bu_b = swap(w_out), swap(w_up), swap(w_down), swap(bias_up)
    query, keyed, valued, expo, att_own, att_other, inv = attend(
        lengths, tokens, w_query, w_key, w_value, bias_query, bias_value, length
    )
    first_low, layer_own, small, down_a, up_a, *halves = feed(
        lengths,
        tokens,
        out_grad,
        (att_own, swap(att_other)),
        (w_out, wo_b),
        (bias_out, gain_one, shift_one, bias_down, gain_two, shift_two),
        (bias_up, bu_b),
        (w_up, wu_b),
        (w_down, wd_b),
        length,
    )
    first_came = swap(first_low)
    down_kept, down_gone, up_kept, up_gone = (swap(half) for half in halves)
    layer_other = swap(layer_own)
    if near:
        down_sent = first_near(lengths, down_a, down_gone, after=[first_came])
        near_down = flip(down_sent, NEAR)
    after = []
    if near:
        up_sent = first_near(lengths, up_a, up_gone, small, [down_sent])
        near_up = flip(up_sent, NEAR)
        after = [up_sent]
    grads, small_heads, keep_p, send_p, keep_q, send_q = attend_back(
        lengths,
        (first_low, first_came),
        tokens,
        w_out,
        (query, keyed, valued, expo, att_own, att_other, inv),
        length,
        after,
    )
    after = []
    if near:
        came_p, came_q = flip(send_p, NEAR), flip(send_q, LOW)
        sent, down = second(
            lengths, "down_far", down_a, down_kept, near_down, after=[keep_p]
        )
        far_down = flip(sent, FAR)
        sent, up, small = second(
            lengths, "up_far", up_a, up_kept, near_up, small, [sent]
        )
        far_up = flip(sent, FAR)
        after = [sent]
    input_own, input_other, layer_output = input_part(
        lengths,
        first_low,
        grads,
        (w_query, w_key, w_value),
        [(layer_own, layer_other)],
        length,
        after,
    )
    input_other = swap(input_other)
    if near:
        came_p = together(came_p, input_own)[0]
        sent, heads_p, small_heads = onward(
            "heads_low",
            [(keep_p, came_p, 0)],
            (small_heads, came_p, model // 2),
        )
        low_p = flip(sent, LOW)
        sent, heads_q = onward("heads_near", [(keep_q, came_q, 0)], None, [sent])
        near_q = flip(sent, NEAR)
        sent, down = onward("down_low", [(down, far_down, 0)], None, [sent])
        low_down = flip(sent, LOW)
        sent, up, small = onward(
            "up_low", [(up, far_up, 0)], (small, far_up, up.shape[0]), [sent]
        )
        low_up = flip(sent, LOW)
        sent, heads_p, heads_q, small_heads = onward(
            "heads_far",
            [(heads_p, low_p, 0), (heads_q, near_q, 0)],
            (small_heads, low_p, heads_p.shape[0]),
            [sent],
        )
        far_heads = flip(sent, FAR)
        sent, down = onward("down_high", [(down, low_down, 0)], None, [sent])
        high_down = flip(sent, HIGH)
        input_other = together(input_other, sent)[0]
    input_own = (input_own.astype(F32) + input_other.astype(F32)).astype(BF16)
    (input_grad,) = call(
        lambda *_: None, "join", lengths, [], [], vmem=16, joins=[(input_own, swap(input_own))]
    )
    if near:
        rows = heads_p.shape[0]
        sent, heads_p, heads_q, small_heads = onward(
            "heads_high",
            [(heads_p, far_heads, 0), (heads_q, far_heads, rows)],
            (small_heads, far_heads, 2 * rows),
            [input_own],
        )
        high_heads = flip(sent, HIGH)
        sent, up, small = onward(
            "up_high", [(up, low_up, 0)], (small, low_up, up.shape[0]), [sent]
        )
        high_up = flip(sent, HIGH)
        grad_down = add(down, high_down)
        high_up = together(high_up, input_grad)[0]
        grad_up, small = last_up(up, small, high_up)
        high_heads = together(high_heads, input_grad)[0]
        grad_query, grad_key, grad_value, grad_out, small_heads = last_heads(
            heads_p, heads_q, small_heads, high_heads
        )
    else:
        grad_down = scatter(total([down_a, jnp.concatenate([down_kept, down_gone], axis=0)]))
        grad_up = scatter(total([up_a, jnp.concatenate([up_kept, up_gone], axis=0)]))
        heads_p = scatter(jnp.concatenate([keep_p, send_p[: model // 2]], axis=0).astype(F32))
        heads_q = scatter(jnp.concatenate([keep_q, send_q], axis=0).astype(F32))
        small, small_heads = lax.psum((small, small_heads), "dp")
        grad_query, grad_key = heads_p[:, :width], heads_p[:, width:]
        grad_value, grad_out = heads_q[:, :width], heads_q[:, width:]
    small_other = together(swap(small), small_heads)[0]
    norms = (small[:3] + small_other[:3]).reshape(6, model)
    bias_up_grad = small[3] + small_other[4]
    bias_query_grad, bias_value_grad = small_heads[0, :width], small_heads[0, width:]
    gain_two_grad, shift_two_grad, bias_down_grad = norms[0], norms[1], norms[2]
    gain_one_grad, shift_one_grad, bias_out_grad = norms[3], norms[4], norms[5]
    return (
        layer_output,
        input_grad,
        grad_query,
        grad_key,
        grad_value,
        bias_query_grad,
        bias_value_grad,
        grad_out.T,
        bias_out_grad,
        gain_one_grad,
        shift_one_grad,
        grad_up,
        bias_up_grad,
        grad_down.T,
        bias_down_grad,
        gain_two_grad,
        shift_two_grad,
    )


def solution(mesh):
    return jax.shard_map(
        local,
        mesh=mesh,
        in_specs=(
            P("dp", None),
            P("dp"),
            P("dp", None),
            P(None, "tp"),
            P("tp"),
            P(None, "tp"),
            P(None, "tp"),
            P("tp"),
            P("tp", None),
            P(),
            P(),
            P(),
            P(None, "tp"),
            P("tp"),
            P("tp", None),
            P(),
            P(),
            P(),
        ),
        out_specs=(
            P("dp", None),
            P("dp", None),
            P("dp", "tp"),
            P("dp", "tp"),
            P("dp", "tp"),
            P("tp"),
            P("tp"),
            P("tp", "dp"),
            P(),
            P(),
            P(),
            P("dp", "tp"),
            P("tp"),
            P("tp", "dp"),
            P(),
            P(),
            P(),
        ),
        check_vma=False,
    )
```
